128 devices in a mesh: fsdp: 32 (over z, x, core), ctx: 4 (over y).
Axes of the slice: x: 4, y: 4, z: 4, core: 2. Of those that a mesh axis runs over, the one named last changes fastest.
Arguments:
- block_input: bfloat16 [16384, 896], P(('fsdp', 'ctx')), may hold values from -6 to 6
- positions: int32 [16384], P(('fsdp', 'ctx')), may hold values from 0 to 1023, as said below
- first_gain: bfloat16 [896], P('fsdp'), may hold values from 0.099609375 to 1.8984375
- query_weight: bfloat16 [896, 896], P('fsdp'), may hold values from -0.1875 to 0.1875
- query_bias: bfloat16 [896], P('fsdp'), may hold values from -3 to 3
- key_weight: bfloat16 [896, 128], P('fsdp'), may hold values from -0.1875 to 0.1875
- value_weight: bfloat16 [896, 128], P('fsdp'), may hold values from -0.1875 to 0.1875
- value_bias: bfloat16 [128], P('fsdp'), may hold values from -3 to 3
- output_weight: bfloat16 [896, 896], P('fsdp'), may hold values from -0.5 to 0.5
- second_gain: bfloat16 [896], P('fsdp'), may hold values from 0.099609375 to 1.8984375
- gate_weight: bfloat16 [896, 4864], P('fsdp'), may hold values from -0.1875 to 0.1875
- up_weight: bfloat16 [896, 4864], P('fsdp'), may hold values from -0.1875 to 0.1875
- down_weight: bfloat16 [4864, 896], P('fsdp'), may hold values from -0.078125 to 0.078125
- cotangent: bfloat16 [16384, 896], P(('fsdp', 'ctx')), may hold values from -6 to 6
Outputs:
- block_output: bfloat16 [16384, 896], P(('fsdp', 'ctx'))
- grad_input: bfloat16 [16384, 896], P(('fsdp', 'ctx'))
- grad_first_gain: float32 [896], P(('fsdp', 'ctx'))
- grad_query_weight: float32 [896, 896], P(('fsdp', 'ctx'))
- grad_query_bias: float32 [896], P(('fsdp', 'ctx'))
- grad_key_weight: float32 [896, 128], P(('fsdp', 'ctx'))
- grad_value_weight: float32 [896, 128], P(('fsdp', 'ctx'))
- grad_value_bias: float32 [128], P(('fsdp', 'ctx'))
- grad_output_weight: float32 [896, 896], P(('fsdp', 'ctx'))
- grad_second_gain: float32 [896], P(('fsdp', 'ctx'))
- grad_gate_weight: float32 [896, 4864], P(('fsdp', 'ctx'))
- grad_up_weight: float32 [896, 4864], P(('fsdp', 'ctx'))
- grad_down_weight: float32 [4864, 896], P(('fsdp', 'ctx'))
The draws below stay inside these ranges and needn't reach their ends.
Inputs may be any that keep to these rules, and one draw needn't show every extreme that they name: positions count up by one from 0 along each sequence, a token with position 0 begins a new sequence, the first token has position 0, no sequence is longer than 1024 tokens and one has exactly 1024.
All inputs are finite; a program needn't handle non-finite values.
Results may differ from the reference program's by a relative error of at most 0.018.
Values may be sent and summed in bfloat16 or wider, within the bound.
A program may use at most 192 MiB of HBM per device.

```python
import math
import jax
import jax.numpy as jnp
from jax import lax

D = 896
HEADS = 14
KV_HEADS = 2
HEAD_SIZE = 64
FF = 4864
SEQ = 1024
GROUP_HEADS = 7
Q_WIDTH = 896
KV_WIDTH = 128
TOKENS = 16384


def draw_positions(key, part):
    count = 4 * TOKENS // SEQ + 2
    lengths = jax.random.randint(jax.random.fold_in(key, 11), (count,), SEQ // 4, SEQ + 1)
    chosen = jax.random.randint(jax.random.fold_in(key, 12), (), 0, TOKENS // SEQ)
    lengths = jnp.where(jnp.arange(count) == chosen, SEQ, lengths).astype(jnp.int32)
    ends = jnp.cumsum(lengths)
    index = jnp.arange(TOKENS, dtype=jnp.int32)
    finished = ends[None, :] <= index[:, None]
    begin = jnp.sum(jnp.where(finished, lengths[None, :], 0), axis=1)
    return (index - begin).astype(jnp.int32)


def level_of(stream_key, dims, cuts, low, top_value):
    def one(axis_at, blocks):
        heights = jax.random.uniform(jax.random.fold_in(jax.random.fold_in(stream_key, 6), axis_at), (blocks,), jnp.float32, low / len(cuts), top_value / len(cuts))
        return jnp.repeat(jnp.exp(heights), dims[axis_at] // blocks).reshape((-1,) + (1,) * (len(dims) - axis_at - 1))

    level = one(*cuts[0])
    for cut in cuts[1:]:
        level = level * one(*cut)
    return level


def scatter_about(rng, shape, width, most, split=(), kind=jnp.bfloat16):
    loudness = level_of(rng, shape, split, -0.22, 0.18) if split else 1.0
    values = jax.random.normal(rng, shape, jnp.float32) * width * loudness
    return jnp.minimum(jnp.maximum(values, -most), most).astype(kind)


def setup_inputs(seed: int = 0) -> dict:
    streams_of = jax.random.split(jax.random.key(seed), 15)
    return {
        "block_input": scatter_about(streams_of[0], (TOKENS, D), 1.0, 6.0, ((0, 128),)),
        "positions": draw_positions(jax.random.fold_in(streams_of[14], 71), 0),
        "first_gain": jnp.clip(1.0 + 0.18 * jax.random.normal(streams_of[2], (D,), jnp.float32), 0.099609375, 1.8984375).astype(jnp.bfloat16),
        "query_weight": scatter_about(streams_of[3], (D, Q_WIDTH), D ** -0.5, 0.1875, ((0, 32),)),
        "query_bias": scatter_about(streams_of[4], (Q_WIDTH,), 0.5, 3.0, ((0, 32),)),
        "key_weight": scatter_about(streams_of[5], (D, KV_WIDTH), D ** -0.5, 0.1875, ((0, 32),)),
        "value_weight": scatter_about(streams_of[6], (D, KV_WIDTH), D ** -0.5, 0.1875, ((0, 32),)),
        "value_bias": scatter_about(streams_of[7], (KV_WIDTH,), 0.5, 3.0, ((0, 32),)),
        "output_weight": scatter_about(streams_of[8], (Q_WIDTH, D), (Q_WIDTH // 8) ** -0.5, 0.5, ((0, 32),)),
        "second_gain": jnp.clip(1.0 + 0.18 * jax.random.normal(streams_of[9], (D,), jnp.float32), 0.099609375, 1.8984375).astype(jnp.bfloat16),
        "gate_weight": scatter_about(streams_of[10], (D, FF), D ** -0.5, 0.1875, ((0, 32),)),
        "up_weight": scatter_about(streams_of[11], (D, FF), D ** -0.5, 0.1875, ((0, 32),)),
        "down_weight": scatter_about(streams_of[12], (FF, D), FF ** -0.5, 0.078125, ((0, 32),)),
        "cotangent": scatter_about(streams_of[13], (TOKENS, D), 1.0, 6.0, ((0, 128),)),
    }


EPSILON = 1e-06
ROTARY_BASE = 1000000.0

def rotary_tables(positions, head_size):
    half = head_size // 2
    frequency = ROTARY_BASE ** (-(jnp.arange(half, dtype=jnp.float32) * 2.0 / head_size))
    angles = positions.astype(jnp.float32)[:, None] * frequency[None, :]
    return (jnp.cos(angles), jnp.sin(angles))

def rotate(values, cosine, sine, heads, head_size):
    count = values.shape[0]
    shaped = values.reshape(count, heads, head_size)
    half = head_size // 2
    first = shaped[..., :half]
    second = shaped[..., half:]
    cos_rows = cosine[:, None, :]
    sin_rows = sine[:, None, :]
    turned = jnp.concatenate([first * cos_rows - second * sin_rows, second * cos_rows + first * sin_rows], axis=-1)
    return turned.reshape(count, heads * head_size)

def rotate_back(grads, cosine, sine, heads, head_size):
    count = grads.shape[0]
    shaped = grads.reshape(count, heads, head_size)
    half = head_size // 2
    first = shaped[..., :half]
    second = shaped[..., half:]
    cos_rows = cosine[:, None, :]
    sin_rows = sine[:, None, :]
    turned = jnp.concatenate([first * cos_rows + second * sin_rows, second * cos_rows - first * sin_rows], axis=-1)
    return turned.reshape(count, heads * head_size)

def norm_forward(values):
    factor = lax.rsqrt(lax.optimization_barrier(jnp.mean(values * values, axis=-1, keepdims=True)) + EPSILON)
    return (values * factor, factor)

def norm_backward(grad_out, normed, factor, gain):
    grad_normed = grad_out * gain
    inner = lax.optimization_barrier(jnp.mean(grad_normed * normed, axis=-1, keepdims=True))
    return (factor * (grad_normed - normed * inner), lax.optimization_barrier(jnp.sum(grad_out * normed, axis=0)))

def attend_forward(queries, keys, values, allowed):
    count = queries.shape[0]
    scale = 1.0 / math.sqrt(HEAD_SIZE)
    shaped_q = queries.astype(jnp.float32).reshape(count, KV_HEADS, GROUP_HEADS, HEAD_SIZE)
    shaped_k = keys.astype(jnp.float32).reshape(-1, KV_HEADS, HEAD_SIZE)
    shaped_v = values.astype(jnp.float32).reshape(-1, KV_HEADS, HEAD_SIZE)
    scores = jnp.einsum('qghd,kgd->ghqk', shaped_q, shaped_k) * scale
    scores = jnp.where(allowed[None, None], scores, -jnp.inf)
    top = lax.optimization_barrier(jnp.max(scores, axis=-1, keepdims=True))
    log_total = top + jnp.log(lax.optimization_barrier(jnp.sum(jnp.exp(scores - top), axis=-1, keepdims=True)))
    probability = jnp.exp(scores - log_total).astype(jnp.bfloat16)
    mixed = jnp.einsum('ghqk,kgd->qghd', probability.astype(jnp.float32), shaped_v)
    return (mixed.reshape(count, Q_WIDTH).astype(jnp.bfloat16), log_total)

def attend_backward(queries, keys, values, allowed, mixed, log_total, grad_mixed):
    count = queries.shape[0]
    scale = 1.0 / math.sqrt(HEAD_SIZE)
    shaped_q = queries.astype(jnp.float32).reshape(count, KV_HEADS, GROUP_HEADS, HEAD_SIZE)
    shaped_k = keys.astype(jnp.float32).reshape(-1, KV_HEADS, HEAD_SIZE)
    shaped_v = values.astype(jnp.float32).reshape(-1, KV_HEADS, HEAD_SIZE)
    scores = jnp.einsum('qghd,kgd->ghqk', shaped_q, shaped_k) * scale
    scores = jnp.where(allowed[None, None], scores, -jnp.inf)
    probability = jnp.exp(scores - log_total)
    probability_low = probability.astype(jnp.bfloat16).astype(jnp.float32)
    shaped_g = grad_mixed.astype(jnp.float32).reshape(count, KV_HEADS, GROUP_HEADS, HEAD_SIZE)
    shaped_m = mixed.astype(jnp.float32).reshape(count, KV_HEADS, GROUP_HEADS, HEAD_SIZE)
    delta = jnp.transpose(lax.optimization_barrier(jnp.sum(shaped_g * shaped_m, axis=-1)), (1, 2, 0))[..., None]
    grad_prob = jnp.einsum('qghd,kgd->ghqk', shaped_g, shaped_v)
    grad_scores = (probability * (grad_prob - delta)).astype(jnp.bfloat16).astype(jnp.float32)
    grad_q = jnp.einsum('ghqk,kgd->qghd', grad_scores, shaped_k) * scale
    grad_k = jnp.einsum('ghqk,qghd->kgd', grad_scores, shaped_q) * scale
    grad_v = jnp.einsum('ghqk,qghd->kgd', probability_low, shaped_g)
    return (grad_q.reshape(count, Q_WIDTH), grad_k.reshape(-1, KV_WIDTH), grad_v.reshape(-1, KV_WIDTH))

def reference(block_input, positions, first_gain, query_weight, query_bias, key_weight, value_weight, value_bias, output_weight, second_gain, gate_weight, up_weight, down_weight, cotangent):
    blocks = TOKENS // SEQ
    residual_in = block_input.astype(jnp.float32)
    normed_one, scale_one = norm_forward(residual_in)
    gain_first = first_gain.astype(jnp.float32)
    normed_input = (normed_one * gain_first).astype(jnp.bfloat16)
    query_pre = jnp.dot(normed_input, query_weight, preferred_element_type=jnp.float32) + query_bias.astype(jnp.float32)
    key_pre = jnp.dot(normed_input, key_weight, preferred_element_type=jnp.float32)
    value_rows = (jnp.dot(normed_input, value_weight, preferred_element_type=jnp.float32) + value_bias.astype(jnp.float32)).astype(jnp.bfloat16)
    cosine, sine = rotary_tables(positions, HEAD_SIZE)
    query_rot = rotate(query_pre, cosine, sine, HEADS, HEAD_SIZE).astype(jnp.bfloat16)
    key_rot = rotate(key_pre, cosine, sine, KV_HEADS, HEAD_SIZE).astype(jnp.bfloat16)
    row_index = jnp.arange(TOKENS, dtype=jnp.int32)
    first_index = row_index - positions.astype(jnp.int32)
    pad_keys = jnp.concatenate([jnp.zeros((SEQ, KV_WIDTH), jnp.bfloat16), key_rot], axis=0)
    pad_values = jnp.concatenate([jnp.zeros((SEQ, KV_WIDTH), jnp.bfloat16), value_rows], axis=0)

    def window_mask(start):
        query_index = start + jnp.arange(SEQ, dtype=jnp.int32)
        key_index = start - SEQ + jnp.arange(2 * SEQ, dtype=jnp.int32)
        begin = lax.dynamic_slice_in_dim(first_index, start, SEQ, 0)
        return (key_index[None, :] >= begin[:, None]) & (key_index[None, :] <= query_index[:, None])

    def forward_block(number):
        start = (number * SEQ).astype(jnp.int32)
        queries = lax.dynamic_slice_in_dim(query_rot, start, SEQ, 0)
        keys = lax.dynamic_slice_in_dim(pad_keys, start, 2 * SEQ, 0)
        values = lax.dynamic_slice_in_dim(pad_values, start, 2 * SEQ, 0)
        return attend_forward(queries, keys, values, window_mask(start))
    numbers = jnp.arange(blocks, dtype=jnp.int32)
    attended, log_total = lax.map(forward_block, numbers)
    attended = attended.reshape(TOKENS, Q_WIDTH)
    residual_mid = residual_in + jnp.dot(attended, output_weight, preferred_element_type=jnp.float32)
    gain_second = second_gain.astype(jnp.float32)

    def ffn_block(carry, number):
        start = (number * SEQ).astype(jnp.int32)
        middle = lax.dynamic_slice_in_dim(residual_mid, start, SEQ, 0)
        grad_out = lax.dynamic_slice_in_dim(cotangent, start, SEQ, 0)
        normed_two, scale_two = norm_forward(middle)
        normed_mid = (normed_two * gain_second).astype(jnp.bfloat16)
        gate_pre = jnp.dot(normed_mid, gate_weight, preferred_element_type=jnp.float32)
        up_pre = jnp.dot(normed_mid, up_weight, preferred_element_type=jnp.float32)
        sigma = jax.nn.sigmoid(gate_pre)
        hidden = (gate_pre * sigma * up_pre).astype(jnp.bfloat16)
        output_rows = (middle + jnp.dot(hidden, down_weight, preferred_element_type=jnp.float32)).astype(jnp.bfloat16)
        grad_down = jnp.dot(hidden.T, grad_out, preferred_element_type=jnp.float32)
        grad_hidden = jnp.dot(grad_out, down_weight.T, preferred_element_type=jnp.float32)
        grad_gate_pre = (grad_hidden * up_pre * sigma * (1.0 + gate_pre * (1.0 - sigma))).astype(jnp.bfloat16)
        grad_up_pre = (grad_hidden * gate_pre * sigma).astype(jnp.bfloat16)
        grad_gate = jnp.dot(normed_mid.T, grad_gate_pre, preferred_element_type=jnp.float32)
        grad_up = jnp.dot(normed_mid.T, grad_up_pre, preferred_element_type=jnp.float32)
        grad_normed_mid = jnp.dot(grad_gate_pre, gate_weight.T, preferred_element_type=jnp.float32) + jnp.dot(grad_up_pre, up_weight.T, preferred_element_type=jnp.float32)
        grad_norm_part, grad_gain_two = norm_backward(grad_normed_mid, normed_two, scale_two, gain_second)
        grad_mid = grad_out.astype(jnp.float32) + grad_norm_part
        carry = (carry[0] + grad_gain_two, carry[1] + grad_gate, carry[2] + grad_up, carry[3] + grad_down)
        return (carry, (output_rows, grad_mid))
    start_sums = (jnp.zeros((D,), jnp.float32), jnp.zeros((D, FF), jnp.float32), jnp.zeros((D, FF), jnp.float32), jnp.zeros((FF, D), jnp.float32))
    ffn_sums, (output_rows, grad_mid) = lax.scan(ffn_block, start_sums, numbers)
    block_output = output_rows.reshape(TOKENS, D)
    grad_mid = grad_mid.reshape(TOKENS, D)
    grad_mid_low = grad_mid.astype(jnp.bfloat16)
    grad_output_weight = jnp.dot(attended.T, grad_mid_low, preferred_element_type=jnp.float32)
    grad_attended = jnp.dot(grad_mid_low, output_weight.T, preferred_element_type=jnp.float32).astype(jnp.bfloat16)

    def backward_block(carry, number):
        pad_grad_keys, pad_grad_values = carry
        start = (number * SEQ).astype(jnp.int32)
        queries = lax.dynamic_slice_in_dim(query_rot, start, SEQ, 0)
        keys = lax.dynamic_slice_in_dim(pad_keys, start, 2 * SEQ, 0)
        values = lax.dynamic_slice_in_dim(pad_values, start, 2 * SEQ, 0)
        mixed = lax.dynamic_slice_in_dim(attended, start, SEQ, 0)
        grad_mixed = lax.dynamic_slice_in_dim(grad_attended, start, SEQ, 0)
        grad_q, grad_k, grad_v = attend_backward(queries, keys, values, window_mask(start), mixed, log_total[number], grad_mixed)
        pad_grad_keys = lax.dynamic_update_slice_in_dim(pad_grad_keys, lax.dynamic_slice_in_dim(pad_grad_keys, start, 2 * SEQ, 0) + grad_k, start, 0)
        pad_grad_values = lax.dynamic_update_slice_in_dim(pad_grad_values, lax.dynamic_slice_in_dim(pad_grad_values, start, 2 * SEQ, 0) + grad_v, start, 0)
        return ((pad_grad_keys, pad_grad_values), grad_q)
    start_pads = (jnp.zeros((TOKENS + SEQ, KV_WIDTH), jnp.float32), jnp.zeros((TOKENS + SEQ, KV_WIDTH), jnp.float32))
    (pad_grad_keys, pad_grad_values), grad_query_rot = lax.scan(backward_block, start_pads, numbers)
    grad_query_rot = grad_query_rot.reshape(TOKENS, Q_WIDTH)
    grad_keys = pad_grad_keys[SEQ:]
    grad_values = pad_grad_values[SEQ:]
    grad_query_pre = rotate_back(grad_query_rot, cosine, sine, HEADS, HEAD_SIZE)
    grad_key_pre = rotate_back(grad_keys, cosine, sine, KV_HEADS, HEAD_SIZE)
    grad_query_bias = lax.optimization_barrier(jnp.sum(grad_query_pre, axis=0))
    grad_value_bias = lax.optimization_barrier(jnp.sum(grad_values, axis=0))
    query_low = grad_query_pre.astype(jnp.bfloat16)
    key_low = grad_key_pre.astype(jnp.bfloat16)
    value_low = grad_values.astype(jnp.bfloat16)
    grad_query_weight = jnp.dot(normed_input.T, query_low, preferred_element_type=jnp.float32)
    grad_key_weight = jnp.dot(normed_input.T, key_low, preferred_element_type=jnp.float32)
    grad_value_weight = jnp.dot(normed_input.T, value_low, preferred_element_type=jnp.float32)
    grad_normed_input = jnp.dot(query_low, query_weight.T, preferred_element_type=jnp.float32) + jnp.dot(key_low, key_weight.T, preferred_element_type=jnp.float32) + jnp.dot(value_low, value_weight.T, preferred_element_type=jnp.float32)
    grad_norm_part, grad_first_gain = norm_backward(grad_normed_input, normed_one, scale_one, gain_first)
    grad_input = (grad_mid + grad_norm_part).astype(jnp.bfloat16)
    return (block_output, grad_input, grad_first_gain, grad_query_weight, grad_query_bias, grad_key_weight, grad_value_weight, grad_value_bias, grad_output_weight, ffn_sums[0], ffn_sums[1], ffn_sums[2], ffn_sums[3])
```

```python
import functools
import math

import jax
import jax.numpy as jnp
from jax import lax
from jax.experimental import pallas as pl
from jax.experimental.pallas import tpu as pltpu
from jax.sharding import PartitionSpec as P

D = 896
HEADS = 14
KV_HEADS = 2
HEAD_SIZE = 64
FF = 4864
SEQ = 1024
TOK = 128
REACH = 8
DP = 1024
UN = 38
UP = 48
UC = 32 * UP
AW = 2048

EPSILON = 1e-06
ROTARY_BASE = 1000000.0
MESH = pl.DeviceIdType.MESH
BF = jnp.bfloat16
F32 = jnp.float32
ANY = pl.BlockSpec(memory_space=pl.ANY)
VMEM = pl.BlockSpec(memory_space=pltpu.VMEM)


def place():
    f = lax.axis_index("fsdp")
    return f // 8, (f // 2) % 4, f % 2, lax.axis_index("ctx")


def plus(i, d):
    return lax.rem(i + d, 4)


def device(z, x, k, c):
    return ((z * 4 + x) * 2 + k, c)


def greet(targets):
    barrier = pltpu.get_barrier_semaphore()
    for t in targets:
        pl.semaphore_signal(barrier, inc=1, device_id=t, device_id_type=MESH)
    pl.semaphore_wait(barrier, len(targets))


class Copies:
    def __init__(self, send, recv):
        self.send, self.recv, self.count, self.all = send, recv, 0, []

    def go(self, src, dst, target):
        n = self.count
        self.count += 1
        copy = pltpu.make_async_remote_copy(
            src_ref=src,
            dst_ref=dst,
            send_sem=self.send.at[n],
            recv_sem=self.recv.at[n],
            device_id=target,
            device_id_type=MESH,
        )
        copy.start()
        self.all.append(copy)
        return copy

    def finish(self):
        for copy in self.all:
            copy.wait_send()


def gather_kernel(a, d, g, u, t, ao, do, go, uo, to, send, recv, loc):
    z, x, k, c = place()
    zs = [device(plus(z, i), x, k, c) for i in (1, 2, 3)]
    xs = [device(z, plus(x, i), k, c) for i in (1, 2, 3)]
    ys = [device(z, x, k, plus(c, i)) for i in (1, 2, 3)]
    sibling = device(z, x, 1 - k, c)
    own = []
    for n, (src, out) in enumerate(((a, ao), (d, do), (g, go), (u, uo))):
        own.append(pltpu.make_async_copy(src, out.at[z, x, k], loc.at[n]))
    own.append(pltpu.make_async_copy(t, to.at[c], loc.at[4]))
    for copy in own:
        copy.start()
    greet(zs + xs + ys + [sibling])
    cp = Copies(send, recv)
    plan = ((a, ao, 0, own[0]), (g, go, 1, own[2]), (d, do, 0, own[1]), (u, uo, 1, own[3]))
    first = []
    for src, out, way, _ in plan:
        peers = xs if way else zs
        first.append([cp.go(src, out.at[z, x, k], p) for p in peers])
    tokens = [cp.go(t, to.at[c], p) for p in ys]
    second, third = [], []
    for (src, out, way, local), copies in zip(plan, first):
        local.wait()
        for copy in copies:
            copy.wait_recv()
        part = out.at[z, :, k] if way else out.at[:, x, k]
        second.append([cp.go(part, part, p) for p in (zs if way else xs)])
        third.append(cp.go(part, part, sibling))
    for (src, out, way, _), copies in zip(plan, second):
        for i, copy in zip((1, 2, 3), copies):
            copy.wait_recv()
            part = out.at[plus(z, 4 - i), :, k] if way else out.at[:, plus(x, 4 - i), k]
            third.append(cp.go(part, part, sibling))
    own[4].wait()
    for copy in tokens + third:
        copy.wait_recv()
    cp.finish()


def gather(a, d, g, u, t):
    def out(s):
        return jax.ShapeDtypeStruct((4, 4, 2) + s.shape, BF)

    return pl.pallas_call(
        gather_kernel,
        out_shape=[out(a), out(d), out(g), out(u), jax.ShapeDtypeStruct((4,) + t.shape, BF)],
        in_specs=[ANY] * 5,
        out_specs=[ANY] * 5,
        scratch_shapes=[
            pltpu.SemaphoreType.DMA((43,)),
            pltpu.SemaphoreType.DMA((43,)),
            pltpu.SemaphoreType.DMA((5,)),
        ],
        compiler_params=pltpu.CompilerParams(collective_id=0, has_side_effects=True),
        name="gather_weights",
    )(a, d, g, u, t)


def stretch_device(i):
    i = lax.rem(i + 128, 128)
    return (i // 4, lax.rem(i, 4))


def window_kernel(kv, out, send, recv):
    me = lax.axis_index("fsdp") * 4 + lax.axis_index("ctx")
    barrier = pltpu.get_barrier_semaphore()
    for o in range(1, REACH + 1):
        pl.semaphore_signal(
            barrier, inc=1, device_id=stretch_device(me - o), device_id_type=MESH
        )
    pl.semaphore_wait(barrier, REACH)
    cp = Copies(send, recv)
    copies = [
        cp.go(kv, out.at[REACH - o], stretch_device(me + o)) for o in range(REACH, 0, -1)
    ]
    out[REACH] = kv[...]
    for copy in copies:
        copy.wait_recv()
    cp.finish()


def window(kv):
    return pl.pallas_call(
        window_kernel,
        out_shape=jax.ShapeDtypeStruct((REACH + 1,) + kv.shape, BF),
        in_specs=[VMEM],
        out_specs=VMEM,
        scratch_shapes=[pltpu.SemaphoreType.DMA((REACH,)), pltpu.SemaphoreType.DMA((REACH,))],
        compiler_params=pltpu.CompilerParams(collective_id=1, has_side_effects=True),
        name="window_keys_values",
    )(kv)


def back_kernel(own, parts, out, got, send, recv):
    me = lax.axis_index("fsdp") * 4 + lax.axis_index("ctx")
    barrier = pltpu.get_barrier_semaphore()
    for o in range(1, REACH + 1):
        pl.semaphore_signal(
            barrier, inc=1, device_id=stretch_device(me + o), device_id_type=MESH
        )
    pl.semaphore_wait(barrier, REACH)
    cp = Copies(send, recv)
    copies = [
        cp.go(parts.at[REACH - o], got.at[o - 1], stretch_device(me - o))
        for o in range(REACH, 0, -1)
    ]
    for copy in copies:
        copy.wait_recv()
    total = own[...]
    for o in range(REACH):
        total = total + got[o].astype(F32)
    out[...] = total
    cp.finish()


def back(own, parts):
    return pl.pallas_call(
        back_kernel,
        out_shape=jax.ShapeDtypeStruct(own.shape, F32),
        in_specs=[VMEM, VMEM],
        out_specs=VMEM,
        scratch_shapes=[
            pltpu.VMEM((REACH,) + own.shape, BF),
            pltpu.SemaphoreType.DMA((REACH,)),
            pltpu.SemaphoreType.DMA((REACH,)),
        ],
        compiler_params=pltpu.CompilerParams(collective_id=2, has_side_effects=True),
        name="window_grads",
    )(own, parts)


def tokens_kernel(t, out, send, recv):
    z, x, k, c = place()
    ys = [device(z, x, k, plus(c, i)) for i in (1, 2, 3)]
    greet(ys)
    cp = Copies(send, recv)
    copies = [cp.go(t, out.at[c], p) for p in ys]
    out[c] = t[...]
    for copy in copies:
        copy.wait_recv()
    cp.finish()


def tokens_gather(t):
    return pl.pallas_call(
        tokens_kernel,
        out_shape=jax.ShapeDtypeStruct((4,) + t.shape, BF),
        in_specs=[VMEM],
        out_specs=VMEM,
        scratch_shapes=[pltpu.SemaphoreType.DMA((3,)), pltpu.SemaphoreType.DMA((3,))],
        compiler_params=pltpu.CompilerParams(collective_id=3, has_side_effects=True),
        name="gather_tokens",
    )(t)


def tokens_sum_kernel(p, q, po, qo, pg, qg, send, recv):
    z, x, k, c = place()
    ys = [device(z, x, k, plus(c, i)) for i in (1, 2, 3)]
    greet(ys)
    cp = Copies(send, recv)
    first = [cp.go(q.at[plus(c, i)], qg.at[i - 1], ys[i - 1]) for i in (1, 2, 3)]
    second = [cp.go(p.at[plus(c, i)], pg.at[i - 1], ys[i - 1]) for i in (1, 2, 3)]
    for copies, src, got, out in ((first, q, qg, qo), (second, p, pg, po)):
        for copy in copies:
            copy.wait_recv()
        total = src[c].astype(F32)
        for i in range(3):
            total = total + got[i].astype(F32)
        out[...] = total
    cp.finish()


def tokens_sum(p, q):
    rows = p.shape[1:]
    return pl.pallas_call(
        tokens_sum_kernel,
        out_shape=[jax.ShapeDtypeStruct(rows, F32)] * 2,
        in_specs=[VMEM, VMEM],
        out_specs=[VMEM, VMEM],
        scratch_shapes=[
            pltpu.VMEM((3,) + rows, BF),
            pltpu.VMEM((3,) + rows, BF),
            pltpu.SemaphoreType.DMA((6,)),
            pltpu.SemaphoreType.DMA((6,)),
        ],
        compiler_params=pltpu.CompilerParams(collective_id=4, has_side_effects=True),
        name="scatter_tokens",
    )(p, q)


def scatter_kernel(ways, *refs):
    n = len(ways)
    ins, refs = refs[:n], refs[n:]
    outs, refs = refs[:n], refs[n:]
    own, refs = refs[:n], refs[n:]
    got1, refs = refs[:n], refs[n:]
    got2, refs = refs[:n], refs[n:]
    sum2, refs = refs[:n], refs[n:]
    got3, refs = refs[:n], refs[n:]
    fin_a, fin_g, fin_u, got_y, send, recv, loc = refs
    z, x, k, c = place()
    zs = [device(plus(z, i), x, k, c) for i in (1, 2, 3)]
    xs = [device(z, plus(x, i), k, c) for i in (1, 2, 3)]
    ys = [device(z, x, k, plus(c, i)) for i in (1, 2, 3)]
    sibling = device(z, x, 1 - k, c)

    def spot(m, i):
        return plus(z if ways[m] else x, i)

    def piece(ref, m, p, *more):
        return ref.at[(p, slice(None)) + more] if ways[m] else ref.at[(slice(None), p) + more]

    local = {}
    for i in (1, 2, 3, 0):
        for m in range(n):
            p = spot(m, i)
            copy = pltpu.make_async_copy(
                piece(ins[m], m, p, k), piece(own[m], m, p), loc.at[m * 4 + i]
            )
            copy.start()
            local[m, i] = copy
    greet(zs + xs + ys + [sibling])
    cp = Copies(send, recv)
    first, second, third = {}, {}, {}
    for i in (1, 2, 3, 0):
        for m in range(n):
            p = spot(m, i)
            first[m, i] = cp.go(piece(ins[m], m, p, 1 - k), piece(got1[m], m, p), sibling)
    for i in (1, 2, 3, 0):
        for m in range(n):
            p = spot(m, i)
            local[m, i].wait()
            first[m, i].wait_recv()

            def add(j, carry, m=m, p=p):
                at = (p, j) if ways[m] else (j, p)
                own[m][at] = (own[m][at].astype(F32) + got1[m][at].astype(F32)).astype(BF)
                return carry

            lax.fori_loop(0, 4, add, 0)
            if i:
                peer = (zs if ways[m] else xs)[i - 1]
                second[m, i] = cp.go(piece(own[m], m, p), got2[m].at[i - 1], peer)
    for m in range(n):
        for i in (1, 2, 3):
            second[m, i].wait_recv()
        p = spot(m, 0)

        def add(j, carry, m=m, p=p):
            at = (p, j) if ways[m] else (j, p)
            total = own[m][at].astype(F32)
            for i in range(3):
                total = total + got2[m][i, j].astype(F32)
            sum2[m][j] = total.astype(BF)
            return carry

        lax.fori_loop(0, 4, add, 0)
        for i in (1, 2, 3):
            q = plus(x if ways[m] else z, i)
            peer = (xs if ways[m] else zs)[i - 1]
            third[m, i] = cp.go(sum2[m].at[q], got3[m].at[i - 1], peer)
    last = []
    fins = (fin_a, fin_g, None, fin_u)
    for m in range(n):
        for i in (1, 2, 3):
            third[m, i].wait_recv()
        total = sum2[m][x if ways[m] else z].astype(F32)
        for i in range(3):
            total = total + got3[m][i].astype(F32)
        fin = fins[m]
        if fin is None:
            outs[m][...] = total
            continue
        fin[...] = total.reshape(fin.shape)
        for i in (1, 2, 3):
            target = got_y.at[i - 1] if m == 0 else outs[m].at[c]
            last.append(cp.go(fin.at[plus(c, i)], target, ys[i - 1]))
        if m:
            outs[m][c] = fin[c]
    for copy in last:
        copy.wait_recv()
    total = fin_a[c]
    for i in range(3):
        total = total + got_y[i]
    outs[0][...] = total
    cp.finish()


def scatter(a, g, d, u):
    arrays = [a, g, d, u]
    ways = (0, 1, 0, 1)
    shapes = [s.shape[3:] for s in arrays]
    outs = [(8, AW), (4, 8, UC), (UP, D), (4, 8, UC)]
    scratch = []
    for lead in ((4, 4), (4, 4), (3, 4), (4,), (3,)):
        scratch += [pltpu.VMEM(lead + s, BF) for s in shapes]
    scratch += [
        pltpu.VMEM((4, 8, AW), F32),
        pltpu.VMEM((4, 8, UC), F32),
        pltpu.VMEM((4, 8, UC), F32),
        pltpu.VMEM((3, 8, AW), F32),
        pltpu.SemaphoreType.DMA((49,)),
        pltpu.SemaphoreType.DMA((49,)),
        pltpu.SemaphoreType.DMA((16,)),
    ]
    return pl.pallas_call(
        functools.partial(scatter_kernel, ways),
        out_shape=[jax.ShapeDtypeStruct(s, F32) for s in outs],
        in_specs=[ANY] * 4,
        out_specs=[VMEM] * 4,
        scratch_shapes=scratch,
        compiler_params=pltpu.CompilerParams(
            collective_id=5, has_side_effects=True, vmem_limit_bytes=48 * 1024 * 1024
        ),
        name="scatter_grads",
    )(*arrays)


def rotary_tables(positions, head_size):
    half = head_size // 2
    frequency = ROTARY_BASE ** (-(jnp.arange(half, dtype=F32) * 2.0 / head_size))
    angles = positions.astype(F32)[:, None] * frequency[None, :]
    return (jnp.cos(angles), jnp.sin(angles))


def rotate(values, cosine, sine, heads, head_size):
    count = values.shape[0]
    shaped = values.reshape(count, heads, head_size)
    half = head_size // 2
    first = shaped[..., :half]
    second = shaped[..., half:]
    cos_rows = cosine[:, None, :]
    sin_rows = sine[:, None, :]
    turned = jnp.concatenate(
        [first * cos_rows - second * sin_rows, second * cos_rows + first * sin_rows], axis=-1
    )
    return turned.reshape(count, heads * head_size)


def norm_forward(values):
    factor = lax.rsqrt(jnp.mean(values * values, axis=-1, keepdims=True) + EPSILON)
    return (values * factor, factor)


def norm_backward(grad_out, normed, factor, gain):
    grad_normed = grad_out * gain
    inner = jnp.mean(grad_normed * normed, axis=-1, keepdims=True)
    return (factor * (grad_normed - normed * inner), jnp.sum(grad_out * normed, axis=0))


def attend_forward(queries, keys, values, allowed):
    count = queries.shape[0]
    scale = 1.0 / math.sqrt(HEAD_SIZE)
    shaped_q = queries.reshape(count, KV_HEADS, HEADS // KV_HEADS, HEAD_SIZE)
    shaped_k = keys.reshape(-1, KV_HEADS, HEAD_SIZE)
    shaped_v = values.reshape(-1, KV_HEADS, HEAD_SIZE)
    scores = jnp.einsum("qghd,kgd->ghqk", shaped_q, shaped_k, preferred_element_type=F32) * scale
    scores = jnp.where(allowed[None, None], scores, -jnp.inf)
    top = jnp.max(scores, axis=-1, keepdims=True)
    log_total = top + jnp.log(jnp.sum(jnp.exp(scores - top), axis=-1, keepdims=True))
    probability = jnp.exp(scores - log_total).astype(BF)
    mixed = jnp.einsum("ghqk,kgd->qghd", probability, shaped_v, preferred_element_type=F32)
    return (mixed.reshape(count, HEADS * HEAD_SIZE).astype(BF), log_total)


def attend_backward(queries, keys, values, allowed, mixed, log_total, grad_mixed):
    count = queries.shape[0]
    scale = 1.0 / math.sqrt(HEAD_SIZE)
    shaped_q = queries.reshape(count, KV_HEADS, HEADS // KV_HEADS, HEAD_SIZE)
    shaped_k = keys.reshape(-1, KV_HEADS, HEAD_SIZE)
    shaped_v = values.reshape(-1, KV_HEADS, HEAD_SIZE)
    scores = jnp.einsum("qghd,kgd->ghqk", shaped_q, shaped_k, preferred_element_type=F32) * scale
    scores = jnp.where(allowed[None, None], scores, -jnp.inf)
    probability = jnp.exp(scores - log_total)
    probability_low = probability.astype(BF)
    shaped_g = grad_mixed.reshape(count, KV_HEADS, HEADS // KV_HEADS, HEAD_SIZE)
    shaped_m = mixed.reshape(count, KV_HEADS, HEADS // KV_HEADS, HEAD_SIZE)
    delta = jnp.sum(shaped_g.astype(F32) * shaped_m.astype(F32), axis=-1)
    delta = jnp.transpose(delta, (1, 2, 0))[..., None]
    grad_prob = jnp.einsum("qghd,kgd->ghqk", shaped_g, shaped_v, preferred_element_type=F32)
    grad_scores = (probability * (grad_prob - delta)).astype(BF)
    grad_q = (
        jnp.einsum("ghqk,kgd->qghd", grad_scores, shaped_k, preferred_element_type=F32) * scale
    )
    grad_k = (
        jnp.einsum("ghqk,qghd->kgd", grad_scores, shaped_q, preferred_element_type=F32) * scale
    )
    grad_v = jnp.einsum("ghqk,qghd->kgd", probability_low, shaped_g, preferred_element_type=F32)
    width = KV_HEADS * HEAD_SIZE
    return (
        grad_q.reshape(count, HEADS * HEAD_SIZE),
        grad_k.reshape(-1, width),
        grad_v.reshape(-1, width),
    )


def dot(a, b):
    return jnp.dot(a, b, preferred_element_type=F32)


def dot_t(a, b):
    return lax.dot_general(a, b, (((1,), (1,)), ((), ())), preferred_element_type=F32)


def t_dot(a, b):
    return lax.dot_general(a, b, (((0,), (0,)), ((), ())), preferred_element_type=F32)


def choose(flags):
    return flags.astype(BF)


def local(
    block_input,
    positions,
    first_gain,
    query_weight,
    query_bias,
    key_weight,
    value_weight,
    value_bias,
    output_weight,
    second_gain,
    gate_weight,
    up_weight,
    down_weight,
    cotangent,
):
    f = lax.axis_index("fsdp")
    c = lax.axis_index("ctx")
    stretch = f * 4 + c

    i28 = jnp.arange(28)
    spread28 = choose((i28 + i28 // 7)[None, :] == jnp.arange(32)[:, None])
    i896 = jnp.arange(D)
    spread = choose((i896 + i896 // 7)[:, None] == jnp.arange(DP)[None, :])
    j768 = jnp.arange(16 * UP)
    wanted = jnp.where(j768 % UP < UN, (j768 // UP) * 152 + j768 % UP, -1000) + UN * c
    units = choose(wanted[None, :] == jnp.arange(2432)[:, None])
    j48 = jnp.arange(UP)
    down_rows = choose(
        jnp.where(j48 < UN, j48 + UN * c, -1)[:, None] == jnp.arange(152)[None, :]
    )

    zero = jnp.int32(0)
    own_a = dot(
        spread28, jnp.concatenate([query_weight, key_weight, value_weight, output_weight], axis=1)
    ).astype(BF)
    extra = jnp.zeros((1, AW), BF)
    extra = lax.dynamic_update_slice(extra, query_bias[None, :], (zero, 28 * f))
    extra = lax.dynamic_update_slice(extra, value_bias[None, :], (zero, 1024 + 4 * f))
    extra = lax.dynamic_update_slice(extra, first_gain[None, :], (zero, 1152 + 28 * f))
    gain_row = lax.dynamic_update_slice(
        jnp.zeros((1, AW), BF), second_gain[None, :], (zero, 1152 + 28 * f)
    )
    row32 = jnp.arange(32)[:, None]
    own_a = jnp.where(row32 == 7, extra, jnp.where(row32 == 15, gain_row, own_a))
    both = jnp.concatenate([gate_weight, up_weight], axis=0).reshape(112, 2432)
    both = dot(both, units).astype(BF).reshape(2, 28, UC)
    own_g = dot(spread28, both[0]).astype(BF)
    own_u = dot(spread28, both[1]).astype(BF)
    own_d = dot(down_rows, down_weight).astype(BF)

    all_a, all_d, all_g, all_u, cot_all = gather(own_a, own_d, own_g, own_u, cotangent)
    rows_a = all_a.reshape(32, 32, AW)
    gain_first = jnp.sum(rows_a[:, 7, 1152:].astype(F32), axis=0)
    gain_second = jnp.sum(rows_a[:, 15, 1152:].astype(F32), axis=0)
    all_a = all_a.reshape(DP, AW)
    all_g = all_g.reshape(DP, UC)
    all_u = all_u.reshape(DP, UC)
    all_d = all_d.reshape(UC, D)
    cot_all = cot_all.reshape(4 * TOK, D)
    weight_output = all_a[:, 1152:]
    pad_ones = (jnp.arange(DP) % 8 == 7).astype(F32)[None, :]

    residual_in = block_input.astype(F32)
    normed_one, scale_one = norm_forward(residual_in)
    normed_input = (normed_one * gain_first).astype(BF)
    input_pad = (dot(normed_input, spread) + pad_ones).astype(BF)
    qkv = dot(input_pad, all_a[:, :1152])
    cosine, sine = rotary_tables(positions, HEAD_SIZE)
    query_rot = rotate(qkv[:, :896], cosine, sine, HEADS, HEAD_SIZE).astype(BF)
    key_rot = rotate(qkv[:, 896:1024], cosine, sine, KV_HEADS, HEAD_SIZE).astype(BF)
    value_rows = qkv[:, 1024:].astype(BF)
    seen = window(jnp.concatenate([key_rot, value_rows], axis=1))
    seen = seen.reshape((REACH + 1) * TOK, 256)
    window_keys, window_values = seen[:, :128], seen[:, 128:]
    query_index = stretch * TOK + jnp.arange(TOK, dtype=jnp.int32)
    key_index = (stretch - REACH) * TOK + jnp.arange((REACH + 1) * TOK, dtype=jnp.int32)
    first_index = query_index - positions
    allowed = (key_index[None, :] >= first_index[:, None]) & (
        key_index[None, :] <= query_index[:, None]
    )
    attended, log_total = attend_forward(query_rot, window_keys, window_values, allowed)
    attended_pad = dot(attended, spread).astype(BF)
    residual_mid = residual_in + dot(attended_pad, weight_output)

    normed_two, scale_two = norm_forward(residual_mid)
    normed_mid = (normed_two * gain_second).astype(BF)
    mid_all = tokens_gather(normed_mid).reshape(4 * TOK, D)
    mid_pad = dot(mid_all, spread).astype(BF)
    gate_pre = dot(mid_pad, all_g)
    up_pre = dot(mid_pad, all_u)
    sigma = jax.nn.sigmoid(gate_pre)
    hidden = (gate_pre * sigma * up_pre).astype(BF)
    out_part = dot(hidden, all_d).astype(BF)
    grad_hidden = dot_t(cot_all, all_d)
    grad_gate_pre = (grad_hidden * up_pre * sigma * (1.0 + gate_pre * (1.0 - sigma))).astype(BF)
    grad_up_pre = (grad_hidden * gate_pre * sigma).astype(BF)
    mid_part = (dot_t(grad_gate_pre, all_g) + dot_t(grad_up_pre, all_u)).astype(BF)
    mid_part = dot_t(mid_part, spread).astype(BF)
    out_sum, grad_normed_mid = tokens_sum(
        out_part.reshape(4, TOK, D), mid_part.reshape(4, TOK, D)
    )
    block_output = (residual_mid + out_sum).astype(BF)
    grad_down = t_dot(hidden, cot_all).astype(BF)
    grad_gate = t_dot(mid_pad, grad_gate_pre).astype(BF)
    grad_up = t_dot(mid_pad, grad_up_pre).astype(BF)
    grad_norm_part, grad_gain_two = norm_backward(
        grad_normed_mid, normed_two, scale_two, gain_second
    )
    grad_mid = cotangent.astype(F32) + grad_norm_part

    grad_mid_low = grad_mid.astype(BF)
    grad_output_w = t_dot(attended_pad, grad_mid_low)
    grad_attended = dot_t(dot_t(grad_mid_low, weight_output).astype(BF), spread).astype(BF)
    grad_query_rot, grad_window_keys, grad_window_values = attend_backward(
        query_rot, window_keys, window_values, allowed, attended, log_total, grad_attended
    )
    grad_window = jnp.concatenate([grad_window_keys, grad_window_values], axis=1)
    grad_window = grad_window.reshape(REACH + 1, TOK, 256)
    grad_kv = back(grad_window[REACH], grad_window[:REACH].astype(BF))
    query_low = rotate(grad_query_rot, cosine, -sine, HEADS, HEAD_SIZE).astype(BF)
    key_low = rotate(grad_kv[:, :128], cosine, -sine, KV_HEADS, HEAD_SIZE).astype(BF)
    value_low = grad_kv[:, 128:].astype(BF)
    lows = jnp.concatenate([query_low, key_low, value_low], axis=1)
    grad_qkv_w = t_dot(input_pad, lows)
    grad_normed_input = dot_t(dot_t(lows, all_a[:, :1152]).astype(BF), spread)
    grad_in_part, grad_gain_one = norm_backward(
        grad_normed_input, normed_one, scale_one, gain_first
    )
    grad_input = (grad_mid + grad_in_part).astype(BF)

    group = jnp.arange(DP)[:, None] // 8
    gains = jnp.where(
        i896[None, :] // 7 == group, grad_gain_one[None, :], jnp.roll(grad_gain_two, 448)[None, :]
    )
    grad_output_w = jnp.where(jnp.arange(DP)[:, None] % 8 == 7, gains, grad_output_w)
    grad_a = jnp.concatenate([grad_qkv_w, grad_output_w], axis=1).astype(BF)

    sum_a, sum_g, sum_d, sum_u = scatter(
        grad_a.reshape(4, 4, 2, 32, AW),
        grad_gate.reshape(4, 4, 2, 32, UC),
        grad_down.reshape(4, 4, 2, UP, D),
        grad_up.reshape(4, 4, 2, 32, UC),
    )

    def columns(parts):
        parts = parts[:, :7].reshape(4, 7, 32, UP)[..., :UN]
        return jnp.transpose(parts, (1, 2, 0, 3)).reshape(7, FF)

    vectors = sum_a[7]
    at = 7 * stretch
    return (
        block_output,
        grad_input,
        lax.dynamic_slice(vectors, (1152 + at,), (7,)),
        sum_a[:7, :896],
        lax.dynamic_slice(vectors, (at,), (7,)),
        sum_a[:7, 896:1024],
        sum_a[:7, 1024:1152],
        lax.dynamic_slice(vectors, (1024 + stretch,), (1,)),
        sum_a[:7, 1152:],
        lax.dynamic_slice(vectors, (1152 + lax.rem(at + 448, 896),), (7,)),
        columns(sum_g),
        columns(sum_u),
        sum_d[:UN],
    )


def solution(mesh):
    tokens = P(("fsdp", "ctx"), None)
    entries = P(("fsdp", "ctx"))
    rows = P("fsdp", None)
    vector = P("fsdp")
    in_specs = (
        tokens,
        entries,
        vector,
        rows,
        vector,
        rows,
        rows,
        vector,
        rows,
        vector,
        rows,
        rows,
        rows,
        tokens,
    )
    out_specs = (
        tokens,
        tokens,
        entries,
        tokens,
        entries,
        tokens,
        tokens,
        entries,
        tokens,
        entries,
        tokens,
        tokens,
        tokens,
    )
    return jax.shard_map(local, mesh=mesh, in_specs=in_specs, out_specs=out_specs, check_vma=False)
```

```python
import functools
import math

import jax
import jax.numpy as jnp
from jax import lax
from jax.experimental import pallas as pl
from jax.experimental.pallas import tpu as pltpu
from jax.sharding import PartitionSpec as P

D = 896
HEADS = 14
KV_HEADS = 2
HEAD_SIZE = 64
FF = 4864
SEQ = 1024
TOK = 128
REACH = 8
DP = 1024
UN = 38
UP = 48
UC = 32 * UP
AW = 2048

EPSILON = 1e-06
ROTARY_BASE = 1000000.0
MESH = pl.DeviceIdType.MESH
BF = jnp.bfloat16
F32 = jnp.float32
ANY = pl.BlockSpec(memory_space=pl.ANY)
VMEM = pl.BlockSpec(memory_space=pltpu.VMEM)


def place():
    f = lax.axis_index("fsdp")
    return f // 8, (f // 2) % 4, f % 2, lax.axis_index("ctx")


def plus(i, d):
    return lax.rem(i + d, 4)


def device(z, x, k, c):
    return ((z * 4 + x) * 2 + k, c)


def greet(targets):
    barrier = pltpu.get_barrier_semaphore()
    for t in targets:
        pl.semaphore_signal(barrier, inc=1, device_id=t, device_id_type=MESH)
    pl.semaphore_wait(barrier, len(targets))


class Copies:
    def __init__(self, send, recv):
        self.send, self.recv, self.count, self.all = send, recv, 0, []

    def go(self, src, dst, target):
        n = self.count
        self.count += 1
        copy = pltpu.make_async_remote_copy(
            src_ref=src,
            dst_ref=dst,
            send_sem=self.send.at[n],
            recv_sem=self.recv.at[n],
            device_id=target,
            device_id_type=MESH,
        )
        copy.start()
        self.all.append(copy)
        return copy

    def finish(self):
        for copy in self.all:
            copy.wait_send()


class RingGather:
    def __init__(self, cp, part, own, p, up, down):
        self.cp, self.part, self.p, self.up, self.down = cp, part, p, up, down
        self.up0 = cp.go(own(0), part(p, 0), up)
        self.down1 = cp.go(own(1), part(p, 1), down)
        self.up1 = cp.go(own(1), part(p, 1), up)
        self.down0 = cp.go(own(0), part(p, 0), down)

    def forward(self):
        self.up0.wait_recv()
        ref = self.part(plus(self.p, 3), 0)
        self.far0 = self.cp.go(ref, ref, self.up)
        self.down1.wait_recv()
        ref = self.part(plus(self.p, 1), 1)
        self.far1 = self.cp.go(ref, ref, self.down)

    def near(self):
        self.up1.wait_recv()
        self.down0.wait_recv()

    def far(self):
        self.far0.wait_recv()
        self.far1.wait_recv()


class RingScatter:
    def __init__(self, cp, send, add, p, up, down, far, near):
        self.cp, self.send, self.add, self.p, self.up, self.down = cp, send, add, p, up, down
        self.far, self.near = far, near
        self.far0 = cp.go(send(plus(p, 2), 0), far[0], up)
        self.far1 = cp.go(send(plus(p, 2), 1), far[1], down)

    def plain(self):
        self.up1 = self.cp.go(self.send(plus(self.p, 1), 1), self.near[0](1), self.up)
        self.down0 = self.cp.go(self.send(plus(self.p, 3), 0), self.near[1](0), self.down)

    def forward(self):
        self.far0.wait_recv()
        ref = self.add(plus(self.p, 1), 0, self.far[0])
        self.up0 = self.cp.go(ref, self.near[0](0), self.up)
        self.far1.wait_recv()
        ref = self.add(plus(self.p, 3), 1, self.far[1])
        self.down1 = self.cp.go(ref, self.near[1](1), self.down)

    def finish(self):
        for copy in (self.up1, self.down0, self.up0, self.down1):
            copy.wait_recv()


def halves(rows):
    first = rows // 2 // 16 * 16
    return (pl.ds(0, first), pl.ds(first, rows - first))


def pack_kernel(qkv, o, gate, up, down, bias, gains, a_out, o_out, g_out, u_out, d_out, units):
    f, c = lax.axis_index("fsdp"), lax.axis_index("ctx")

    def iota(shape, axis):
        return lax.broadcasted_iota(jnp.int32, shape, axis)

    def where(flags):
        return flags.astype(F32).astype(BF)

    i = iota((32, 28), 1)
    spread = where(i + i // 7 == iota((32, 28), 0))
    row = iota((32, 1), 0)
    i, j = iota((32, 1152), 0), iota((32, 1152), 1)
    spot = jnp.where(i < 28, 28 * f + i, 1024 + 4 * f + i - 28)
    extra = dot(bias[...], where(spot == j))
    a_out[...] = (dot(spread, qkv[...]) + jnp.where(row == 7, extra, 0.0)).astype(BF)
    i, j = iota((28, D), 0), iota((28, D), 1)
    extra = dot(gains[...], where(28 * f + i == j))
    o_out[...] = (
        dot(spread, o[...])
        + jnp.where(row == 7, extra[0:1], 0.0)
        + jnp.where(row == 15, extra[1:2], 0.0)
    ).astype(BF)
    j = iota((1, 16 * UP), 1)
    wanted = jnp.where(j % UP < UN, (j // UP) * 152 + j % UP, -1000) + UN * c
    for r in range(19):
        rows = iota((128, 16 * UP), 0) + r * 128
        units[r * 128 : (r + 1) * 128] = where(rows == wanted)
    for src, out in ((gate, g_out), (up, u_out)):
        wide = dot(spread, src[...]).astype(BF)
        for h in range(2):
            part = dot(wide[:, h * 2432 : (h + 1) * 2432], units[...])
            out[:, h * 768 : (h + 1) * 768] = part.astype(BF)
    i, j = iota((UP, 152), 0), iota((UP, 152), 1)
    d_out[...] = dot(where(jnp.where(i < UN, i + UN * c, -1) == j), down[...]).astype(BF)


def pack(*args):
    shapes = ((32, 1152), (32, D), (32, UC), (32, UC), (UP, D))
    return pl.pallas_call(
        pack_kernel,
        out_shape=[jax.ShapeDtypeStruct(s, BF) for s in shapes],
        in_specs=[VMEM] * 7,
        out_specs=[VMEM] * 5,
        scratch_shapes=[pltpu.VMEM((2432, 16 * UP), BF)],
        compiler_params=pltpu.CompilerParams(vmem_limit_bytes=32 * 1024 * 1024),
        name="pack_weights",
    )(*args)


def gather_kernel(ways, *refs):
    n = len(ways)
    ins, t, refs = refs[:n], refs[n], refs[n + 1 :]
    outs, to, (send, recv, loc) = refs[:n], refs[n], refs[n + 1 :]
    z, x, k, c = place()
    zs = [device(plus(z, i), x, k, c) for i in (1, 3)]
    xs = [device(z, plus(x, i), k, c) for i in (1, 3)]
    ys = [device(z, x, k, plus(c, i)) for i in (1, 3)]
    sibling = device(z, x, 1 - k, c)
    own = [
        pltpu.make_async_copy(src, out.at[z, x, k], loc.at[m])
        for m, (src, out) in enumerate(zip(ins, outs))
    ]
    own.append(pltpu.make_async_copy(t, to.at[c], loc.at[n]))
    for copy in own:
        copy.start()
    greet(zs + xs + ys + [sibling])
    cp = Copies(send, recv)
    first, second, third = [], [], []
    for m in range(n):
        rows = halves(ins[m].shape[0])

        def part(p, h, m=m, rows=rows):
            return outs[m].at[z, p, k, rows[h]] if ways[m] else outs[m].at[p, x, k, rows[h]]

        def mine(h, m=m, rows=rows):
            return ins[m].at[rows[h]]

        first.append(RingGather(cp, part, mine, x if ways[m] else z, *(xs if ways[m] else zs)))
    rows = halves(t.shape[0])
    tokens = RingGather(cp, lambda p, h: to.at[p, rows[h]], lambda h: t.at[rows[h]], c, *ys)
    for m in range(n):
        first[m].forward()
    tokens.forward()
    for m in range(n):
        own[m].wait()
        first[m].near()
        first[m].far()

        def part(p, h, m=m):
            some = pl.ds(2 * h, 2)
            return outs[m].at[p, some, k] if ways[m] else outs[m].at[some, p, k]

        p = z if ways[m] else x
        second.append(
            RingGather(cp, part, functools.partial(part, p), p, *(zs if ways[m] else xs))
        )

    def pass_on(m, i):
        p = plus(z if ways[m] else x, i)
        ref = outs[m].at[p, :, k] if ways[m] else outs[m].at[:, p, k]
        third.append(cp.go(ref, ref, sibling))

    for m in range(n):
        pass_on(m, 0)
    for m in range(n):
        second[m].forward()
    for m in range(n):
        second[m].near()
        pass_on(m, 1)
        pass_on(m, 3)
    for m in range(n):
        second[m].far()
        pass_on(m, 2)
    tokens.near()
    tokens.far()
    own[n].wait()
    for copy in third:
        copy.wait_recv()
    cp.finish()


def gather(arrays, ways, t):
    n = len(arrays)
    outs = [jax.ShapeDtypeStruct((4, 4, 2) + s.shape, BF) for s in arrays]
    return pl.pallas_call(
        functools.partial(gather_kernel, ways),
        out_shape=outs + [jax.ShapeDtypeStruct((4,) + t.shape, BF)],
        in_specs=[ANY] * (n + 1),
        out_specs=[ANY] * (n + 1),
        scratch_shapes=[
            pltpu.SemaphoreType.DMA((16 * n + 6,)),
            pltpu.SemaphoreType.DMA((16 * n + 6,)),
            pltpu.SemaphoreType.DMA((n + 1,)),
        ],
        compiler_params=pltpu.CompilerParams(collective_id=0, has_side_effects=True),
        name="gather_weights",
    )(*arrays, t)


def stretch_device(i):
    i = lax.rem(i + 128, 128)
    return (i // 4, lax.rem(i, 4))


def window_kernel(kv, out, send, recv):
    me = lax.axis_index("fsdp") * 4 + lax.axis_index("ctx")
    barrier = pltpu.get_barrier_semaphore()
    for o in range(1, REACH + 1):
        pl.semaphore_signal(
            barrier, inc=1, device_id=stretch_device(me - o), device_id_type=MESH
        )
    pl.semaphore_wait(barrier, REACH)
    cp = Copies(send, recv)
    copies = [
        cp.go(kv, out.at[REACH - o], stretch_device(me + o)) for o in range(REACH, 0, -1)
    ]
    out[REACH] = kv[...]
    for copy in copies:
        copy.wait_recv()
    cp.finish()


def window(kv):
    return pl.pallas_call(
        window_kernel,
        out_shape=jax.ShapeDtypeStruct((REACH + 1,) + kv.shape, BF),
        in_specs=[VMEM],
        out_specs=VMEM,
        scratch_shapes=[pltpu.SemaphoreType.DMA((REACH,)), pltpu.SemaphoreType.DMA((REACH,))],
        compiler_params=pltpu.CompilerParams(collective_id=1, has_side_effects=True),
        name="window_keys_values",
    )(kv)


def back_kernel(own, parts, out, got, send, recv):
    me = lax.axis_index("fsdp") * 4 + lax.axis_index("ctx")
    barrier = pltpu.get_barrier_semaphore()
    for o in range(1, REACH + 1):
        pl.semaphore_signal(
            barrier, inc=1, device_id=stretch_device(me + o), device_id_type=MESH
        )
    pl.semaphore_wait(barrier, REACH)
    cp = Copies(send, recv)
    copies = [
        cp.go(parts.at[REACH - o], got.at[o - 1], stretch_device(me - o))
        for o in range(REACH, 0, -1)
    ]
    for copy in copies:
        copy.wait_recv()
    total = own[...]
    for o in range(REACH):
        total = total + got[o].astype(F32)
    out[...] = total
    cp.finish()


def back(own, parts):
    return pl.pallas_call(
        back_kernel,
        out_shape=jax.ShapeDtypeStruct(own.shape, F32),
        in_specs=[VMEM, VMEM],
        out_specs=VMEM,
        scratch_shapes=[
            pltpu.VMEM((REACH,) + own.shape, BF),
            pltpu.SemaphoreType.DMA((REACH,)),
            pltpu.SemaphoreType.DMA((REACH,)),
        ],
        compiler_params=pltpu.CompilerParams(collective_id=2, has_side_effects=True),
        name="window_grads",
    )(own, parts)


def tokens_kernel(t, out, send, recv):
    z, x, k, c = place()
    ys = [device(z, x, k, plus(c, i)) for i in (1, 3)]
    greet(ys)
    cp = Copies(send, recv)
    rows = halves(t.shape[0])
    ring = RingGather(cp, lambda p, h: out.at[p, rows[h]], lambda h: t.at[rows[h]], c, *ys)
    out[c] = t[...]
    ring.forward()
    ring.near()
    ring.far()
    cp.finish()


def tokens_gather(t):
    return pl.pallas_call(
        tokens_kernel,
        out_shape=jax.ShapeDtypeStruct((4,) + t.shape, BF),
        in_specs=[VMEM],
        out_specs=VMEM,
        scratch_shapes=[pltpu.SemaphoreType.DMA((6,)), pltpu.SemaphoreType.DMA((6,))],
        compiler_params=pltpu.CompilerParams(collective_id=3, has_side_effects=True),
        name="gather_tokens",
    )(t)


def tokens_ring(cp, t, acc, far, near, c, ys):
    rows = halves(t.shape[1])

    def send(p, h):
        return t.at[p, rows[h]]

    def add(p, h, got):
        acc[h] = (t[p, rows[h]].astype(F32) + got[...].astype(F32)).astype(BF)
        return acc.at[h]

    return RingScatter(
        cp,
        send,
        add,
        c,
        *ys,
        (far.at[0], far.at[1]),
        (lambda h: near.at[0, rows[h]], lambda h: near.at[1, rows[h]]),
    )


def tokens_scratch(rows):
    half = (2, rows[0] // 2, rows[1])
    return [pltpu.VMEM(half, BF), pltpu.VMEM(half, BF), pltpu.VMEM((2,) + rows, BF)]


def tokens_sum_kernel(t, out, acc, far, near, send, recv):
    z, x, k, c = place()
    ys = [device(z, x, k, plus(c, i)) for i in (1, 3)]
    greet(ys)
    cp = Copies(send, recv)
    ring = tokens_ring(cp, t, acc, far, near, c, ys)
    ring.plain()
    ring.forward()
    ring.finish()
    out[...] = t[c].astype(F32) + near[0].astype(F32) + near[1].astype(F32)
    cp.finish()


def tokens_sum(t):
    rows = t.shape[1:]
    return pl.pallas_call(
        tokens_sum_kernel,
        out_shape=jax.ShapeDtypeStruct(rows, F32),
        in_specs=[VMEM],
        out_specs=VMEM,
        scratch_shapes=tokens_scratch(rows)
        + [pltpu.SemaphoreType.DMA((6,)), pltpu.SemaphoreType.DMA((6,))],
        compiler_params=pltpu.CompilerParams(collective_id=4, has_side_effects=True),
        name="scatter_tokens",
    )(t)


def scatter_kernel(ways, modes, *refs):
    n = len(ways)

    def take(count):
        nonlocal refs
        head, refs = refs[:count], refs[count:]
        return head

    ins, (t,) = take(n), take(1)
    outs, (t_out,) = take(n), take(1)
    own, got1, far2, near2, sum2, far3, near3, fins, gots = (take(n) for _ in range(9))
    acc, far, near, send, recv, loc = refs
    z, x, k, c = place()
    zs = [device(plus(z, i), x, k, c) for i in (1, 3)]
    xs = [device(z, plus(x, i), k, c) for i in (1, 3)]
    ys = [device(z, x, k, plus(c, i)) for i in (1, 2, 3)]
    sibling = device(z, x, 1 - k, c)

    def spot(m, i):
        return plus(z if ways[m] else x, i)

    def piece(ref, m, p, *rest):
        return ref.at[(p, slice(None)) + rest] if ways[m] else ref.at[(slice(None), p) + rest]

    local = {}
    for i in (2, 1, 3, 0):
        for m in range(n):
            p = spot(m, i)
            copy = pltpu.make_async_copy(
                piece(ins[m], m, p, k), piece(own[m], m, p), loc.at[m * 4 + i]
            )
            copy.start()
            local[m, i] = copy
    greet(zs + xs + ys + [sibling])
    cp = Copies(send, recv)
    first, second, third = {}, [], []
    for i in (2, 1, 3, 0):
        for m in range(n):
            p = spot(m, i)
            first[m, i] = cp.go(piece(ins[m], m, p, 1 - k), piece(got1[m], m, p), sibling)
    tokens = tokens_ring(cp, t, acc, far, near, c, (ys[0], ys[2]))
    tokens.plain()

    def join(m, i):
        p = spot(m, i)
        local[m, i].wait()
        first[m, i].wait_recv()

        def add(j, carry):
            at = (p, j) if ways[m] else (j, p)
            own[m][at] = (own[m][at].astype(F32) + got1[m][at].astype(F32)).astype(BF)
            return carry

        lax.fori_loop(0, 4, add, 0)

    def start(m):
        def send(p, h):
            some = pl.ds(2 * h, 2)
            return own[m].at[p, some] if ways[m] else own[m].at[some, p]

        def add(p, h, got):
            def one(j, carry):
                at = (p, 2 * h + j) if ways[m] else (2 * h + j, p)
                own[m][at] = (own[m][at].astype(F32) + got[j].astype(F32)).astype(BF)
                return carry

            lax.fori_loop(0, 2, one, 0)
            return send(p, h)

        return RingScatter(
            cp,
            send,
            add,
            spot(m, 0),
            *(zs if ways[m] else xs),
            (far2[m].at[0], far2[m].at[1]),
            (
                lambda h: near2[m].at[0, pl.ds(2 * h, 2)],
                lambda h: near2[m].at[1, pl.ds(2 * h, 2)],
            ),
        )

    for m in range(n):
        join(m, 2)
        second.append(start(m))
    for m in range(n):
        join(m, 1)
        join(m, 3)
        second[m].plain()
    for m in range(n):
        second[m].forward()
    tokens.forward()
    for m in range(n):
        join(m, 0)

    def start_third(m):
        rows = halves(sum2[m].shape[1])

        def send(p, h):
            return sum2[m].at[p, rows[h]]

        def add(p, h, got):
            sum2[m][p, rows[h]] = (sum2[m][p, rows[h]].astype(F32) + got[...].astype(F32)).astype(BF)
            return send(p, h)

        return RingScatter(
            cp,
            send,
            add,
            x if ways[m] else z,
            *(xs if ways[m] else zs),
            (far3[m].at[0, rows_of(rows[0])], far3[m].at[1, rows_of(rows[1])]),
            (lambda h: near3[m].at[0, rows[h]], lambda h: near3[m].at[1, rows[h]]),
        )

    def rows_of(some):
        return pl.ds(0, some.size)

    for m in range(n):
        second[m].finish()
        p = spot(m, 0)

        def add(j, carry, m=m, p=p):
            at = (p, j) if ways[m] else (j, p)
            total = own[m][at].astype(F32) + near2[m][0, j].astype(F32)
            sum2[m][j] = (total + near2[m][1, j].astype(F32)).astype(BF)
            return carry

        lax.fori_loop(0, 4, add, 0)
        third.append(start_third(m))
        third[m].plain()
    for m in range(n):
        third[m].forward()
    tokens.finish()
    t_out[...] = t[c].astype(F32) + near[0].astype(F32) + near[1].astype(F32)
    closing = {}
    for m in range(n):
        third[m].finish()
        total = sum2[m][x if ways[m] else z].astype(F32)
        total = total + near3[m][0].astype(F32) + near3[m][1].astype(F32)
        if modes[m] == "none":
            outs[m][...] = total
            continue
        fin = fins[m]
        fin[...] = total.reshape(fin.shape)
        for i in (1, 2, 3):
            target = gots[m].at[i - 1] if modes[m] == "sum" else outs[m].at[c]
            closing[m, i] = cp.go(fin.at[plus(c, i)], target, ys[i - 1])
        if modes[m] == "rows":
            outs[m][c] = fin[c]
    for copy in closing.values():
        copy.wait_recv()
    for m in range(n):
        if modes[m] == "sum":
            total = fins[m][c]
            for i in range(3):
                total = total + gots[m][i]
            outs[m][...] = total
    cp.finish()


def scatter(arrays, ways, modes, t):
    n = len(arrays)
    shapes = [s.shape[3:] for s in arrays]
    quarter = [(s[0] // 4, s[1]) for s in shapes]
    tiny = (8, 128)
    outs = []
    for m in range(n):
        outs.append({"none": shapes[m], "sum": quarter[m], "rows": (4,) + quarter[m]}[modes[m]])
    scratch = []
    for lead in ((4, 4), (4, 4), (2, 2), (2, 4), (4,)):
        scratch += [pltpu.VMEM(lead + s, BF) for s in shapes]
    scratch += [pltpu.VMEM((2, halves(s[0])[1].size, s[1]), BF) for s in shapes]
    scratch += [pltpu.VMEM((2,) + s, BF) for s in shapes]
    scratch += [
        pltpu.VMEM(tiny if modes[m] == "none" else (4,) + quarter[m], F32) for m in range(n)
    ]
    scratch += [
        pltpu.VMEM((3,) + quarter[m] if modes[m] == "sum" else tiny, F32) for m in range(n)
    ]
    count = sum(16 if mode == "none" else 19 for mode in modes) + 6
    scratch += tokens_scratch(t.shape[1:])
    scratch += [
        pltpu.SemaphoreType.DMA((count,)),
        pltpu.SemaphoreType.DMA((count,)),
        pltpu.SemaphoreType.DMA((4 * n,)),
    ]
    return pl.pallas_call(
        functools.partial(scatter_kernel, ways, modes),
        out_shape=[jax.ShapeDtypeStruct(s, F32) for s in outs]
        + [jax.ShapeDtypeStruct(t.shape[1:], F32)],
        in_specs=[ANY] * n + [VMEM],
        out_specs=[VMEM] * (n + 1),
        scratch_shapes=scratch,
        compiler_params=pltpu.CompilerParams(
            collective_id=5, has_side_effects=True, vmem_limit_bytes=48 * 1024 * 1024
        ),
        name="scatter_grads",
    )(*arrays, t)


def rotary_tables(positions, head_size):
    half = head_size // 2
    frequency = ROTARY_BASE ** (-(jnp.arange(half, dtype=F32) * 2.0 / head_size))
    angles = positions.astype(F32)[:, None] * frequency[None, :]
    return (jnp.cos(angles), jnp.sin(angles))


def rotate(values, cosine, sine, heads, head_size):
    count = values.shape[0]
    shaped = values.reshape(count, heads, head_size)
    half = head_size // 2
    first = shaped[..., :half]
    second = shaped[..., half:]
    cos_rows = cosine[:, None, :]
    sin_rows = sine[:, None, :]
    turned = jnp.concatenate(
        [first * cos_rows - second * sin_rows, second * cos_rows + first * sin_rows], axis=-1
    )
    return turned.reshape(count, heads * head_size)


def norm_forward(values):
    factor = lax.rsqrt(jnp.mean(values * values, axis=-1, keepdims=True) + EPSILON)
    return (values * factor, factor)


def norm_backward(grad_out, normed, factor, gain):
    grad_normed = grad_out * gain
    inner = jnp.mean(grad_normed * normed, axis=-1, keepdims=True)
    return (factor * (grad_normed - normed * inner), jnp.sum(grad_out * normed, axis=0))


def attend_forward(queries, keys, values, allowed):
    count = queries.shape[0]
    scale = 1.0 / math.sqrt(HEAD_SIZE)
    shaped_q = queries.reshape(count, KV_HEADS, HEADS // KV_HEADS, HEAD_SIZE)
    shaped_k = keys.reshape(-1, KV_HEADS, HEAD_SIZE)
    shaped_v = values.reshape(-1, KV_HEADS, HEAD_SIZE)
    scores = jnp.einsum("qghd,kgd->ghqk", shaped_q, shaped_k, preferred_element_type=F32) * scale
    scores = jnp.where(allowed[None, None], scores, -jnp.inf)
    top = jnp.max(scores, axis=-1, keepdims=True)
    log_total = top + jnp.log(jnp.sum(jnp.exp(scores - top), axis=-1, keepdims=True))
    probability = jnp.exp(scores - log_total).astype(BF)
    mixed = jnp.einsum("ghqk,kgd->qghd", probability, shaped_v, preferred_element_type=F32)
    return (mixed.reshape(count, HEADS * HEAD_SIZE).astype(BF), log_total)


def attend_backward(queries, keys, values, allowed, mixed, log_total, grad_mixed):
    count = queries.shape[0]
    scale = 1.0 / math.sqrt(HEAD_SIZE)
    shaped_q = queries.reshape(count, KV_HEADS, HEADS // KV_HEADS, HEAD_SIZE)
    shaped_k = keys.reshape(-1, KV_HEADS, HEAD_SIZE)
    shaped_v = values.reshape(-1, KV_HEADS, HEAD_SIZE)
    scores = jnp.einsum("qghd,kgd->ghqk", shaped_q, shaped_k, preferred_element_type=F32) * scale
    scores = jnp.where(allowed[None, None], scores, -jnp.inf)
    probability = jnp.exp(scores - log_total)
    probability_low = probability.astype(BF)
    shaped_g = grad_mixed.reshape(count, KV_HEADS, HEADS // KV_HEADS, HEAD_SIZE)
    shaped_m = mixed.reshape(count, KV_HEADS, HEADS // KV_HEADS, HEAD_SIZE)
    delta = jnp.sum(shaped_g.astype(F32) * shaped_m.astype(F32), axis=-1)
    delta = jnp.transpose(delta, (1, 2, 0))[..., None]
    grad_prob = jnp.einsum("qghd,kgd->ghqk", shaped_g, shaped_v, preferred_element_type=F32)
    grad_scores = (probability * (grad_prob - delta)).astype(BF)
    grad_q = (
        jnp.einsum("ghqk,kgd->qghd", grad_scores, shaped_k, preferred_element_type=F32) * scale
    )
    grad_k = (
        jnp.einsum("ghqk,qghd->kgd", grad_scores, shaped_q, preferred_element_type=F32) * scale
    )
    grad_v = jnp.einsum("ghqk,qghd->kgd", probability_low, shaped_g, preferred_element_type=F32)
    width = KV_HEADS * HEAD_SIZE
    return (
        grad_q.reshape(count, HEADS * HEAD_SIZE),
        grad_k.reshape(-1, width),
        grad_v.reshape(-1, width),
    )


def dot(a, b):
    return jnp.dot(a, b, preferred_element_type=F32)


def dot_t(a, b):
    return lax.dot_general(a, b, (((1,), (1,)), ((), ())), preferred_element_type=F32)


def t_dot(a, b):
    return lax.dot_general(a, b, (((0,), (0,)), ((), ())), preferred_element_type=F32)


def choose(flags):
    return flags.astype(BF)


def local(
    block_input,
    positions,
    first_gain,
    query_weight,
    query_bias,
    key_weight,
    value_weight,
    value_bias,
    output_weight,
    second_gain,
    gate_weight,
    up_weight,
    down_weight,
    cotangent,
):
    f = lax.axis_index("fsdp")
    c = lax.axis_index("ctx")
    stretch = f * 4 + c

    i896 = jnp.arange(D)
    spread = choose((i896 + i896 // 7)[:, None] == jnp.arange(DP)[None, :])

    own_a, own_o, own_g, own_u, own_d = pack(
        jnp.concatenate([query_weight, key_weight, value_weight], axis=1),
        output_weight,
        gate_weight,
        up_weight,
        down_weight,
        jnp.concatenate([query_bias, value_bias])[None],
        jnp.stack([first_gain, second_gain]),
    )
    all_a, all_o, all_d, all_g, all_u, cot_all = gather(
        (own_a, own_o, own_d, own_g, own_u), (0, 0, 0, 1, 1), cotangent
    )
    all_g = all_g.reshape(DP, UC)
    all_u = all_u.reshape(DP, UC)
    all_d = all_d.reshape(UC, D)
    rows_o = all_o.reshape(32, 32, D)
    gain_first = jnp.sum(rows_o[:, 7].astype(F32), axis=0)
    gain_second = jnp.sum(rows_o[:, 15].astype(F32), axis=0)
    all_a = all_a.reshape(DP, 1152)
    cot_all = cot_all.reshape(4 * TOK, D)
    weight_output = all_o.reshape(DP, D)
    pad_ones = (jnp.arange(DP) % 8 == 7).astype(F32)[None, :]

    residual_in = block_input.astype(F32)
    normed_one, scale_one = norm_forward(residual_in)
    normed_input = (normed_one * gain_first).astype(BF)
    input_pad = (dot(normed_input, spread) + pad_ones).astype(BF)
    qkv = dot(input_pad, all_a)
    cosine, sine = rotary_tables(positions, HEAD_SIZE)
    query_rot = rotate(qkv[:, :896], cosine, sine, HEADS, HEAD_SIZE).astype(BF)
    key_rot = rotate(qkv[:, 896:1024], cosine, sine, KV_HEADS, HEAD_SIZE).astype(BF)
    value_rows = qkv[:, 1024:].astype(BF)
    seen = window(jnp.concatenate([key_rot, value_rows], axis=1))
    seen = seen.reshape((REACH + 1) * TOK, 256)
    window_keys, window_values = seen[:, :128], seen[:, 128:]
    query_index = stretch * TOK + jnp.arange(TOK, dtype=jnp.int32)
    key_index = (stretch - REACH) * TOK + jnp.arange((REACH + 1) * TOK, dtype=jnp.int32)
    first_index = query_index - positions
    allowed = (key_index[None, :] >= first_index[:, None]) & (
        key_index[None, :] <= query_index[:, None]
    )
    attended, log_total = attend_forward(query_rot, window_keys, window_values, allowed)
    attended_pad = dot(attended, spread).astype(BF)
    residual_mid = residual_in + dot(attended_pad, weight_output)

    normed_two, scale_two = norm_forward(residual_mid)
    normed_mid = (normed_two * gain_second).astype(BF)
    mid_all = tokens_gather(normed_mid).reshape(4 * TOK, D)
    mid_pad = dot(mid_all, spread).astype(BF)
    gate_pre = dot(mid_pad, all_g)
    up_pre = dot(mid_pad, all_u)
    sigma = jax.nn.sigmoid(gate_pre)
    hidden = (gate_pre * sigma * up_pre).astype(BF)
    out_part = dot(hidden, all_d).astype(BF)
    grad_hidden = dot_t(cot_all, all_d)
    grad_gate_pre = (grad_hidden * up_pre * sigma * (1.0 + gate_pre * (1.0 - sigma))).astype(BF)
    grad_up_pre = (grad_hidden * gate_pre * sigma).astype(BF)
    mid_part = (dot_t(grad_gate_pre, all_g) + dot_t(grad_up_pre, all_u)).astype(BF)
    mid_part = dot_t(mid_part, spread).astype(BF)
    grad_normed_mid = tokens_sum(mid_part.reshape(4, TOK, D))
    grad_down = t_dot(hidden, cot_all).astype(BF)
    grad_gate = t_dot(mid_pad, grad_gate_pre).astype(BF)
    grad_up = t_dot(mid_pad, grad_up_pre).astype(BF)
    grad_norm_part, grad_gain_two = norm_backward(
        grad_normed_mid, normed_two, scale_two, gain_second
    )
    grad_mid = cotangent.astype(F32) + grad_norm_part

    grad_mid_low = grad_mid.astype(BF)
    grad_output_w = t_dot(attended_pad, grad_mid_low)
    grad_attended = dot_t(dot_t(grad_mid_low, weight_output).astype(BF), spread).astype(BF)
    grad_query_rot, grad_window_keys, grad_window_values = attend_backward(
        query_rot, window_keys, window_values, allowed, attended, log_total, grad_attended
    )
    grad_window = jnp.concatenate([grad_window_keys, grad_window_values], axis=1)
    grad_window = grad_window.reshape(REACH + 1, TOK, 256)
    grad_kv = back(grad_window[REACH], grad_window[:REACH].astype(BF))
    query_low = rotate(grad_query_rot, cosine, -sine, HEADS, HEAD_SIZE).astype(BF)
    key_low = rotate(grad_kv[:, :128], cosine, -sine, KV_HEADS, HEAD_SIZE).astype(BF)
    value_low = grad_kv[:, 128:].astype(BF)
    lows = jnp.concatenate([query_low, key_low, value_low], axis=1)
    grad_qkv_w = t_dot(input_pad, lows)
    grad_normed_input = dot_t(dot_t(lows, all_a).astype(BF), spread)
    grad_in_part, grad_gain_one = norm_backward(
        grad_normed_input, normed_one, scale_one, gain_first
    )
    grad_input = (grad_mid + grad_in_part).astype(BF)

    group = jnp.arange(DP)[:, None] // 8
    gains = jnp.where(
        i896[None, :] // 7 == group, grad_gain_one[None, :], jnp.roll(grad_gain_two, 448)[None, :]
    )
    grad_output_w = jnp.where(jnp.arange(DP)[:, None] % 8 == 7, gains, grad_output_w)
    sum_g, sum_u, sum_d, sum_a, sum_o, out_sum = scatter(
        (
            grad_gate.reshape(4, 4, 2, 32, UC),
            grad_up.reshape(4, 4, 2, 32, UC),
            grad_down.reshape(4, 4, 2, UP, D),
            grad_qkv_w.astype(BF).reshape(4, 4, 2, 32, 1152),
            grad_output_w.astype(BF).reshape(4, 4, 2, 32, D),
        ),
        (1, 1, 0, 0, 0),
        ("rows", "rows", "none", "sum", "sum"),
        out_part.reshape(4, TOK, D),
    )
    block_output = (residual_mid + out_sum).astype(BF)

    def columns(parts):
        parts = parts[:, :7].reshape(4, 7, 32, UP)[..., :UN]
        return jnp.transpose(parts, (1, 2, 0, 3)).reshape(7, FF)

    at = 7 * stretch
    return (
        block_output,
        grad_input,
        lax.dynamic_slice(sum_o[7], (at,), (7,)),
        sum_a[:7, :896],
        lax.dynamic_slice(sum_a[7], (at,), (7,)),
        sum_a[:7, 896:1024],
        sum_a[:7, 1024:1152],
        lax.dynamic_slice(sum_a[7], (1024 + stretch,), (1,)),
        sum_o[:7],
        lax.dynamic_slice(sum_o[7], (lax.rem(at + 448, 896),), (7,)),
        columns(sum_g),
        columns(sum_u),
        sum_d[:UN],
    )


def solution(mesh):
    tokens = P(("fsdp", "ctx"), None)
    entries = P(("fsdp", "ctx"))
    rows = P("fsdp", None)
    vector = P("fsdp")
    in_specs = (
        tokens,
        entries,
        vector,
        rows,
        vector,
        rows,
        rows,
        vector,
        rows,
        vector,
        rows,
        rows,
        rows,
        tokens,
    )
    out_specs = (
        tokens,
        tokens,
        entries,
        tokens,
        entries,
        tokens,
        tokens,
        entries,
        tokens,
        entries,
        tokens,
        tokens,
        tokens,
    )
    return jax.shard_map(local, mesh=mesh, in_specs=in_specs, out_specs=out_specs, check_vma=False)
```

```python
import functools
import math

import jax
import jax.numpy as jnp
from jax import lax
from jax.experimental import pallas as pl
from jax.experimental.pallas import tpu as pltpu
from jax.sharding import PartitionSpec as P

D = 896
HEADS = 14
KV_HEADS = 2
HEAD_SIZE = 64
FF = 4864
SEQ = 1024
TOK = 128
REACH = 8
DP = 1024
UN = 38
UP = 48
UC = 32 * UP
AW = 2048

EPSILON = 1e-06
ROTARY_BASE = 1000000.0
MESH = pl.DeviceIdType.MESH
BF = jnp.bfloat16
F32 = jnp.float32
ANY = pl.BlockSpec(memory_space=pl.ANY)
VMEM = pl.BlockSpec(memory_space=pltpu.VMEM)


def place():
    f = lax.axis_index("fsdp")
    return f // 8, (f // 2) % 4, f % 2, lax.axis_index("ctx")


def plus(i, d):
    return lax.rem(i + d, 4)


def device(z, x, k, c):
    return ((z * 4 + x) * 2 + k, c)


def greet(targets):
    barrier = pltpu.get_barrier_semaphore()
    for t in targets:
        pl.semaphore_signal(barrier, inc=1, device_id=t, device_id_type=MESH)
    pl.semaphore_wait(barrier, len(targets))


class Copies:
    def __init__(self, send, recv):
        self.send, self.recv, self.count, self.all = send, recv, 0, []

    def go(self, src, dst, target):
        n = self.count
        self.count += 1
        copy = pltpu.make_async_remote_copy(
            src_ref=src,
            dst_ref=dst,
            send_sem=self.send.at[n],
            recv_sem=self.recv.at[n],
            device_id=target,
            device_id_type=MESH,
        )
        copy.start()
        self.all.append(copy)
        return copy

    def finish(self):
        for copy in self.all:
            copy.wait_send()


class RingGather:
    def __init__(self, cp, part, own, p, up, down):
        self.cp, self.part, self.p, self.up, self.down = cp, part, p, up, down
        self.up0 = cp.go(own(0), part(p, 0), up)
        self.down1 = cp.go(own(1), part(p, 1), down)
        self.up1 = cp.go(own(1), part(p, 1), up)
        self.down0 = cp.go(own(0), part(p, 0), down)

    def forward(self):
        self.up0.wait_recv()
        ref = self.part(plus(self.p, 3), 0)
        self.far0 = self.cp.go(ref, ref, self.up)
        self.down1.wait_recv()
        ref = self.part(plus(self.p, 1), 1)
        self.far1 = self.cp.go(ref, ref, self.down)

    def near(self):
        self.up1.wait_recv()
        self.down0.wait_recv()

    def far(self):
        self.far0.wait_recv()
        self.far1.wait_recv()


class RingScatter:
    def __init__(self, cp, send, add, p, up, down, far, near):
        self.cp, self.send, self.add, self.p, self.up, self.down = cp, send, add, p, up, down
        self.far, self.near = far, near
        self.far0 = cp.go(send(plus(p, 2), 0), far[0], up)
        self.far1 = cp.go(send(plus(p, 2), 1), far[1], down)

    def plain(self):
        self.up1 = self.cp.go(self.send(plus(self.p, 1), 1), self.near[0](1), self.up)
        self.down0 = self.cp.go(self.send(plus(self.p, 3), 0), self.near[1](0), self.down)

    def forward(self):
        self.far0.wait_recv()
        ref = self.add(plus(self.p, 1), 0, self.far[0])
        self.up0 = self.cp.go(ref, self.near[0](0), self.up)
        self.far1.wait_recv()
        ref = self.add(plus(self.p, 3), 1, self.far[1])
        self.down1 = self.cp.go(ref, self.near[1](1), self.down)

    def finish(self):
        for copy in (self.up1, self.down0, self.up0, self.down1):
            copy.wait_recv()


def halves(rows):
    first = rows // 2 // 16 * 16
    return (pl.ds(0, first), pl.ds(first, rows - first))


PIECES = ((0, 0, 0, D, UP), (2, 0, 0, 768, 32), (1, 1, 0, UC, 32), (2, 1, 768, 768, 32))
FFN = ((UP, D), (32, UC), (32, UC))


def start_line(cp, spot, refs, own):
    z, x, k, c, zs, xs = spot
    rings = []
    for n, way, first, count, rows in PIECES:
        cut, cols = halves(rows), pl.ds(first, count)

        def part(p, h, n=n, way=way, cut=cut, cols=cols):
            at = (z, p, k, cut[h], cols) if way else (p, x, k, cut[h], cols)
            return refs[n].at[at]

        def mine(h, n=n, cut=cut, cols=cols):
            return own[n].at[cut[h], cols]

        rings.append(RingGather(cp, part, mine, x if way else z, *(xs if way else zs)))
    return rings


def start_plane(cp, spot, refs):
    z, x, k, c, zs, xs = spot
    rings = []
    for n, way, first, count, rows in PIECES:
        cols = pl.ds(first, count)

        def part(p, h, n=n, way=way, cols=cols):
            some = pl.ds(2 * h, 2)
            at = (p, some, k, slice(None), cols) if way else (some, p, k, slice(None), cols)
            return refs[n].at[at]

        p = z if way else x
        rings.append(RingGather(cp, part, functools.partial(part, p), p, *(zs if way else xs)))
    return rings


def gather_kernel(q, kw, v, o, down, gate, up, vec, t, *refs):
    ao, oo, do, go, uo, to = refs[:6]
    wq, wk, wv, wo, wd, wg, wu, units, own_a, own_o, own_d, own_g, own_u = refs[6:19]
    send, recv, load, loc = refs[19:]
    z, x, k, c = place()
    f = lax.axis_index("fsdp")
    zs = [device(plus(z, i), x, k, c) for i in (1, 3)]
    xs = [device(z, plus(x, i), k, c) for i in (1, 3)]
    ys = [device(z, x, k, plus(c, i)) for i in (1, 3)]
    sibling = device(z, x, 1 - k, c)
    loads = [
        pltpu.make_async_copy(src, dst, load.at[i])
        for i, (src, dst) in enumerate(
            ((q, wq), (kw, wk), (v, wv), (o, wo), (gate, wg), (up, wu), (down, wd))
        )
    ]
    for copy in loads:
        copy.start()
    token_copy = pltpu.make_async_copy(t, to.at[c], loc.at[5])
    token_copy.start()
    for n, device_id in enumerate(zs + xs + ys + [sibling]):
        pl.semaphore_signal(
            pltpu.get_barrier_semaphore(), inc=1, device_id=device_id, device_id_type=MESH
        )

    def iota(shape, axis):
        return lax.broadcasted_iota(jnp.int32, shape, axis)

    def where(flags):
        return flags.astype(F32).astype(BF)

    i = iota((32, 28), 1)
    spread = where(i + i // 7 == iota((32, 28), 0))
    row = iota((32, 1), 0)
    i, j = iota((88, 1152), 0), iota((88, 1152), 1)
    place_at = jnp.where(i < 28, 28 * f + i, jnp.where(i < 32, 1024 + 4 * f + i - 28, -1))
    extra = dot(vec[...], where(place_at == j))
    extra = jnp.where(row == 7, extra, 0.0)
    for copy in loads[:3]:
        copy.wait()
    own_a[:, :896] = (dot(spread, wq[...]) + extra[:, :896]).astype(BF)
    own_a[:, 896:1024] = dot(spread, wk[...]).astype(BF)
    own_a[:, 1024:] = (dot(spread, wv[...]) + extra[:, 1024:]).astype(BF)
    i, j = iota((88, D), 0), iota((88, D), 1)
    one = dot(vec[...], where((i >= 32) & (i < 60) & (28 * f + i - 32 == j)))
    two = dot(vec[...], where((i >= 60) & (28 * f + i - 60 == j)))
    loads[3].wait()
    own_o[...] = (
        dot(spread, wo[...]) + jnp.where(row == 7, one, 0.0) + jnp.where(row == 15, two, 0.0)
    ).astype(BF)

    pl.semaphore_wait(pltpu.get_barrier_semaphore(), 7)
    cp = Copies(send, recv)
    ways = (0, 1)
    own, outs = (own_a, own_o), (ao, oo)
    local = []

    def keep(src, out):
        copy = pltpu.make_async_copy(src, out.at[z, x, k], loc.at[len(local)])
        copy.start()
        local.append(copy)

    first, second, third = [], [], []
    cut = halves(32)
    for m in range(2):

        def part(p, h, m=m):
            return outs[m].at[z, p, k, cut[h]] if ways[m] else outs[m].at[p, x, k, cut[h]]

        def mine(h, m=m):
            return own[m].at[cut[h]]

        first.append(RingGather(cp, part, mine, x if ways[m] else z, *(xs if ways[m] else zs)))
        keep(own[m], outs[m])
    rows = halves(t.shape[0])
    tokens = RingGather(cp, lambda p, h: to.at[p, rows[h]], lambda h: t.at[rows[h]], c, *ys)

    loads[6].wait()
    i, j = iota((UP, 152), 0), iota((UP, 152), 1)
    own_d[...] = dot(where(jnp.where(i < UN, i + UN * c, -1) == j), wd[...]).astype(BF)
    j = iota((1, 16 * UP), 1)
    wanted = jnp.where(j % UP < UN, (j // UP) * 152 + j % UP, -1000) + UN * c
    for r in range(19):
        units[r * 128 : (r + 1) * 128] = where(iota((128, 16 * UP), 0) + r * 128 == wanted)
    for m in range(2):
        first[m].forward()
    for copy, src, out in ((loads[4], wg, own_g), (loads[5], wu, own_u)):
        copy.wait()
        wide = dot(spread, src[...]).astype(BF)
        for h in range(2):
            some = dot(wide[:, h * 2432 : (h + 1) * 2432], units[...])
            out[:, h * 768 : (h + 1) * 768] = some.astype(BF)
    for m in range(2):
        first[m].near()
        first[m].far()
        local[m].wait()

        def part(p, h, m=m):
            some = pl.ds(2 * h, 2)
            return outs[m].at[p, some, k] if ways[m] else outs[m].at[some, p, k]

        p = z if ways[m] else x
        second.append(
            RingGather(cp, part, functools.partial(part, p), p, *(zs if ways[m] else xs))
        )
    line = start_line(cp, (z, x, k, c, zs, xs), (do, go, uo), (own_d, own_g, own_u))
    for src, out in ((own_d, do), (own_g, go), (own_u, uo)):
        keep(src, out)

    def pass_on(m, i):
        p = plus(z if ways[m] else x, i)
        ref = outs[m].at[p, :, k] if ways[m] else outs[m].at[:, p, k]
        third.append(cp.go(ref, ref, sibling))

    for m in range(2):
        pass_on(m, 0)
    for m in range(2):
        second[m].forward()
    tokens.forward()
    for ring in line:
        ring.forward()
    for m in range(2):
        second[m].near()
        pass_on(m, 1)
        pass_on(m, 3)
    for m in range(2):
        second[m].far()
        pass_on(m, 2)
    for ring in line + [tokens]:
        ring.near()
        ring.far()
    token_copy.wait()
    for copy in local[2:]:
        copy.wait()
    for copy in third:
        copy.wait_recv()
    cp.finish()


def gather(q, kw, v, o, down, gate, up, vec, t):
    def out(rows, columns):
        return jax.ShapeDtypeStruct((4, 4, 2, rows, columns), BF)

    weights = (q, kw, v, o, down, gate, up)
    packed = ((32, 1152), (32, D)) + FFN
    count = 16 * 2 + 6 + 6 * len(PIECES)
    return pl.pallas_call(
        gather_kernel,
        out_shape=[out(*p) for p in packed] + [jax.ShapeDtypeStruct((4,) + t.shape, BF)],
        in_specs=[ANY] * 7 + [VMEM, ANY],
        out_specs=[ANY] * 6,
        scratch_shapes=[pltpu.VMEM(w.shape, BF) for w in weights]
        + [pltpu.VMEM((2432, 16 * UP), BF)]
        + [pltpu.VMEM(p, BF) for p in packed]
        + [
            pltpu.SemaphoreType.DMA((count,)),
            pltpu.SemaphoreType.DMA((count,)),
            pltpu.SemaphoreType.DMA((7,)),
            pltpu.SemaphoreType.DMA((6,)),
        ],
        compiler_params=pltpu.CompilerParams(
            collective_id=0, has_side_effects=True, vmem_limit_bytes=40 * 1024 * 1024
        ),
        name="gather_weights",
    )(*weights, vec, t)


def stretch_device(i):
    i = lax.rem(i + 128, 128)
    return (i // 4, lax.rem(i, 4))


def iota(shape, axis):
    return lax.broadcasted_iota(jnp.int32, shape, axis)


def head_move(head, scale):
    i, j = iota((128, 128), 0), iota((128, 128), 1)
    half, group = head % 2, head // (HEADS // KV_HEADS)
    hit = (i // 64 == half) & (j // 64 == group) & (i % 64 == j % 64)
    return (hit.astype(F32) * scale).astype(BF)


def spread_heads(src, out, scale):
    for pair in range(HEADS // 2):
        tile = src[:, pair * 128 : (pair + 1) * 128]
        for head in (2 * pair, 2 * pair + 1):
            out[head] = dot(tile, head_move(head, scale)).astype(BF)


def join_heads(src, out):
    for pair in range(HEADS // 2):
        total = 0.0
        for head in (2 * pair, 2 * pair + 1):
            total = total + dot_t(src[head], head_move(head, 1.0))
        out[:, pair * 128 : (pair + 1) * 128] = total.astype(BF)


def seen_mask(first):
    key = iota((TOK, (REACH + 1) * TOK), 1)
    query = REACH * TOK + iota((TOK, 1), 0)
    return (key >= first[...]) & (key <= query)


def window_kernel(q, kv, first, d_in, g_in, u_in, out, att, logs, do, go, uo, qs, os, send, recv):
    me = lax.axis_index("fsdp") * 4 + lax.axis_index("ctx")
    z, x, k, c = place()
    zs = [device(plus(z, i), x, k, c) for i in (1, 3)]
    xs = [device(z, plus(x, i), k, c) for i in (1, 3)]
    greet([stretch_device(me - o) for o in range(1, REACH + 1)] + zs + xs)
    cp = Copies(send, recv)
    copies = [
        cp.go(kv, out.at[REACH - o], stretch_device(me + o)) for o in range(REACH, 0, -1)
    ]
    plane = start_plane(cp, (z, x, k, c, zs, xs), (do, go, uo))
    out[REACH] = kv[...]
    spread_heads(q, qs, 1.0 / math.sqrt(HEAD_SIZE))
    logs[...] = jnp.zeros(logs.shape, F32)
    for copy in copies:
        copy.wait_recv()
    for ring in plane:
        ring.forward()

    def one(head, carry):
        keys = out[:, :, :128].reshape((REACH + 1) * TOK, 128)
        values = out[:, :, 128:].reshape((REACH + 1) * TOK, 128)
        scores = jnp.where(seen_mask(first), dot_t(qs[head], keys), -jnp.inf)
        top = jnp.max(scores, axis=1, keepdims=True)
        weights = jnp.exp(scores - top)
        total = jnp.sum(weights, axis=1, keepdims=True)
        os[head] = dot((weights * (1.0 / total)).astype(BF), values).astype(BF)
        logs[...] += jnp.where(iota((TOK, 128), 1) == head, top + jnp.log(total), 0.0)
        return carry

    lax.fori_loop(0, HEADS, one, 0)
    join_heads(os, att)
    for ring in plane:
        ring.near()
        ring.far()
    cp.finish()


def window(q, kv, first, weights):
    count = REACH + 6 * len(PIECES)
    return pl.pallas_call(
        window_kernel,
        out_shape=[
            jax.ShapeDtypeStruct((REACH + 1,) + kv.shape, BF),
            jax.ShapeDtypeStruct(q.shape, BF),
            jax.ShapeDtypeStruct((TOK, 128), F32),
        ]
        + [jax.ShapeDtypeStruct(w.shape, BF) for w in weights],
        in_specs=[VMEM] * 3 + [ANY] * 3,
        out_specs=[VMEM] * 3 + [ANY] * 3,
        input_output_aliases={3: 3, 4: 4, 5: 5},
        scratch_shapes=[
            pltpu.VMEM((HEADS, TOK, 128), BF),
            pltpu.VMEM((HEADS, TOK, 128), BF),
            pltpu.SemaphoreType.DMA((count,)),
            pltpu.SemaphoreType.DMA((count,)),
        ],
        compiler_params=pltpu.CompilerParams(
            collective_id=1, has_side_effects=True, vmem_limit_bytes=48 * 1024 * 1024
        ),
        name="attention_forward",
    )(q, kv, first, *weights)


def back_kernel(q, grad, att, logs, seen, first, turn, *refs):
    n = len(PIECES)

    def take(count):
        nonlocal refs
        head, refs = refs[:count], refs[count:]
        return head

    ins, (out,), sums = take(n), take(1), take(n)
    own, far, near = take(n), take(n), take(n)
    qs, gs, os, grad_keys, grad_values, parts, got, send, recv, loc = refs
    me = lax.axis_index("fsdp") * 4 + lax.axis_index("ctx")
    z, x, k, c = place()
    zs = [device(plus(z, i), x, k, c) for i in (1, 3)]
    xs = [device(z, plus(x, i), k, c) for i in (1, 3)]
    loads = []
    for m in range(n):
        loads.append(pltpu.make_async_copy(ins[m], own[m], loc.at[m]))
        loads[m].start()
    greet([stretch_device(me + o) for o in range(1, REACH + 1)] + zs + xs)
    cp = Copies(send, recv)
    rings = []
    for m in range(n):
        way = PIECES[m][1]
        loads[m].wait()
        rings.append(
            RingScatter(
                cp,
                functools.partial(half_of, own[m], way),
                functools.partial(add_half, own[m], way),
                z if way else x,
                *(zs if way else xs),
                (far[m].at[0], far[m].at[1]),
                (
                    lambda h, m=m: near[m].at[0, pl.ds(2 * h, 2)],
                    lambda h, m=m: near[m].at[1, pl.ds(2 * h, 2)],
                ),
            )
        )
        rings[m].plain()
    spread_heads(q, qs, 1.0 / math.sqrt(HEAD_SIZE))
    spread_heads(grad, gs, 1.0)
    spread_heads(att, os, 1.0)
    rows = (REACH + 1) * TOK
    grad_keys[...] = jnp.zeros((rows, 128), F32)
    grad_values[...] = jnp.zeros((rows, 128), F32)

    def turned(values):
        low = iota(values.shape, 1) % 64 < 32
        other = jnp.where(low, pltpu.roll(values, 96, 1), pltpu.roll(values, 32, 1))
        return values * turn[0] + other * turn[1]

    def one(head, carry):
        keys = seen[:, :, :128].reshape(rows, 128)
        values = seen[:, :, 128:].reshape(rows, 128)
        here = iota((TOK, 128), 1) == head
        log_total = jnp.sum(jnp.where(here, logs[...], 0.0), axis=1, keepdims=True)
        delta = jnp.sum(
            gs[head].astype(F32) * os[head].astype(F32), axis=1, keepdims=True
        )
        scores = jnp.where(seen_mask(first), dot_t(qs[head], keys), -jnp.inf)
        probability = jnp.exp(scores - log_total)
        grad_scores = (probability * (dot_t(gs[head], values) - delta)).astype(BF)
        grad_values[...] += t_dot(probability.astype(BF), gs[head])
        grad_keys[...] += t_dot(grad_scores, qs[head])
        grad_query = dot(grad_scores, keys) * (1.0 / math.sqrt(HEAD_SIZE))
        os[head] = turned(grad_query).astype(BF)
        return carry

    lax.fori_loop(0, HEADS // 2, one, 0)
    for m in range(n):
        rings[m].forward()
    lax.fori_loop(HEADS // 2, HEADS, one, 0)
    parts[:, :, :128] = grad_keys[: REACH * TOK].astype(BF).reshape(REACH, TOK, 128)
    parts[:, :, 128:] = grad_values[: REACH * TOK].astype(BF).reshape(REACH, TOK, 128)
    copies = [
        cp.go(parts.at[REACH - o], got.at[o - 1], stretch_device(me - o))
        for o in range(REACH, 0, -1)
    ]
    join_heads(os, out)
    for m in range(n):
        rings[m].finish()
        sum_line(own[m], near[m], sums[m], PIECES[m][1], z if PIECES[m][1] else x)
    for copy in copies:
        copy.wait_recv()
    total_keys, total_values = grad_keys[REACH * TOK :], grad_values[REACH * TOK :]
    for o in range(REACH):
        total_keys = total_keys + got[o, :, :128].astype(F32)
        total_values = total_values + got[o, :, 128:].astype(F32)
    out[:, 896:1024] = turned(total_keys).astype(BF)
    out[:, 1024:] = total_values.astype(BF)
    cp.finish()


def half_of(ref, way, p, h):
    some = pl.ds(2 * h, 2)
    return ref.at[p, some] if way else ref.at[some, p]


def add_half(ref, way, p, h, got):
    def one(j, carry):
        at = (p, 2 * h + j) if way else (2 * h + j, p)
        ref[at] = (ref[at].astype(F32) + got[j].astype(F32)).astype(BF)
        return carry

    lax.fori_loop(0, 2, one, 0)
    return half_of(ref, way, p, h)


def sum_line(own, near, out, way, p):
    def one(j, carry):
        at = (p, j) if way else (j, p)
        total = own[at].astype(F32) + near[0, j].astype(F32)
        out[j] = (total + near[1, j].astype(F32)).astype(BF)
        return carry

    lax.fori_loop(0, 4, one, 0)


def back(q, grad, att, logs, seen, first, turn, arrays):
    n = len(PIECES)
    shapes = [s.shape[2:] for s in arrays]
    count = REACH + 6 * n
    rows = (REACH + 1) * TOK
    return pl.pallas_call(
        back_kernel,
        out_shape=[jax.ShapeDtypeStruct((TOK, 1152), BF)]
        + [jax.ShapeDtypeStruct((4,) + s, BF) for s in shapes],
        in_specs=[VMEM] * 7 + [ANY] * n,
        out_specs=[VMEM] * (n + 1),
        scratch_shapes=[pltpu.VMEM((4, 4) + s, BF) for s in shapes]
        + [pltpu.VMEM((2, 2) + s, BF) for s in shapes]
        + [pltpu.VMEM((2, 4) + s, BF) for s in shapes]
        + [pltpu.VMEM((HEADS, TOK, 128), BF)] * 3
        + [pltpu.VMEM((rows, 128), F32)] * 2
        + [pltpu.VMEM((REACH, TOK, 256), BF)] * 2
        + [
            pltpu.SemaphoreType.DMA((count,)),
            pltpu.SemaphoreType.DMA((count,)),
            pltpu.SemaphoreType.DMA((n,)),
        ],
        compiler_params=pltpu.CompilerParams(
            collective_id=2, has_side_effects=True, vmem_limit_bytes=48 * 1024 * 1024
        ),
        name="attention_backward",
    )(q, grad, att, logs, seen, first, turn, *arrays)


def tokens_kernel(t, d_in, g_in, u_in, out, do, go, uo, send, recv):
    z, x, k, c = place()
    ys = [device(z, x, k, plus(c, i)) for i in (1, 3)]
    sibling = device(z, x, 1 - k, c)
    greet(ys + [sibling])
    cp = Copies(send, recv)
    rows = halves(t.shape[0])
    ring = RingGather(cp, lambda p, h: out.at[p, rows[h]], lambda h: t.at[rows[h]], c, *ys)
    copies = []
    for ref in (go, uo, do):
        copies.append(cp.go(ref.at[:, :, k], ref.at[:, :, k], sibling))
    out[c] = t[...]
    ring.forward()
    ring.near()
    ring.far()
    for copy in copies:
        copy.wait_recv()
    cp.finish()


def tokens_gather(t, weights):
    return pl.pallas_call(
        tokens_kernel,
        out_shape=[jax.ShapeDtypeStruct((4,) + t.shape, BF)]
        + [jax.ShapeDtypeStruct(w.shape, BF) for w in weights],
        in_specs=[VMEM] + [ANY] * 3,
        out_specs=[VMEM] + [ANY] * 3,
        input_output_aliases={1: 1, 2: 2, 3: 3},
        scratch_shapes=[pltpu.SemaphoreType.DMA((9,)), pltpu.SemaphoreType.DMA((9,))],
        compiler_params=pltpu.CompilerParams(collective_id=3, has_side_effects=True),
        name="gather_tokens",
    )(t, *weights)


def tokens_ring(cp, t, acc, far, near, c, ys):
    rows = halves(t.shape[1])

    def send(p, h):
        return t.at[p, rows[h]]

    def add(p, h, got):
        acc[h] = (t[p, rows[h]].astype(F32) + got[...].astype(F32)).astype(BF)
        return acc.at[h]

    return RingScatter(
        cp,
        send,
        add,
        c,
        *ys,
        (far.at[0], far.at[1]),
        (lambda h: near.at[0, rows[h]], lambda h: near.at[1, rows[h]]),
    )


def tokens_scratch(rows):
    half = (2, rows[0] // 2, rows[1])
    return [pltpu.VMEM(half, BF), pltpu.VMEM(half, BF), pltpu.VMEM((2,) + rows, BF)]


def tokens_sum_kernel(t, hidden, cot, mid, gg, gu, wd, out, part, *refs):
    n = len(PIECES)

    def take(count):
        nonlocal refs
        head, refs = refs[:count], refs[count:]
        return head

    sums, full, got = take(n), take(3), take(n)
    acc, far, near, send, recv = refs
    z, x, k, c = place()
    ys = [device(z, x, k, plus(c, i)) for i in (1, 3)]
    sibling = device(z, x, 1 - k, c)
    greet(ys + [sibling])
    cp = Copies(send, recv)
    ring = tokens_ring(cp, t, acc, far, near, c, ys)
    ring.plain()
    firsts = {}

    def product(m, lhs, rhs):
        rows = lhs.shape[1] // 4
        shape = (4, 2) + full[m].shape[3:]

        def one(i, carry):
            columns = pl.ds(pl.multiple_of(i * rows, 128), rows)
            full[m][i] = t_dot(lhs[:, columns], rhs[...]).astype(BF).reshape(shape)
            return carry

        lax.fori_loop(0, 4, one, 0)
        for j in range(n):
            a, _, first, count, _ = PIECES[j]
            if a == m:
                src = full[m].at[:, :, 1 - k, :, pl.ds(first, count)]
                firsts[j] = cp.go(src, got[j], sibling)

    product(0, hidden, cot)
    ring.forward()
    product(1, mid, gg)
    product(2, mid, gu)
    ring.finish()
    out[...] = t[c].astype(F32) + near[0].astype(F32) + near[1].astype(F32)

    def down(i, carry):
        rows = pl.ds(pl.multiple_of(i * TOK, TOK), TOK)
        part[i] = dot(hidden[rows], wd[...]).astype(BF)
        return carry

    lax.fori_loop(0, 4, down, 0)
    for j in (0, 2, 1, 3):
        a, _, first, count, _ = PIECES[j]
        firsts[j].wait_recv()

        def add(i, carry, j=j, a=a, first=first, count=count):
            at = (i // 4, i % 4)
            mine = full[a][at + (k, slice(None), slice(first, first + count))]
            sums[j][at] = (mine.astype(F32) + got[j][at].astype(F32)).astype(BF)
            return carry

        lax.fori_loop(0, 16, add, 0)
    cp.finish()


def tokens_sum(t, hidden, cot, mid, gg, gu, wd):
    rows = t.shape[1:]
    n = len(PIECES)
    shapes = [(p[4], p[3]) for p in PIECES]
    return pl.pallas_call(
        tokens_sum_kernel,
        out_shape=[jax.ShapeDtypeStruct(rows, F32), jax.ShapeDtypeStruct(t.shape, BF)]
        + [jax.ShapeDtypeStruct((4, 4) + s, BF) for s in shapes],
        in_specs=[VMEM] * 7,
        out_specs=[VMEM] * (n + 2),
        scratch_shapes=[pltpu.VMEM((4, 4, 2) + s, BF) for s in FFN]
        + [pltpu.VMEM((4, 4) + s, BF) for s in shapes]
        + tokens_scratch(rows)
        + [pltpu.SemaphoreType.DMA((6 + n,)), pltpu.SemaphoreType.DMA((6 + n,))],
        compiler_params=pltpu.CompilerParams(
            collective_id=4, has_side_effects=True, vmem_limit_bytes=48 * 1024 * 1024
        ),
        name="scatter_tokens",
    )(t, hidden, cot, mid, gg, gu, wd)


def scatter_kernel(a, o, p0, p1, p2, p3, t, *refs):
    n = len(PIECES)

    def take(count):
        nonlocal refs
        head, refs = refs[:count], refs[count:]
        return head

    outs, (t_out,) = take(2 + n), take(1)
    own, got1, far2, near2, sum2 = (take(2) for _ in range(5))
    line = sum2 + take(n)
    far3, near3, fins, gots = take(2 + n), take(2 + n), take(2 + n), take(2)
    acc, far, near, send, recv, loc = refs
    ins = (a, o)
    ways = (0, 1) + tuple(p[1] for p in PIECES)
    z, x, k, c = place()
    zs = [device(plus(z, i), x, k, c) for i in (1, 3)]
    xs = [device(z, plus(x, i), k, c) for i in (1, 3)]
    ys = [device(z, x, k, plus(c, i)) for i in (1, 2, 3)]
    sibling = device(z, x, 1 - k, c)

    def spot(m, i):
        return plus(z if ways[m] else x, i)

    def piece(ref, m, p, *rest):
        return ref.at[(p, slice(None)) + rest] if ways[m] else ref.at[(slice(None), p) + rest]

    local = {}
    for i in (2, 1, 3, 0):
        for m in range(2):
            p = spot(m, i)
            copy = pltpu.make_async_copy(
                piece(ins[m], m, p, k), piece(own[m], m, p), loc.at[m * 4 + i]
            )
            copy.start()
            local[m, i] = copy
    loads = []
    for m, src in enumerate((p0, p1, p2, p3)):
        loads.append(pltpu.make_async_copy(src, line[2 + m], loc.at[8 + m]))
        loads[m].start()
    greet(zs + xs + ys + [sibling])
    cp = Copies(send, recv)
    first, second, third, closing = {}, [], {}, {}
    for i in (2, 1, 3, 0):
        for m in range(2):
            p = spot(m, i)
            first[m, i] = cp.go(piece(ins[m], m, p, 1 - k), piece(got1[m], m, p), sibling)

    def rows_of(some):
        return pl.ds(0, some.size)

    def start_third(m):
        ref, rows = line[m], halves(line[m].shape[1])

        def send(p, h):
            return ref.at[p, rows[h]]

        def add(p, h, got):
            ref[p, rows[h]] = (ref[p, rows[h]].astype(F32) + got[...].astype(F32)).astype(BF)
            return send(p, h)

        third[m] = RingScatter(
            cp,
            send,
            add,
            x if ways[m] else z,
            *(xs if ways[m] else zs),
            (far3[m].at[0, rows_of(rows[0])], far3[m].at[1, rows_of(rows[1])]),
            (lambda h: near3[m].at[0, rows[h]], lambda h: near3[m].at[1, rows[h]]),
        )
        third[m].plain()

    def close(m):
        third[m].finish()
        total = line[m][x if ways[m] else z].astype(F32)
        total = total + near3[m][0].astype(F32) + near3[m][1].astype(F32)
        if m == 2:
            outs[m][...] = total
            return
        fins[m][...] = total.reshape(fins[m].shape)
        for i in (1, 2, 3):
            target = gots[m].at[i - 1] if m < 2 else outs[m].at[c]
            closing[m, i] = cp.go(fins[m].at[plus(c, i)], target, ys[i - 1])
        if m > 2:
            outs[m][c] = fins[m][c]

    def join(m, i):
        p = spot(m, i)
        local[m, i].wait()
        first[m, i].wait_recv()

        def add(j, carry):
            at = (p, j) if ways[m] else (j, p)
            own[m][at] = (own[m][at].astype(F32) + got1[m][at].astype(F32)).astype(BF)
            return carry

        lax.fori_loop(0, 4, add, 0)

    for m in range(2):
        join(m, 2)
        second.append(
            RingScatter(
                cp,
                functools.partial(half_of, own[m], ways[m]),
                functools.partial(add_half, own[m], ways[m]),
                spot(m, 0),
                *(zs if ways[m] else xs),
                (far2[m].at[0], far2[m].at[1]),
                (
                    lambda h, m=m: near2[m].at[0, pl.ds(2 * h, 2)],
                    lambda h, m=m: near2[m].at[1, pl.ds(2 * h, 2)],
                ),
            )
        )
    for m in range(2):
        join(m, 1)
        join(m, 3)
        second[m].plain()
    for m in range(n):
        loads[m].wait()
        start_third(2 + m)
    tokens = tokens_ring(cp, t, acc, far, near, c, (ys[0], ys[2]))
    tokens.plain()
    for m in range(2):
        second[m].forward()
    for m in range(2):
        join(m, 0)
    for m in range(n):
        third[2 + m].forward()
    tokens.forward()
    for m in range(2):
        second[m].finish()
        sum_line(own[m], near2[m], line[m], ways[m], spot(m, 0))
        start_third(m)
    for m in range(n):
        close(2 + m)
    for m in range(2):
        third[m].forward()
    tokens.finish()
    t_out[...] = t[c].astype(F32) + near[0].astype(F32) + near[1].astype(F32)
    for m in range(2):
        close(m)
    for copy in closing.values():
        copy.wait_recv()
    for m in range(2):
        total = fins[m][c]
        for i in range(3):
            total = total + gots[m][i]
        outs[m][...] = total
    cp.finish()


def scatter(a, o, sums, t):
    n = len(PIECES)
    pair = [a.shape[3:], o.shape[3:]]
    shapes = pair + [s.shape[1:] for s in sums]
    quarter = [(s[0] // 4, s[1]) for s in shapes]
    outs = quarter[:2] + [shapes[2]] + [(4,) + q for q in quarter[3:]]
    scratch = []
    for lead in ((4, 4), (4, 4), (2, 2), (2, 4)):
        scratch += [pltpu.VMEM(lead + s, BF) for s in pair]
    scratch += [pltpu.VMEM((4,) + s, BF) for s in shapes]
    scratch += [pltpu.VMEM((2, halves(s[0])[1].size, s[1]), BF) for s in shapes]
    scratch += [pltpu.VMEM((2,) + s, BF) for s in shapes]
    scratch += [pltpu.VMEM((4,) + q if m != 2 else (8, 128), F32) for m, q in enumerate(quarter)]
    scratch += [pltpu.VMEM((3,) + q, F32) for q in quarter[:2]]
    scratch += tokens_scratch(t.shape[1:])
    count = 2 * 19 + 6 * n + 3 * (n - 1) + 6
    scratch += [
        pltpu.SemaphoreType.DMA((count,)),
        pltpu.SemaphoreType.DMA((count,)),
        pltpu.SemaphoreType.DMA((8 + n,)),
    ]
    return pl.pallas_call(
        scatter_kernel,
        out_shape=[jax.ShapeDtypeStruct(s, F32) for s in outs]
        + [jax.ShapeDtypeStruct(t.shape[1:], F32)],
        in_specs=[ANY] * (2 + n) + [VMEM],
        out_specs=[VMEM] * (3 + n),
        scratch_shapes=scratch,
        compiler_params=pltpu.CompilerParams(
            collective_id=5, has_side_effects=True, vmem_limit_bytes=40 * 1024 * 1024
        ),
        name="scatter_grads",
    )(a, o, *sums, t)


def rotary_tables(positions, head_size):
    half = head_size // 2
    frequency = ROTARY_BASE ** (-(jnp.arange(half, dtype=F32) * 2.0 / head_size))
    angles = positions.astype(F32)[:, None] * frequency[None, :]
    return (jnp.cos(angles), jnp.sin(angles))


def rotate(values, cosine, sine, heads, head_size):
    count = values.shape[0]
    shaped = values.reshape(count, heads, head_size)
    half = head_size // 2
    first = shaped[..., :half]
    second = shaped[..., half:]
    cos_rows = cosine[:, None, :]
    sin_rows = sine[:, None, :]
    turned = jnp.concatenate(
        [first * cos_rows - second * sin_rows, second * cos_rows + first * sin_rows], axis=-1
    )
    return turned.reshape(count, heads * head_size)


def norm_forward(values):
    factor = lax.rsqrt(jnp.mean(values * values, axis=-1, keepdims=True) + EPSILON)
    return (values * factor, factor)


def norm_backward(grad_out, normed, factor, gain):
    grad_normed = grad_out * gain
    inner = jnp.mean(grad_normed * normed, axis=-1, keepdims=True)
    return (factor * (grad_normed - normed * inner), jnp.sum(grad_out * normed, axis=0))


def dot(a, b):
    return jnp.dot(a, b, preferred_element_type=F32)


def dot_t(a, b):
    return lax.dot_general(a, b, (((1,), (1,)), ((), ())), preferred_element_type=F32)


def t_dot(a, b):
    return lax.dot_general(a, b, (((0,), (0,)), ((), ())), preferred_element_type=F32)


def choose(flags):
    return flags.astype(BF)


def local(
    block_input,
    positions,
    first_gain,
    query_weight,
    query_bias,
    key_weight,
    value_weight,
    value_bias,
    output_weight,
    second_gain,
    gate_weight,
    up_weight,
    down_weight,
    cotangent,
):
    f = lax.axis_index("fsdp")
    c = lax.axis_index("ctx")
    stretch = f * 4 + c

    i896 = jnp.arange(D)
    spread = choose((i896 + i896 // 7)[:, None] == jnp.arange(DP)[None, :])

    all_a, all_o, all_d, all_g, all_u, cot_all = gather(
        query_weight,
        key_weight,
        value_weight,
        output_weight,
        down_weight,
        gate_weight,
        up_weight,
        jnp.concatenate([query_bias, value_bias, first_gain, second_gain])[None],
        cotangent,
    )
    rows_o = all_o.reshape(32, 32, D)
    gain_first = jnp.sum(rows_o[:, 7].astype(F32), axis=0)
    gain_second = jnp.sum(rows_o[:, 15].astype(F32), axis=0)
    all_a = all_a.reshape(DP, 1152)
    cot_all = cot_all.reshape(4 * TOK, D)
    weight_output = all_o.reshape(DP, D)
    pad_ones = (jnp.arange(DP) % 8 == 7).astype(F32)[None, :]

    residual_in = block_input.astype(F32)
    normed_one, scale_one = norm_forward(residual_in)
    normed_input = (normed_one * gain_first).astype(BF)
    input_pad = (dot(normed_input, spread) + pad_ones).astype(BF)
    qkv = dot(input_pad, all_a)
    cosine, sine = rotary_tables(positions, HEAD_SIZE)
    query_rot = rotate(qkv[:, :896], cosine, sine, HEADS, HEAD_SIZE).astype(BF)
    key_rot = rotate(qkv[:, 896:1024], cosine, sine, KV_HEADS, HEAD_SIZE).astype(BF)
    value_rows = qkv[:, 1024:].astype(BF)
    first = (REACH * TOK + jnp.arange(TOK, dtype=jnp.int32) - positions)[:, None]
    seen, attended, logs, all_d, all_g, all_u = window(
        query_rot, jnp.concatenate([key_rot, value_rows], axis=1), first, (all_d, all_g, all_u)
    )
    attended_pad = dot(attended, spread).astype(BF)
    residual_mid = residual_in + dot(attended_pad, weight_output)

    normed_two, scale_two = norm_forward(residual_mid)
    normed_mid = (normed_two * gain_second).astype(BF)
    mid_all, all_d, all_g, all_u = tokens_gather(normed_mid, (all_d, all_g, all_u))
    mid_all = mid_all.reshape(4 * TOK, D)
    all_g = all_g.reshape(DP, UC)
    all_u = all_u.reshape(DP, UC)
    all_d = all_d.reshape(UC, D)
    mid_pad = dot(mid_all, spread).astype(BF)
    gate_pre = dot(mid_pad, all_g)
    up_pre = dot(mid_pad, all_u)
    sigma = jax.nn.sigmoid(gate_pre)
    hidden = (gate_pre * sigma * up_pre).astype(BF)
    grad_hidden = dot_t(cot_all, all_d)
    grad_gate_pre = (grad_hidden * up_pre * sigma * (1.0 + gate_pre * (1.0 - sigma))).astype(BF)
    grad_up_pre = (grad_hidden * gate_pre * sigma).astype(BF)
    mid_part = (dot_t(grad_gate_pre, all_g) + dot_t(grad_up_pre, all_u)).astype(BF)
    mid_part = dot_t(mid_part, spread).astype(BF)
    grad_normed_mid, out_part, *sums = tokens_sum(
        mid_part.reshape(4, TOK, D), hidden, cot_all, mid_pad, grad_gate_pre, grad_up_pre, all_d
    )
    grad_norm_part, grad_gain_two = norm_backward(
        grad_normed_mid, normed_two, scale_two, gain_second
    )
    grad_mid = cotangent.astype(F32) + grad_norm_part

    grad_mid_low = grad_mid.astype(BF)
    grad_output_w = t_dot(attended_pad, grad_mid_low)
    grad_attended = dot_t(dot_t(grad_mid_low, weight_output).astype(BF), spread).astype(BF)
    turn = jnp.stack(
        [jnp.tile(cosine, (1, 4)), jnp.tile(jnp.concatenate([sine, -sine], axis=1), (1, 2))]
    )
    lows, *sums = back(query_rot, grad_attended, attended, logs, seen, first, turn, sums)
    grad_qkv_w = t_dot(input_pad, lows)
    grad_normed_input = dot_t(dot_t(lows, all_a).astype(BF), spread)
    grad_in_part, grad_gain_one = norm_backward(
        grad_normed_input, normed_one, scale_one, gain_first
    )
    grad_input = (grad_mid + grad_in_part).astype(BF)

    group = jnp.arange(DP)[:, None] // 8
    gains = jnp.where(
        i896[None, :] // 7 == group, grad_gain_one[None, :], jnp.roll(grad_gain_two, 448)[None, :]
    )
    grad_output_w = jnp.where(jnp.arange(DP)[:, None] % 8 == 7, gains, grad_output_w)
    sum_a, sum_o, sum_d, sum_u0, sum_g, sum_u1, out_sum = scatter(
        grad_qkv_w.astype(BF).reshape(4, 4, 2, 32, 1152),
        grad_output_w.astype(BF).reshape(4, 4, 2, 32, D),
        sums,
        out_part,
    )
    sum_u = jnp.concatenate([sum_u0, sum_u1], axis=2)
    block_output = (residual_mid + out_sum).astype(BF)

    def columns(parts):
        parts = parts[:, :7].reshape(4, 7, 32, UP)[..., :UN]
        return jnp.transpose(parts, (1, 2, 0, 3)).reshape(7, FF)

    at = 7 * stretch
    return (
        block_output,
        grad_input,
        lax.dynamic_slice(sum_o[7], (at,), (7,)),
        sum_a[:7, :896],
        lax.dynamic_slice(sum_a[7], (at,), (7,)),
        sum_a[:7, 896:1024],
        sum_a[:7, 1024:1152],
        lax.dynamic_slice(sum_a[7], (1024 + stretch,), (1,)),
        sum_o[:7],
        lax.dynamic_slice(sum_o[7], (lax.rem(at + 448, 896),), (7,)),
        columns(sum_g),
        columns(sum_u),
        sum_d[:UN],
    )


def solution(mesh):
    tokens = P(("fsdp", "ctx"), None)
    entries = P(("fsdp", "ctx"))
    rows = P("fsdp", None)
    vector = P("fsdp")
    in_specs = (
        tokens,
        entries,
        vector,
        rows,
        vector,
        rows,
        rows,
        vector,
        rows,
        vector,
        rows,
        rows,
        rows,
        tokens,
    )
    out_specs = (
        tokens,
        tokens,
        entries,
        tokens,
        entries,
        tokens,
        tokens,
        entries,
        tokens,
        entries,
        tokens,
        tokens,
        tokens,
    )
    return jax.shard_map(local, mesh=mesh, in_specs=in_specs, out_specs=out_specs, check_vma=False)
```

```python
import functools
import math

import jax
import jax.numpy as jnp
from jax import lax
from jax.experimental import pallas as pl
from jax.experimental.pallas import tpu as pltpu
from jax.sharding import PartitionSpec as P

D = 896
HEADS = 14
KV_HEADS = 2
HEAD_SIZE = 64
FF = 4864
SEQ = 1024
TOK = 128
REACH = 8
DP = 1024
UN = 38
UP = 48
UC = 32 * UP
AW = 2048

EPSILON = 1e-06
ROTARY_BASE = 1000000.0
MESH = pl.DeviceIdType.MESH
BF = jnp.bfloat16
F32 = jnp.float32
ANY = pl.BlockSpec(memory_space=pl.ANY)
VMEM = pl.BlockSpec(memory_space=pltpu.VMEM)
HBM = pl.BlockSpec(memory_space=pltpu.HBM)
VMEM_FORWARD = 58 * 1024 * 1024


def place():
    f = lax.axis_index("fsdp")
    return f // 8, (f // 2) % 4, f % 2, lax.axis_index("ctx")


def plus(i, d):
    return lax.rem(i + d, 4)


def device(z, x, k, c):
    return ((z * 4 + x) * 2 + k, c)


def greet(targets):
    barrier = pltpu.get_barrier_semaphore()
    for t in targets:
        pl.semaphore_signal(barrier, inc=1, device_id=t, device_id_type=MESH)
    pl.semaphore_wait(barrier, len(targets))


class Copies:
    def __init__(self, send, recv):
        self.send, self.recv, self.count, self.all = send, recv, 0, []

    def go(self, src, dst, target):
        n = self.count
        self.count += 1
        copy = pltpu.make_async_remote_copy(
            src_ref=src,
            dst_ref=dst,
            send_sem=self.send.at[n],
            recv_sem=self.recv.at[n],
            device_id=target,
            device_id_type=MESH,
        )
        copy.start()
        self.all.append(copy)
        return copy

    def finish(self):
        for copy in self.all:
            copy.wait_send()


class RingGather:
    def __init__(self, cp, part, own, p, up, down):
        self.cp, self.part, self.p, self.up, self.down = cp, part, p, up, down
        self.up0 = cp.go(own(0), part(p, 0), up)
        self.down1 = cp.go(own(1), part(p, 1), down)
        self.up1 = cp.go(own(1), part(p, 1), up)
        self.down0 = cp.go(own(0), part(p, 0), down)

    def forward(self):
        self.up0.wait_recv()
        ref = self.part(plus(self.p, 3), 0)
        self.far0 = self.cp.go(ref, ref, self.up)
        self.down1.wait_recv()
        ref = self.part(plus(self.p, 1), 1)
        self.far1 = self.cp.go(ref, ref, self.down)

    def near(self):
        self.up1.wait_recv()
        self.down0.wait_recv()

    def far(self):
        self.far0.wait_recv()
        self.far1.wait_recv()


class RingScatter:
    def __init__(self, cp, send, add, p, up, down, far, near):
        self.cp, self.send, self.add, self.p, self.up, self.down = cp, send, add, p, up, down
        self.far, self.near = far, near
        self.far0 = cp.go(send(plus(p, 2), 0), far[0], up)
        self.far1 = cp.go(send(plus(p, 2), 1), far[1], down)

    def plain(self):
        self.up1 = self.cp.go(self.send(plus(self.p, 1), 1), self.near[0](1), self.up)
        self.down0 = self.cp.go(self.send(plus(self.p, 3), 0), self.near[1](0), self.down)

    def forward(self):
        self.far0.wait_recv()
        ref = self.add(plus(self.p, 1), 0, self.far[0])
        self.up0 = self.cp.go(ref, self.near[0](0), self.up)
        self.far1.wait_recv()
        ref = self.add(plus(self.p, 3), 1, self.far[1])
        self.down1 = self.cp.go(ref, self.near[1](1), self.down)

    def finish(self):
        for copy in (self.up1, self.down0, self.up0, self.down1):
            copy.wait_recv()


def halves(rows):
    first = rows // 2 // 16 * 16
    return (pl.ds(0, first), pl.ds(first, rows - first))


PIECES = ((0, 0, 0, D, UP), (2, 0, 0, 768, 32), (1, 1, 0, UC, 32), (2, 1, 768, 768, 32))
FFN = ((UP, D), (32, UC), (32, UC))


def start_line(cp, spot, refs, own):
    z, x, k, c, zs, xs = spot
    rings = []
    for n, way, first, count, rows in PIECES:
        cut, cols = halves(rows), pl.ds(first, count)

        def part(p, h, n=n, way=way, cut=cut, cols=cols):
            at = (z, p, k, cut[h], cols) if way else (p, x, k, cut[h], cols)
            return refs[n].at[at]

        def mine(h, n=n, cut=cut, cols=cols):
            return own[n].at[cut[h], cols]

        rings.append(RingGather(cp, part, mine, x if way else z, *(xs if way else zs)))
    return rings


def start_plane(cp, spot, refs):
    z, x, k, c, zs, xs = spot
    rings = []
    for n, way, first, count, rows in PIECES:
        cols = pl.ds(first, count)

        def part(p, h, n=n, way=way, cols=cols):
            some = pl.ds(2 * h, 2)
            at = (p, some, k, slice(None), cols) if way else (some, p, k, slice(None), cols)
            return refs[n].at[at]

        p = z if way else x
        rings.append(RingGather(cp, part, functools.partial(part, p), p, *(zs if way else xs)))
    return rings


def stretch_device(i):
    i = lax.rem(i + 128, 128)
    return (i // 4, lax.rem(i, 4))


def iota(shape, axis):
    return lax.broadcasted_iota(jnp.int32, shape, axis)


def head_move(head, scale):
    i, j = iota((128, 128), 0), iota((128, 128), 1)
    half, group = head % 2, head // (HEADS // KV_HEADS)
    hit = (i // 64 == half) & (j // 64 == group) & (i % 64 == j % 64)
    return (hit.astype(F32) * scale).astype(BF)


def spread_heads(src, out, scale):
    for pair in range(HEADS // 2):
        tile = src[:, pair * 128 : (pair + 1) * 128]
        for head in (2 * pair, 2 * pair + 1):
            out[head] = dot(tile, head_move(head, scale)).astype(BF)


def join_heads(src, out):
    for pair in range(HEADS // 2):
        total = 0.0
        for head in (2 * pair, 2 * pair + 1):
            total = total + dot_t(src[head], head_move(head, 1.0))
        out[:, pair * 128 : (pair + 1) * 128] = total.astype(BF)


def seen_mask(first_key):
    key = iota((TOK, (REACH + 1) * TOK), 1)
    query = REACH * TOK + iota((TOK, 1), 0)
    return (key >= first_key) & (key <= query)


def where(flags):
    return flags.astype(F32).astype(BF)


def spread_matrix():
    i, j = iota((D, DP), 0), iota((D, DP), 1)
    return where(i + i // 7 == j)


def rotary(pos, freq):
    angles = pos[...].astype(F32) * freq[...]
    sign = jnp.where(iota((TOK, 128), 1) % 64 < 32, 1.0, -1.0)
    return jnp.cos(angles), jnp.sin(angles) * sign


def turned(values, cosine, sine):
    low = iota(values.shape, 1) % 64 < 32
    other = jnp.where(low, pltpu.roll(values, 96, 1), pltpu.roll(values, 32, 1))
    return values * cosine + other * sine


def forward_kernel(q, kw, v, o, down, gate, up, vec, t, block, pos, freq, *refs):
    ao, oo, do, go, uo, to, mo, seen, qo, att, logs, mid, gains, turn = refs[:14]
    wq, wk, wv, wo, wd, wg, wu, units, own_a, own_o, own_d, own_g, own_u = refs[14:27]
    spread, kv, low, qs, os, send, recv, load, loc = refs[27:]
    z, x, k, c = place()
    f = lax.axis_index("fsdp")
    me = f * 4 + c
    zs = [device(plus(z, i), x, k, c) for i in (1, 3)]
    xs = [device(z, plus(x, i), k, c) for i in (1, 3)]
    ys = [device(z, x, k, plus(c, i)) for i in (1, 3)]
    sibling = device(z, x, 1 - k, c)
    barrier = pltpu.get_barrier_semaphore()
    window = [stretch_device(me - o) for o in range(1, REACH + 1)]
    for device_id in zs + xs + ys + [sibling] + window:
        pl.semaphore_signal(barrier, inc=1, device_id=device_id, device_id_type=MESH)
    loads = [
        pltpu.make_async_copy(src, dst, load.at[i])
        for i, (src, dst) in enumerate(
            ((q, wq), (kw, wk), (v, wv), (o, wo), (gate, wg), (up, wu), (down, wd))
        )
    ]
    for copy in loads:
        copy.start()
    token_copy = pltpu.make_async_copy(t, to.at[c], loc.at[5])
    token_copy.start()

    i = iota((32, 28), 1)
    rows28 = where(i + i // 7 == iota((32, 28), 0))
    row = iota((32, 1), 0)
    i, j = iota((88, 1152), 0), iota((88, 1152), 1)
    place_at = jnp.where(i < 28, 28 * f + i, jnp.where(i < 32, 1024 + 4 * f + i - 28, -1))
    extra = jnp.where(row == 7, dot(vec[...], where(place_at == j)), 0.0)
    for copy in loads[:3]:
        copy.wait()
    own_a[:, :896] = (dot(rows28, wq[...]) + extra[:, :896]).astype(BF)
    own_a[:, 896:1024] = dot(rows28, wk[...]).astype(BF)
    own_a[:, 1024:] = (dot(rows28, wv[...]) + extra[:, 1024:]).astype(BF)
    i, j = iota((88, D), 0), iota((88, D), 1)
    one = dot(vec[...], where((i >= 32) & (i < 60) & (28 * f + i - 32 == j)))
    two = dot(vec[...], where((i >= 60) & (28 * f + i - 60 == j)))
    loads[3].wait()
    own_o[...] = (
        dot(rows28, wo[...]) + jnp.where(row == 7, one, 0.0) + jnp.where(row == 15, two, 0.0)
    ).astype(BF)

    pl.semaphore_wait(barrier, 7 + REACH)
    cp = Copies(send, recv)
    ways = (0, 1)
    own, outs = (own_a, own_o), (ao, oo)
    local = []

    def keep(src, out):
        copy = pltpu.make_async_copy(src, out.at[z, x, k], loc.at[len(local)])
        copy.start()
        local.append(copy)

    first, second, third = [], [], []
    cut = halves(32)
    for m in range(2):

        def part(p, h, m=m):
            return outs[m].at[z, p, k, cut[h]] if ways[m] else outs[m].at[p, x, k, cut[h]]

        def mine(h, m=m):
            return own[m].at[cut[h]]

        first.append(RingGather(cp, part, mine, x if ways[m] else z, *(xs if ways[m] else zs)))
        keep(own[m], outs[m])
    rows = halves(TOK)
    tokens = RingGather(cp, lambda p, h: to.at[p, rows[h]], lambda h: t.at[rows[h]], c, *ys)

    loads[6].wait()
    i, j = iota((UP, 152), 0), iota((UP, 152), 1)
    own_d[...] = dot(where(jnp.where(i < UN, i + UN * c, -1) == j), wd[...]).astype(BF)
    j = iota((1, 16 * UP), 1)
    wanted = jnp.where(j % UP < UN, (j // UP) * 152 + j % UP, -1000) + UN * c
    for m in range(2):
        first[m].forward()
    for r in range(19):
        units[r * 128 : (r + 1) * 128] = where(iota((128, 16 * UP), 0) + r * 128 == wanted)
    for m in range(2):
        first[m].near()
        first[m].far()
        local[m].wait()

        def part(p, h, m=m):
            some = pl.ds(2 * h, 2)
            return outs[m].at[p, some, k] if ways[m] else outs[m].at[some, p, k]

        p = z if ways[m] else x
        second.append(
            RingGather(cp, part, functools.partial(part, p), p, *(zs if ways[m] else xs))
        )

    def pass_on(m, i):
        p = plus(z if ways[m] else x, i)
        ref = outs[m].at[p, :, k] if ways[m] else outs[m].at[:, p, k]
        third.append(cp.go(ref, ref, sibling))

    for m in range(2):
        pass_on(m, 0)
    for copy, src, out in ((loads[4], wg, own_g), (loads[5], wu, own_u)):
        copy.wait()
        wide = dot(rows28, src[...]).astype(BF)
        for h in range(2):
            some = dot(wide[:, h * 2432 : (h + 1) * 2432], units[...])
            out[:, h * 768 : (h + 1) * 768] = some.astype(BF)
    for m in range(2):
        second[m].forward()
    spot = (z, x, k, c, zs, xs)
    line = start_line(cp, spot, (do, go, uo), (own_d, own_g, own_u))
    for src, out in ((own_d, do), (own_g, go), (own_u, uo)):
        keep(src, out)
    tokens.forward()
    spread[...] = spread_matrix()
    cosine, sine = rotary(pos, freq)
    turn[0] = cosine
    turn[1] = sine
    for m in range(2):
        second[m].near()
        pass_on(m, 1)
        pass_on(m, 3)
    for ring in line:
        ring.forward()
    for m in range(2):
        second[m].far()
        pass_on(m, 2)
    for copy in local[2:]:
        copy.wait()
    for copy in third:
        copy.wait_recv()
    for ring in line:
        ring.near()
        ring.far()
    plane = start_plane(cp, spot, (do, go, uo))

    i, j = iota((8, DP), 0), iota((8, DP), 1)
    both = dot(where(j % 32 == 7 + 8 * i), oo[...].reshape(DP, D))
    gains[...] = both
    residual = block[...].astype(F32)
    factor = lax.rsqrt(jnp.mean(residual * residual, axis=-1, keepdims=True) + EPSILON)
    normed = (residual * factor * both[0:1]).astype(BF)
    pad = jnp.where(iota((TOK, DP), 1) % 8 == 7, 1.0, dot(normed, spread[...])).astype(BF)
    qkv = dot(pad, ao[...].reshape(DP, 1152))
    kv[:, :128] = turned(qkv[:, 896:1024], cosine, -sine).astype(BF)
    kv[:, 128:] = qkv[:, 1024:].astype(BF)
    copies = [
        cp.go(kv, seen.at[REACH - o], stretch_device(me + o)) for o in range(REACH, 0, -1)
    ]
    seen[REACH] = kv[...]
    for pair in range(HEADS // 2):
        some = slice(pair * 128, (pair + 1) * 128)
        qo[:, some] = turned(qkv[:, some], cosine, -sine).astype(BF)
    spread_heads(qo, qs, 1.0 / math.sqrt(HEAD_SIZE))
    logs[...] = jnp.zeros(logs.shape, F32)
    first_key = REACH * TOK + iota((TOK, 1), 0) - pos[...]
    for copy in copies:
        copy.wait_recv()
    for ring in plane:
        ring.forward()

    def one_head(head, carry):
        keys = seen[:, :, :128].reshape((REACH + 1) * TOK, 128)
        values = seen[:, :, 128:].reshape((REACH + 1) * TOK, 128)
        scores = jnp.where(seen_mask(first_key), dot_t(qs[head], keys), -jnp.inf)
        top = jnp.max(scores, axis=1, keepdims=True)
        weights = jnp.exp(scores - top)
        total = jnp.sum(weights, axis=1, keepdims=True)
        os[head] = dot((weights * (1.0 / total)).astype(BF), values).astype(BF)
        logs[...] += jnp.where(iota((TOK, 128), 1) == head, top + jnp.log(total), 0.0)
        return carry

    lax.fori_loop(0, HEADS, one_head, 0)
    join_heads(os, att)
    att_pad = dot(att[...], spread[...]).astype(BF)
    middle = residual + dot(att_pad, oo[...].reshape(DP, D))
    mid[...] = middle
    factor = lax.rsqrt(jnp.mean(middle * middle, axis=-1, keepdims=True) + EPSILON)
    low[...] = (middle * factor * both[1:2]).astype(BF)
    mid_ring = RingGather(cp, lambda p, h: mo.at[p, rows[h]], lambda h: low.at[rows[h]], c, *ys)
    mo[c] = low[...]
    for ring in plane:
        ring.near()
        ring.far()
    last = [cp.go(ref.at[:, :, k], ref.at[:, :, k], sibling) for ref in (go, uo, do)]
    tokens.near()
    tokens.far()
    token_copy.wait()
    mid_ring.forward()
    mid_ring.near()
    mid_ring.far()
    for copy in last:
        copy.wait_recv()
    cp.finish()


def forward(weights, vec, t, block, pos, freq):
    def out(rows, columns):
        return jax.ShapeDtypeStruct((4, 4, 2, rows, columns), BF)

    packed = ((32, 1152), (32, D)) + FFN
    count = 16 * 2 + 6 + 12 * len(PIECES) + REACH + 3 + 6
    group = jax.ShapeDtypeStruct((4,) + t.shape, BF)
    rows = jax.ShapeDtypeStruct((TOK, D), BF)
    return pl.pallas_call(
        forward_kernel,
        out_shape=[out(*p) for p in packed]
        + [
            group,
            group,
            jax.ShapeDtypeStruct((REACH + 1, TOK, 256), BF),
            rows,
            rows,
            jax.ShapeDtypeStruct((TOK, 128), F32),
            jax.ShapeDtypeStruct((TOK, D), F32),
            jax.ShapeDtypeStruct((8, D), F32),
            jax.ShapeDtypeStruct((2, TOK, 128), F32),
        ],
        in_specs=[HBM] * 7 + [VMEM] + [HBM] + [VMEM] * 3,
        out_specs=[VMEM] * 14,
        scratch_shapes=[pltpu.VMEM(w.shape, BF) for w in weights]
        + [pltpu.VMEM((2432, 16 * UP), BF)]
        + [pltpu.VMEM(p, BF) for p in packed]
        + [
            pltpu.VMEM((D, DP), BF),
            pltpu.VMEM((TOK, 256), BF),
            pltpu.VMEM((TOK, D), BF),
            pltpu.VMEM((HEADS, TOK, 128), BF),
            pltpu.VMEM((HEADS, TOK, 128), BF),
            pltpu.SemaphoreType.DMA((count,)),
            pltpu.SemaphoreType.DMA((count,)),
            pltpu.SemaphoreType.DMA((7,)),
            pltpu.SemaphoreType.DMA((6,)),
        ],
        compiler_params=pltpu.CompilerParams(
            collective_id=0, has_side_effects=True, vmem_limit_bytes=VMEM_FORWARD
        ),
        name="forward",
    )(*weights, vec, t, block, pos, freq)


def back_kernel(q, grad, att, logs, seen, pos, turn, *refs):
    n = len(PIECES)

    def take(count):
        nonlocal refs
        head, refs = refs[:count], refs[count:]
        return head

    ins, (out,), sums = take(n), take(1), take(n)
    own, far, near = take(n), take(n), take(n)
    qs, gs, os, grad_keys, grad_values, parts, got, send, recv, loc = refs
    me = lax.axis_index("fsdp") * 4 + lax.axis_index("ctx")
    z, x, k, c = place()
    zs = [device(plus(z, i), x, k, c) for i in (1, 3)]
    xs = [device(z, plus(x, i), k, c) for i in (1, 3)]
    loads = []
    for m in range(n):
        loads.append(pltpu.make_async_copy(ins[m], own[m], loc.at[m]))
        loads[m].start()
    greet([stretch_device(me + o) for o in range(1, REACH + 1)] + zs + xs)
    cp = Copies(send, recv)
    rings = []
    for m in range(n):
        way = PIECES[m][1]
        loads[m].wait()
        rings.append(
            RingScatter(
                cp,
                functools.partial(half_of, own[m], way),
                functools.partial(add_half, own[m], way),
                z if way else x,
                *(zs if way else xs),
                (far[m].at[0], far[m].at[1]),
                (
                    lambda h, m=m: near[m].at[0, pl.ds(2 * h, 2)],
                    lambda h, m=m: near[m].at[1, pl.ds(2 * h, 2)],
                ),
            )
        )
        rings[m].plain()
    spread_heads(q, qs, 1.0 / math.sqrt(HEAD_SIZE))
    spread_heads(grad, gs, 1.0)
    spread_heads(att, os, 1.0)
    first_key = REACH * TOK + iota((TOK, 1), 0) - pos[...]
    rows = (REACH + 1) * TOK
    grad_keys[...] = jnp.zeros((rows, 128), F32)
    grad_values[...] = jnp.zeros((rows, 128), F32)

    def one(head, carry):
        keys = seen[:, :, :128].reshape(rows, 128)
        values = seen[:, :, 128:].reshape(rows, 128)
        here = iota((TOK, 128), 1) == head
        log_total = jnp.sum(jnp.where(here, logs[...], 0.0), axis=1, keepdims=True)
        delta = jnp.sum(
            gs[head].astype(F32) * os[head].astype(F32), axis=1, keepdims=True
        )
        scores = jnp.where(seen_mask(first_key), dot_t(qs[head], keys), -jnp.inf)
        probability = jnp.exp(scores - log_total)
        grad_scores = (probability * (dot_t(gs[head], values) - delta)).astype(BF)
        grad_values[...] += t_dot(probability.astype(BF), gs[head])
        grad_keys[...] += t_dot(grad_scores, qs[head])
        grad_query = dot(grad_scores, keys) * (1.0 / math.sqrt(HEAD_SIZE))
        os[head] = turned(grad_query, turn[0], turn[1]).astype(BF)
        return carry

    lax.fori_loop(0, HEADS // 2, one, 0)
    for m in range(n):
        rings[m].forward()
    lax.fori_loop(HEADS // 2, HEADS, one, 0)
    parts[:, :, :128] = grad_keys[: REACH * TOK].astype(BF).reshape(REACH, TOK, 128)
    parts[:, :, 128:] = grad_values[: REACH * TOK].astype(BF).reshape(REACH, TOK, 128)
    copies = [
        cp.go(parts.at[REACH - o], got.at[o - 1], stretch_device(me - o))
        for o in range(REACH, 0, -1)
    ]
    join_heads(os, out)
    for m in range(n):
        rings[m].finish()
        sum_line(own[m], near[m], sums[m], PIECES[m][1], z if PIECES[m][1] else x)
    for copy in copies:
        copy.wait_recv()
    total_keys, total_values = grad_keys[REACH * TOK :], grad_values[REACH * TOK :]
    for o in range(REACH):
        total_keys = total_keys + got[o, :, :128].astype(F32)
        total_values = total_values + got[o, :, 128:].astype(F32)
    out[:, 896:1024] = turned(total_keys, turn[0], turn[1]).astype(BF)
    out[:, 1024:] = total_values.astype(BF)
    cp.finish()


def half_of(ref, way, p, h):
    some = pl.ds(2 * h, 2)
    return ref.at[p, some] if way else ref.at[some, p]


def add_half(ref, way, p, h, got):
    def one(j, carry):
        at = (p, 2 * h + j) if way else (2 * h + j, p)
        ref[at] = (ref[at].astype(F32) + got[j].astype(F32)).astype(BF)
        return carry

    lax.fori_loop(0, 2, one, 0)
    return half_of(ref, way, p, h)


def sum_line(own, near, out, way, p):
    def one(j, carry):
        at = (p, j) if way else (j, p)
        total = own[at].astype(F32) + near[0, j].astype(F32)
        out[j] = (total + near[1, j].astype(F32)).astype(BF)
        return carry

    lax.fori_loop(0, 4, one, 0)


def back(q, grad, att, logs, seen, pos, turn, arrays):
    n = len(PIECES)
    shapes = [s.shape[2:] for s in arrays]
    count = REACH + 6 * n
    rows = (REACH + 1) * TOK
    return pl.pallas_call(
        back_kernel,
        out_shape=[jax.ShapeDtypeStruct((TOK, 1152), BF)]
        + [jax.ShapeDtypeStruct((4,) + s, BF) for s in shapes],
        in_specs=[VMEM] * 7 + [ANY] * n,
        out_specs=[VMEM] * (n + 1),
        scratch_shapes=[pltpu.VMEM((4, 4) + s, BF) for s in shapes]
        + [pltpu.VMEM((2, 2) + s, BF) for s in shapes]
        + [pltpu.VMEM((2, 4) + s, BF) for s in shapes]
        + [pltpu.VMEM((HEADS, TOK, 128), BF)] * 3
        + [pltpu.VMEM((rows, 128), F32)] * 2
        + [pltpu.VMEM((REACH, TOK, 256), BF)] * 2
        + [
            pltpu.SemaphoreType.DMA((count,)),
            pltpu.SemaphoreType.DMA((count,)),
            pltpu.SemaphoreType.DMA((n,)),
        ],
        compiler_params=pltpu.CompilerParams(
            collective_id=2, has_side_effects=True, vmem_limit_bytes=58 * 1024 * 1024
        ),
        name="attention_backward",
    )(q, grad, att, logs, seen, pos, turn, *arrays)


def tokens_ring(cp, t, acc, far, near, c, ys):
    rows = halves(t.shape[1])

    def send(p, h):
        return t.at[p, rows[h]]

    def add(p, h, got):
        acc[h] = (t[p, rows[h]].astype(F32) + got[...].astype(F32)).astype(BF)
        return acc.at[h]

    return RingScatter(
        cp,
        send,
        add,
        c,
        *ys,
        (far.at[0], far.at[1]),
        (lambda h: near.at[0, rows[h]], lambda h: near.at[1, rows[h]]),
    )


def tokens_scratch(rows):
    half = (2, rows[0] // 2, rows[1])
    return [pltpu.VMEM(half, BF), pltpu.VMEM(half, BF), pltpu.VMEM((2,) + rows, BF)]


def tokens_sum_kernel(t, hidden, cot, mid, gg, gu, wd, out, part, *refs):
    n = len(PIECES)

    def take(count):
        nonlocal refs
        head, refs = refs[:count], refs[count:]
        return head

    sums, full, got = take(n), take(3), take(n)
    acc, far, near, send, recv = refs
    z, x, k, c = place()
    ys = [device(z, x, k, plus(c, i)) for i in (1, 3)]
    sibling = device(z, x, 1 - k, c)
    greet(ys + [sibling])
    cp = Copies(send, recv)
    ring = tokens_ring(cp, t, acc, far, near, c, ys)
    ring.plain()
    firsts = {}

    def product(m, lhs, rhs):
        rows = lhs.shape[1] // 4
        shape = (4, 2) + full[m].shape[3:]

        def one(i, carry):
            columns = pl.ds(pl.multiple_of(i * rows, 128), rows)
            full[m][i] = t_dot(lhs[:, columns], rhs[...]).astype(BF).reshape(shape)
            return carry

        lax.fori_loop(0, 4, one, 0)
        for j in range(n):
            a, _, first, count, _ = PIECES[j]
            if a == m:
                src = full[m].at[:, :, 1 - k, :, pl.ds(first, count)]
                firsts[j] = cp.go(src, got[j], sibling)

    product(0, hidden, cot)
    ring.forward()
    product(1, mid, gg)
    product(2, mid, gu)
    ring.finish()
    out[...] = t[c].astype(F32) + near[0].astype(F32) + near[1].astype(F32)

    def down(i, carry):
        rows = pl.ds(pl.multiple_of(i * TOK, TOK), TOK)
        part[i] = dot(hidden[rows], wd[...]).astype(BF)
        return carry

    lax.fori_loop(0, 4, down, 0)
    for j in (0, 2, 1, 3):
        a, _, first, count, _ = PIECES[j]
        firsts[j].wait_recv()

        def add(i, carry, j=j, a=a, first=first, count=count):
            at = (i // 4, i % 4)
            mine = full[a][at + (k, slice(None), slice(first, first + count))]
            sums[j][at] = (mine.astype(F32) + got[j][at].astype(F32)).astype(BF)
            return carry

        lax.fori_loop(0, 16, add, 0)
    cp.finish()


def tokens_sum(t, hidden, cot, mid, gg, gu, wd):
    rows = t.shape[1:]
    n = len(PIECES)
    shapes = [(p[4], p[3]) for p in PIECES]
    return pl.pallas_call(
        tokens_sum_kernel,
        out_shape=[jax.ShapeDtypeStruct(rows, F32), jax.ShapeDtypeStruct(t.shape, BF)]
        + [jax.ShapeDtypeStruct((4, 4) + s, BF) for s in shapes],
        in_specs=[VMEM] * 7,
        out_specs=[VMEM] * (n + 2),
        scratch_shapes=[pltpu.VMEM((4, 4, 2) + s, BF) for s in FFN]
        + [pltpu.VMEM((4, 4) + s, BF) for s in shapes]
        + tokens_scratch(rows)
        + [pltpu.SemaphoreType.DMA((6 + n,)), pltpu.SemaphoreType.DMA((6 + n,))],
        compiler_params=pltpu.CompilerParams(
            collective_id=4, has_side_effects=True, vmem_limit_bytes=58 * 1024 * 1024
        ),
        name="scatter_tokens",
    )(t, hidden, cot, mid, gg, gu, wd)


def scatter_kernel(a, o, p0, p1, p2, p3, t, *refs):
    n = len(PIECES)

    def take(count):
        nonlocal refs
        head, refs = refs[:count], refs[count:]
        return head

    outs, (t_out,) = take(2 + n), take(1)
    own, got1, far2, near2, sum2 = (take(2) for _ in range(5))
    line = sum2 + take(n)
    far3, near3, fins, gots = take(2 + n), take(2 + n), take(2 + n), take(2)
    acc, far, near, send, recv, loc = refs
    ins = (a, o)
    ways = (0, 1) + tuple(p[1] for p in PIECES)
    z, x, k, c = place()
    zs = [device(plus(z, i), x, k, c) for i in (1, 3)]
    xs = [device(z, plus(x, i), k, c) for i in (1, 3)]
    ys = [device(z, x, k, plus(c, i)) for i in (1, 2, 3)]
    sibling = device(z, x, 1 - k, c)

    def spot(m, i):
        return plus(z if ways[m] else x, i)

    def piece(ref, m, p, *rest):
        return ref.at[(p, slice(None)) + rest] if ways[m] else ref.at[(slice(None), p) + rest]

    local = {}
    for i in (2, 1, 3, 0):
        for m in range(2):
            p = spot(m, i)
            copy = pltpu.make_async_copy(
                piece(ins[m], m, p, k), piece(own[m], m, p), loc.at[m * 4 + i]
            )
            copy.start()
            local[m, i] = copy
    loads = []
    for m, src in enumerate((p0, p1, p2, p3)):
        loads.append(pltpu.make_async_copy(src, line[2 + m], loc.at[8 + m]))
        loads[m].start()
    greet(zs + xs + ys + [sibling])
    cp = Copies(send, recv)
    first, second, third, closing = {}, [], {}, {}
    for i in (2, 1, 3, 0):
        for m in range(2):
            p = spot(m, i)
            first[m, i] = cp.go(piece(ins[m], m, p, 1 - k), piece(got1[m], m, p), sibling)

    def rows_of(some):
        return pl.ds(0, some.size)

    def start_third(m):
        ref, rows = line[m], halves(line[m].shape[1])

        def send(p, h):
            return ref.at[p, rows[h]]

        def add(p, h, got):
            ref[p, rows[h]] = (ref[p, rows[h]].astype(F32) + got[...].astype(F32)).astype(BF)
            return send(p, h)

        third[m] = RingScatter(
            cp,
            send,
            add,
            x if ways[m] else z,
            *(xs if ways[m] else zs),
            (far3[m].at[0, rows_of(rows[0])], far3[m].at[1, rows_of(rows[1])]),
            (lambda h: near3[m].at[0, rows[h]], lambda h: near3[m].at[1, rows[h]]),
        )
        third[m].plain()

    def close(m):
        third[m].finish()
        total = line[m][x if ways[m] else z].astype(F32)
        total = total + near3[m][0].astype(F32) + near3[m][1].astype(F32)
        if m == 2:
            outs[m][...] = total
            return
        fins[m][...] = total.reshape(fins[m].shape)
        for i in (1, 2, 3):
            target = gots[m].at[i - 1] if m < 2 else outs[m].at[c]
            closing[m, i] = cp.go(fins[m].at[plus(c, i)], target, ys[i - 1])
        if m > 2:
            outs[m][c] = fins[m][c]

    def join(m, i):
        p = spot(m, i)
        local[m, i].wait()
        first[m, i].wait_recv()

        def add(j, carry):
            at = (p, j) if ways[m] else (j, p)
            own[m][at] = (own[m][at].astype(F32) + got1[m][at].astype(F32)).astype(BF)
            return carry

        lax.fori_loop(0, 4, add, 0)

    for m in range(2):
        join(m, 2)
        second.append(
            RingScatter(
                cp,
                functools.partial(half_of, own[m], ways[m]),
                functools.partial(add_half, own[m], ways[m]),
                spot(m, 0),
                *(zs if ways[m] else xs),
                (far2[m].at[0], far2[m].at[1]),
                (
                    lambda h, m=m: near2[m].at[0, pl.ds(2 * h, 2)],
                    lambda h, m=m: near2[m].at[1, pl.ds(2 * h, 2)],
                ),
            )
        )
    for m in range(2):
        join(m, 1)
        join(m, 3)
        second[m].plain()
    for m in range(n):
        loads[m].wait()
        start_third(2 + m)
    tokens = tokens_ring(cp, t, acc, far, near, c, (ys[0], ys[2]))
    tokens.plain()
    for m in range(2):
        second[m].forward()
    for m in range(2):
        join(m, 0)
    for m in range(n):
        third[2 + m].forward()
    tokens.forward()
    for m in range(2):
        second[m].finish()
        sum_line(own[m], near2[m], line[m], ways[m], spot(m, 0))
        start_third(m)
    for m in range(n):
        close(2 + m)
    for m in range(2):
        third[m].forward()
    tokens.finish()
    t_out[...] = t[c].astype(F32) + near[0].astype(F32) + near[1].astype(F32)
    for m in range(2):
        close(m)
    for copy in closing.values():
        copy.wait_recv()
    for m in range(2):
        total = fins[m][c]
        for i in range(3):
            total = total + gots[m][i]
        outs[m][...] = total
    cp.finish()


def scatter(a, o, sums, t):
    n = len(PIECES)
    pair = [a.shape[3:], o.shape[3:]]
    shapes = pair + [s.shape[1:] for s in sums]
    quarter = [(s[0] // 4, s[1]) for s in shapes]
    outs = quarter[:2] + [shapes[2]] + [(4,) + q for q in quarter[3:]]
    scratch = []
    for lead in ((4, 4), (4, 4), (2, 2), (2, 4)):
        scratch += [pltpu.VMEM(lead + s, BF) for s in pair]
    scratch += [pltpu.VMEM((4,) + s, BF) for s in shapes]
    scratch += [pltpu.VMEM((2, halves(s[0])[1].size, s[1]), BF) for s in shapes]
    scratch += [pltpu.VMEM((2,) + s, BF) for s in shapes]
    scratch += [pltpu.VMEM((4,) + q if m != 2 else (8, 128), F32) for m, q in enumerate(quarter)]
    scratch += [pltpu.VMEM((3,) + q, F32) for q in quarter[:2]]
    scratch += tokens_scratch(t.shape[1:])
    count = 2 * 19 + 6 * n + 3 * (n - 1) + 6
    scratch += [
        pltpu.SemaphoreType.DMA((count,)),
        pltpu.SemaphoreType.DMA((count,)),
        pltpu.SemaphoreType.DMA((8 + n,)),
    ]
    return pl.pallas_call(
        scatter_kernel,
        out_shape=[jax.ShapeDtypeStruct(s, F32) for s in outs]
        + [jax.ShapeDtypeStruct(t.shape[1:], F32)],
        in_specs=[ANY] * (2 + n) + [VMEM],
        out_specs=[VMEM] * (3 + n),
        scratch_shapes=scratch,
        compiler_params=pltpu.CompilerParams(
            collective_id=5, has_side_effects=True, vmem_limit_bytes=58 * 1024 * 1024
        ),
        name="scatter_grads",
    )(a, o, *sums, t)


def norm_forward(values):
    factor = lax.rsqrt(jnp.mean(values * values, axis=-1, keepdims=True) + EPSILON)
    return (values * factor, factor)


def norm_backward(grad_out, normed, factor, gain):
    grad_normed = grad_out * gain
    inner = jnp.mean(grad_normed * normed, axis=-1, keepdims=True)
    return (factor * (grad_normed - normed * inner), jnp.sum(grad_out * normed, axis=0))


def dot(a, b):
    return jnp.dot(a, b, preferred_element_type=F32)


def dot_t(a, b):
    return lax.dot_general(a, b, (((1,), (1,)), ((), ())), preferred_element_type=F32)


def t_dot(a, b):
    return lax.dot_general(a, b, (((0,), (0,)), ((), ())), preferred_element_type=F32)


def choose(flags):
    return flags.astype(BF)


def local(
    block_input,
    positions,
    first_gain,
    query_weight,
    query_bias,
    key_weight,
    value_weight,
    value_bias,
    output_weight,
    second_gain,
    gate_weight,
    up_weight,
    down_weight,
    cotangent,
):
    f = lax.axis_index("fsdp")
    c = lax.axis_index("ctx")
    stretch = f * 4 + c

    i896 = jnp.arange(D)
    spread = choose((i896 + i896 // 7)[:, None] == jnp.arange(DP)[None, :])

    half = HEAD_SIZE // 2
    frequency = ROTARY_BASE ** (-(jnp.arange(half, dtype=F32) * 2.0 / HEAD_SIZE))
    places = positions[:, None]
    (
        all_a,
        all_o,
        all_d,
        all_g,
        all_u,
        cot_all,
        mid_all,
        seen,
        query_rot,
        attended,
        logs,
        residual_mid,
        gains,
        turn,
    ) = forward(
        (
            query_weight,
            key_weight,
            value_weight,
            output_weight,
            down_weight,
            gate_weight,
            up_weight,
        ),
        jnp.concatenate([query_bias, value_bias, first_gain, second_gain])[None],
        cotangent,
        block_input,
        places,
        jnp.tile(frequency, 4)[None],
    )
    gain_first, gain_second = gains[0], gains[1]
    all_a = all_a.reshape(DP, 1152)
    weight_output = all_o.reshape(DP, D)
    all_g = all_g.reshape(DP, UC)
    all_u = all_u.reshape(DP, UC)
    all_d = all_d.reshape(UC, D)
    cot_all = cot_all.reshape(4 * TOK, D)
    mid_all = mid_all.reshape(4 * TOK, D)
    pad_ones = (jnp.arange(DP) % 8 == 7).astype(F32)[None, :]
    residual_in = block_input.astype(F32)
    normed_one, scale_one = norm_forward(residual_in)
    normed_input = (normed_one * gain_first).astype(BF)
    input_pad = (dot(normed_input, spread) + pad_ones).astype(BF)
    attended_pad = dot(attended, spread).astype(BF)
    normed_two, scale_two = norm_forward(residual_mid)
    mid_pad = dot(mid_all, spread).astype(BF)
    gate_pre = dot(mid_pad, all_g)
    up_pre = dot(mid_pad, all_u)
    sigma = jax.nn.sigmoid(gate_pre)
    hidden = (gate_pre * sigma * up_pre).astype(BF)
    grad_hidden = dot_t(cot_all, all_d)
    grad_gate_pre = (grad_hidden * up_pre * sigma * (1.0 + gate_pre * (1.0 - sigma))).astype(BF)
    grad_up_pre = (grad_hidden * gate_pre * sigma).astype(BF)
    mid_part = (dot_t(grad_gate_pre, all_g) + dot_t(grad_up_pre, all_u)).astype(BF)
    mid_part = dot_t(mid_part, spread).astype(BF)
    grad_normed_mid, out_part, *sums = tokens_sum(
        mid_part.reshape(4, TOK, D), hidden, cot_all, mid_pad, grad_gate_pre, grad_up_pre, all_d
    )
    grad_norm_part, grad_gain_two = norm_backward(
        grad_normed_mid, normed_two, scale_two, gain_second
    )
    grad_mid = cotangent.astype(F32) + grad_norm_part

    grad_mid_low = grad_mid.astype(BF)
    grad_output_w = t_dot(attended_pad, grad_mid_low)
    grad_attended = dot_t(dot_t(grad_mid_low, weight_output).astype(BF), spread).astype(BF)
    lows, *sums = back(query_rot, grad_attended, attended, logs, seen, places, turn, sums)
    grad_qkv_w = t_dot(input_pad, lows)
    grad_normed_input = dot_t(dot_t(lows, all_a).astype(BF), spread)
    grad_in_part, grad_gain_one = norm_backward(
        grad_normed_input, normed_one, scale_one, gain_first
    )
    grad_input = (grad_mid + grad_in_part).astype(BF)

    group = jnp.arange(DP)[:, None] // 8
    gains = jnp.where(
        i896[None, :] // 7 == group, grad_gain_one[None, :], jnp.roll(grad_gain_two, 448)[None, :]
    )
    grad_output_w = jnp.where(jnp.arange(DP)[:, None] % 8 == 7, gains, grad_output_w)
    sum_a, sum_o, sum_d, sum_u0, sum_g, sum_u1, out_sum = scatter(
        grad_qkv_w.astype(BF).reshape(4, 4, 2, 32, 1152),
        grad_output_w.astype(BF).reshape(4, 4, 2, 32, D),
        sums,
        out_part,
    )
    sum_u = jnp.concatenate([sum_u0, sum_u1], axis=2)
    block_output = (residual_mid + out_sum).astype(BF)

    def columns(parts):
        parts = parts[:, :7].reshape(4, 7, 32, UP)[..., :UN]
        return jnp.transpose(parts, (1, 2, 0, 3)).reshape(7, FF)

    at = 7 * stretch
    return (
        block_output,
        grad_input,
        lax.dynamic_slice(sum_o[7], (at,), (7,)),
        sum_a[:7, :896],
        lax.dynamic_slice(sum_a[7], (at,), (7,)),
        sum_a[:7, 896:1024],
        sum_a[:7, 1024:1152],
        lax.dynamic_slice(sum_a[7], (1024 + stretch,), (1,)),
        sum_o[:7],
        lax.dynamic_slice(sum_o[7], (lax.rem(at + 448, 896),), (7,)),
        columns(sum_g),
        columns(sum_u),
        sum_d[:UN],
    )


def solution(mesh):
    tokens = P(("fsdp", "ctx"), None)
    entries = P(("fsdp", "ctx"))
    rows = P("fsdp", None)
    vector = P("fsdp")
    in_specs = (
        tokens,
        entries,
        vector,
        rows,
        vector,
        rows,
        rows,
        vector,
        rows,
        vector,
        rows,
        rows,
        rows,
        tokens,
    )
    out_specs = (
        tokens,
        tokens,
        entries,
        tokens,
        entries,
        tokens,
        tokens,
        entries,
        tokens,
        entries,
        tokens,
        tokens,
        tokens,
    )
    return jax.shard_map(local, mesh=mesh, in_specs=in_specs, out_specs=out_specs, check_vma=False)
```

```python
import functools
import math

import jax
import jax.numpy as jnp
import numpy as np
from jax import lax
from jax.experimental import pallas as pl
from jax.experimental.pallas import tpu as pltpu
from jax.sharding import PartitionSpec as P

D = 896
HEADS = 14
KV_HEADS = 2
HEAD_SIZE = 64
FF = 4864
SEQ = 1024
TOK = 128
REACH = 8
DP = 1024
UN = 38
UP = 48
UC = 32 * UP
AW = 2048

EPSILON = 1e-06
ROTARY_BASE = 1000000.0
MESH = pl.DeviceIdType.MESH
BF = jnp.bfloat16
F32 = jnp.float32
ANY = pl.BlockSpec(memory_space=pl.ANY)
VMEM = pl.BlockSpec(memory_space=pltpu.VMEM)
HBM = pl.BlockSpec(memory_space=pltpu.HBM)
VMEM_FORWARD = 58 * 1024 * 1024


def place():
    f = lax.axis_index("fsdp")
    return f // 8, (f // 2) % 4, f % 2, lax.axis_index("ctx")


def plus(i, d):
    return lax.rem(i + d, 4)


def device(z, x, k, c):
    return ((z * 4 + x) * 2 + k, c)


def greet(targets):
    barrier = pltpu.get_barrier_semaphore()
    for t in targets:
        pl.semaphore_signal(barrier, inc=1, device_id=t, device_id_type=MESH)
    pl.semaphore_wait(barrier, len(targets))


class Copies:
    def __init__(self, send, recv):
        self.send, self.recv, self.count, self.all = send, recv, 0, []

    def go(self, src, dst, target):
        n = self.count
        self.count += 1
        copy = pltpu.make_async_remote_copy(
            src_ref=src,
            dst_ref=dst,
            send_sem=self.send.at[n],
            recv_sem=self.recv.at[n],
            device_id=target,
            device_id_type=MESH,
        )
        copy.start()
        self.all.append(copy)
        return copy

    def finish(self):
        for copy in self.all:
            copy.wait_send()


class RingGather:
    def __init__(self, cp, part, own, p, up, down):
        self.cp, self.part, self.p, self.up, self.down = cp, part, p, up, down
        self.up0 = cp.go(own(0), part(p, 0), up)
        self.down1 = cp.go(own(1), part(p, 1), down)
        self.up1 = cp.go(own(1), part(p, 1), up)
        self.down0 = cp.go(own(0), part(p, 0), down)

    def forward(self):
        self.up0.wait_recv()
        ref = self.part(plus(self.p, 3), 0)
        self.far0 = self.cp.go(ref, ref, self.up)
        self.down1.wait_recv()
        ref = self.part(plus(self.p, 1), 1)
        self.far1 = self.cp.go(ref, ref, self.down)

    def near(self):
        self.up1.wait_recv()
        self.down0.wait_recv()

    def far(self):
        self.far0.wait_recv()
        self.far1.wait_recv()


class RingScatter:
    def __init__(self, cp, send, add, p, up, down, far, near):
        self.cp, self.send, self.add, self.p, self.up, self.down = cp, send, add, p, up, down
        self.far, self.near = far, near
        self.far0 = cp.go(send(plus(p, 2), 0), far[0], up)
        self.far1 = cp.go(send(plus(p, 2), 1), far[1], down)

    def plain(self):
        self.up1 = self.cp.go(self.send(plus(self.p, 1), 1), self.near[0](1), self.up)
        self.down0 = self.cp.go(self.send(plus(self.p, 3), 0), self.near[1](0), self.down)

    def forward(self):
        self.far0.wait_recv()
        ref = self.add(plus(self.p, 1), 0, self.far[0])
        self.up0 = self.cp.go(ref, self.near[0](0), self.up)
        self.far1.wait_recv()
        ref = self.add(plus(self.p, 3), 1, self.far[1])
        self.down1 = self.cp.go(ref, self.near[1](1), self.down)

    def finish(self):
        for copy in (self.up1, self.down0, self.up0, self.down1):
            copy.wait_recv()


def halves(rows):
    first = rows // 2 // 16 * 16
    return (pl.ds(0, first), pl.ds(first, rows - first))


PIECES = ((0, 0, 0, D, UP), (2, 0, 0, 768, 32), (1, 1, 0, UC, 32), (2, 1, 768, 768, 32))
FFN = ((UP, D), (32, UC), (32, UC))


def start_line(cp, spot, refs, own):
    z, x, k, c, zs, xs = spot
    rings = []
    for n, way, first, count, rows in PIECES:
        cut, cols = halves(rows), pl.ds(first, count)

        def part(p, h, n=n, way=way, cut=cut, cols=cols):
            at = (z, p, k, cut[h], cols) if way else (p, x, k, cut[h], cols)
            return refs[n].at[at]

        def mine(h, n=n, cut=cut, cols=cols):
            return own[n].at[cut[h], cols]

        rings.append(RingGather(cp, part, mine, x if way else z, *(xs if way else zs)))
    return rings


def start_plane(cp, spot, refs):
    z, x, k, c, zs, xs = spot
    rings = []
    for n, way, first, count, rows in PIECES:
        cols = pl.ds(first, count)

        def part(p, h, n=n, way=way, cols=cols):
            some = pl.ds(2 * h, 2)
            at = (p, some, k, slice(None), cols) if way else (some, p, k, slice(None), cols)
            return refs[n].at[at]

        p = z if way else x
        rings.append(RingGather(cp, part, functools.partial(part, p), p, *(zs if way else xs)))
    return rings


def stretch_device(i):
    i = lax.rem(i + 128, 128)
    return (i // 4, lax.rem(i, 4))


def iota(shape, axis):
    return lax.broadcasted_iota(jnp.int32, shape, axis)


def head_move(head, scale):
    i, j = iota((128, 128), 0), iota((128, 128), 1)
    half, group = head % 2, head // (HEADS // KV_HEADS)
    hit = (i // 64 == half) & (j // 64 == group) & (i % 64 == j % 64)
    return (hit.astype(F32) * scale).astype(BF)


def spread_heads(src, out, scale):
    for pair in range(HEADS // 2):
        tile = src[:, pair * 128 : (pair + 1) * 128]
        for head in (2 * pair, 2 * pair + 1):
            out[head] = dot(tile, head_move(head, scale)).astype(BF)


def join_heads(src, out):
    for pair in range(HEADS // 2):
        total = 0.0
        for head in (2 * pair, 2 * pair + 1):
            total = total + dot_t(src[head], head_move(head, 1.0))
        out[:, pair * 128 : (pair + 1) * 128] = total.astype(BF)


def seen_mask(first_key):
    key = iota((TOK, (REACH + 1) * TOK), 1)
    query = REACH * TOK + iota((TOK, 1), 0)
    return (key >= first_key) & (key <= query)


def where(flags):
    return flags.astype(F32).astype(BF)


def spread_matrix():
    i, j = iota((D, DP), 0), iota((D, DP), 1)
    return where(i + i // 7 == j)


def rotary(pos, freq):
    angles = pos[...].astype(F32) * freq[...]
    sign = jnp.where(iota((TOK, 128), 1) % 64 < 32, 1.0, -1.0)
    return jnp.cos(angles), jnp.sin(angles) * sign


def turned(values, cosine, sine):
    low = iota(values.shape, 1) % 64 < 32
    other = jnp.where(low, pltpu.roll(values, 96, 1), pltpu.roll(values, 32, 1))
    return values * cosine + other * sine


def forward_kernel(q, kw, v, o, down, gate, up, vec, t, block, pos, freq, *refs):
    a_out, o_out, do, go, uo, to, mo, seen, qo, att, logs, mid, gains, turn = refs[:14]
    wq, wk, wv, wo, wd, wg, wu, units, own_a, own_o, own_d, own_g, own_u = refs[14:27]
    spread, kv, low, qs, os, ao, oo, send, recv, load, loc = refs[27:]
    z, x, k, c = place()
    f = lax.axis_index("fsdp")
    me = f * 4 + c
    zs = [device(plus(z, i), x, k, c) for i in (1, 3)]
    xs = [device(z, plus(x, i), k, c) for i in (1, 3)]
    ys = [device(z, x, k, plus(c, i)) for i in (1, 3)]
    sibling = device(z, x, 1 - k, c)
    barrier = pltpu.get_barrier_semaphore()
    window = [stretch_device(me - o) for o in range(1, REACH + 1)]
    for device_id in zs + xs + ys + [sibling] + window:
        pl.semaphore_signal(barrier, inc=1, device_id=device_id, device_id_type=MESH)
    loads = [
        pltpu.make_async_copy(src, dst, load.at[i])
        for i, (src, dst) in enumerate(
            ((q, wq), (kw, wk), (v, wv), (o, wo), (gate, wg), (up, wu), (down, wd))
        )
    ]
    for copy in loads:
        copy.start()
    token_copy = pltpu.make_async_copy(t, to.at[c], loc.at[5])
    token_copy.start()

    i = iota((32, 28), 1)
    rows28 = where(i + i // 7 == iota((32, 28), 0))
    row = iota((32, 1), 0)
    i, j = iota((88, 1152), 0), iota((88, 1152), 1)
    place_at = jnp.where(i < 28, 28 * f + i, jnp.where(i < 32, 1024 + 4 * f + i - 28, -1))
    extra = jnp.where(row == 7, dot(vec[...], where(place_at == j)), 0.0)
    for copy in loads[:3]:
        copy.wait()
    own_a[:, :896] = (dot(rows28, wq[...]) + extra[:, :896]).astype(BF)
    own_a[:, 896:1024] = dot(rows28, wk[...]).astype(BF)
    own_a[:, 1024:] = (dot(rows28, wv[...]) + extra[:, 1024:]).astype(BF)
    i, j = iota((88, D), 0), iota((88, D), 1)
    one = dot(vec[...], where((i >= 32) & (i < 60) & (28 * f + i - 32 == j)))
    two = dot(vec[...], where((i >= 60) & (28 * f + i - 60 == j)))
    loads[3].wait()
    own_o[...] = (
        dot(rows28, wo[...]) + jnp.where(row == 7, one, 0.0) + jnp.where(row == 15, two, 0.0)
    ).astype(BF)

    pl.semaphore_wait(barrier, 7 + REACH)
    cp = Copies(send, recv)
    ways = (0, 1)
    own, outs = (own_a, own_o), (ao, oo)
    local = []

    def keep(src, out):
        copy = pltpu.make_async_copy(src, out.at[z, x, k], loc.at[len(local)])
        copy.start()
        local.append(copy)

    first, second, third = [], [], []
    cut = halves(32)
    for m in range(2):

        def part(p, h, m=m):
            return outs[m].at[z, p, k, cut[h]] if ways[m] else outs[m].at[p, x, k, cut[h]]

        def mine(h, m=m):
            return own[m].at[cut[h]]

        first.append(RingGather(cp, part, mine, x if ways[m] else z, *(xs if ways[m] else zs)))
        keep(own[m], outs[m])
    rows = halves(TOK)
    tokens = RingGather(cp, lambda p, h: to.at[p, rows[h]], lambda h: t.at[rows[h]], c, *ys)

    loads[6].wait()
    i, j = iota((UP, 152), 0), iota((UP, 152), 1)
    own_d[...] = dot(where(jnp.where(i < UN, i + UN * c, -1) == j), wd[...]).astype(BF)
    j = iota((1, 16 * UP), 1)
    wanted = jnp.where(j % UP < UN, (j // UP) * 152 + j % UP, -1000) + UN * c
    for m in range(2):
        first[m].forward()
    for r in range(19):
        units[r * 128 : (r + 1) * 128] = where(iota((128, 16 * UP), 0) + r * 128 == wanted)
    for m in range(2):
        first[m].near()
        first[m].far()
        local[m].wait()

        def part(p, h, m=m):
            some = pl.ds(2 * h, 2)
            return outs[m].at[p, some, k] if ways[m] else outs[m].at[some, p, k]

        p = z if ways[m] else x
        second.append(
            RingGather(cp, part, functools.partial(part, p), p, *(zs if ways[m] else xs))
        )

    def pass_on(m, i):
        p = plus(z if ways[m] else x, i)
        ref = outs[m].at[p, :, k] if ways[m] else outs[m].at[:, p, k]
        third.append(cp.go(ref, ref, sibling))

    for m in range(2):
        pass_on(m, 0)
    for copy, src, out in ((loads[4], wg, own_g), (loads[5], wu, own_u)):
        copy.wait()
        wide = dot(rows28, src[...]).astype(BF)
        for h in range(2):
            some = dot(wide[:, h * 2432 : (h + 1) * 2432], units[...])
            out[:, h * 768 : (h + 1) * 768] = some.astype(BF)
    for m in range(2):
        second[m].forward()
    spot = (z, x, k, c, zs, xs)
    line = start_line(cp, spot, (do, go, uo), (own_d, own_g, own_u))
    for src, out in ((own_d, do), (own_g, go), (own_u, uo)):
        keep(src, out)
    tokens.forward()
    spread[...] = spread_matrix()
    cosine, sine = rotary(pos, freq)
    turn[0] = cosine
    turn[1] = sine
    for m in range(2):
        second[m].near()
        pass_on(m, 1)
        pass_on(m, 3)
    for ring in line:
        ring.forward()
    for m in range(2):
        second[m].far()
        pass_on(m, 2)
    for copy in local[2:]:
        copy.wait()
    for copy in third:
        copy.wait_recv()
    stores = [
        pltpu.make_async_copy(ao, a_out, loc.at[6]),
        pltpu.make_async_copy(oo, o_out, loc.at[7]),
    ]
    for copy in stores:
        copy.start()
    for ring in line:
        ring.near()
        ring.far()
    plane = start_plane(cp, spot, (do, go, uo))

    i, j = iota((8, DP), 0), iota((8, DP), 1)
    both = dot(where(j % 32 == 7 + 8 * i), oo[...].reshape(DP, D))
    gains[...] = both
    residual = block[...].astype(F32)
    factor = lax.rsqrt(jnp.mean(residual * residual, axis=-1, keepdims=True) + EPSILON)
    normed = (residual * factor * both[0:1]).astype(BF)
    pad = jnp.where(iota((TOK, DP), 1) % 8 == 7, 1.0, dot(normed, spread[...])).astype(BF)
    qkv = dot(pad, ao[...].reshape(DP, 1152))
    kv[:, :128] = turned(qkv[:, 896:1024], cosine, -sine).astype(BF)
    kv[:, 128:] = qkv[:, 1024:].astype(BF)
    copies = [
        cp.go(kv, seen.at[REACH - o], stretch_device(me + o)) for o in range(REACH, 0, -1)
    ]
    seen[REACH] = kv[...]
    for pair in range(HEADS // 2):
        some = slice(pair * 128, (pair + 1) * 128)
        qo[:, some] = turned(qkv[:, some], cosine, -sine).astype(BF)
    spread_heads(qo, qs, 1.0 / math.sqrt(HEAD_SIZE))
    logs[...] = jnp.zeros(logs.shape, F32)
    first_key = REACH * TOK + iota((TOK, 1), 0) - pos[...]
    for copy in copies:
        copy.wait_recv()
    for ring in plane:
        ring.forward()

    def one_head(head, carry):
        keys = seen[:, :, :128].reshape((REACH + 1) * TOK, 128)
        values = seen[:, :, 128:].reshape((REACH + 1) * TOK, 128)
        scores = jnp.where(seen_mask(first_key), dot_t(qs[head], keys), -jnp.inf)
        top = jnp.max(scores, axis=1, keepdims=True)
        weights = jnp.exp(scores - top)
        total = jnp.sum(weights, axis=1, keepdims=True)
        os[head] = dot((weights * (1.0 / total)).astype(BF), values).astype(BF)
        logs[...] += jnp.where(iota((TOK, 128), 1) == head, top + jnp.log(total), 0.0)
        return carry

    lax.fori_loop(0, HEADS, one_head, 0)
    join_heads(os, att)
    att_pad = dot(att[...], spread[...]).astype(BF)
    middle = residual + dot(att_pad, oo[...].reshape(DP, D))
    mid[...] = middle
    factor = lax.rsqrt(jnp.mean(middle * middle, axis=-1, keepdims=True) + EPSILON)
    low[...] = (middle * factor * both[1:2]).astype(BF)
    mid_ring = RingGather(cp, lambda p, h: mo.at[p, rows[h]], lambda h: low.at[rows[h]], c, *ys)
    stores.append(pltpu.make_async_copy(low, mo.at[c], loc.at[8]))
    stores[2].start()
    for ring in plane:
        ring.near()
        ring.far()
    last = [cp.go(ref.at[:, :, k], ref.at[:, :, k], sibling) for ref in (go, uo, do)]
    tokens.near()
    tokens.far()
    token_copy.wait()
    mid_ring.forward()
    mid_ring.near()
    mid_ring.far()
    for copy in last:
        copy.wait_recv()
    for copy in stores:
        copy.wait()
    cp.finish()


def forward(weights, vec, t, block, pos, freq):
    def out(rows, columns):
        return jax.ShapeDtypeStruct((4, 4, 2, rows, columns), BF)

    packed = ((32, 1152), (32, D)) + FFN
    count = 16 * 2 + 6 + 12 * len(PIECES) + REACH + 3 + 6
    group = jax.ShapeDtypeStruct((4,) + t.shape, BF)
    rows = jax.ShapeDtypeStruct((TOK, D), BF)
    return pl.pallas_call(
        forward_kernel,
        out_shape=[out(*p) for p in packed]
        + [
            group,
            group,
            jax.ShapeDtypeStruct((REACH + 1, TOK, 256), BF),
            rows,
            rows,
            jax.ShapeDtypeStruct((TOK, 128), F32),
            jax.ShapeDtypeStruct((TOK, D), F32),
            jax.ShapeDtypeStruct((8, D), F32),
            jax.ShapeDtypeStruct((2, TOK, 128), F32),
        ],
        in_specs=[HBM] * 7 + [VMEM] + [HBM] + [VMEM] * 3,
        out_specs=[HBM] * 7 + [VMEM] * 7,
        scratch_shapes=[pltpu.VMEM(w.shape, BF) for w in weights]
        + [pltpu.VMEM((2432, 16 * UP), BF)]
        + [pltpu.VMEM(p, BF) for p in packed]
        + [
            pltpu.VMEM((D, DP), BF),
            pltpu.VMEM((TOK, 256), BF),
            pltpu.VMEM((TOK, D), BF),
            pltpu.VMEM((HEADS, TOK, 128), BF),
            pltpu.VMEM((HEADS, TOK, 128), BF),
            pltpu.VMEM((4, 4, 2) + packed[0], BF),
            pltpu.VMEM((4, 4, 2) + packed[1], BF),
            pltpu.SemaphoreType.DMA((count,)),
            pltpu.SemaphoreType.DMA((count,)),
            pltpu.SemaphoreType.DMA((7,)),
            pltpu.SemaphoreType.DMA((9,)),
        ],
        compiler_params=pltpu.CompilerParams(
            collective_id=0, has_side_effects=True, vmem_limit_bytes=VMEM_FORWARD
        ),
        name="forward",
    )(*weights, vec, t, block, pos, freq)


def back_kernel(q, grad, att, logs, seen, pos, turn, *refs):
    n = len(PIECES)

    def take(count):
        nonlocal refs
        head, refs = refs[:count], refs[count:]
        return head

    ins, (out,), sums = take(n), take(1), take(n)
    own, far, near = take(n), take(n), take(n)
    qs, gs, os, grad_keys, grad_values, parts, got, send, recv, loc = refs
    me = lax.axis_index("fsdp") * 4 + lax.axis_index("ctx")
    z, x, k, c = place()
    zs = [device(plus(z, i), x, k, c) for i in (1, 3)]
    xs = [device(z, plus(x, i), k, c) for i in (1, 3)]
    loads = []
    for m in range(n):
        loads.append(pltpu.make_async_copy(ins[m], own[m], loc.at[m]))
        loads[m].start()
    greet([stretch_device(me + o) for o in range(1, REACH + 1)] + zs + xs)
    cp = Copies(send, recv)
    rings = []
    for m in range(n):
        way = PIECES[m][1]
        loads[m].wait()
        rings.append(
            RingScatter(
                cp,
                functools.partial(half_of, own[m], way),
                functools.partial(add_half, own[m], way),
                z if way else x,
                *(zs if way else xs),
                (far[m].at[0], far[m].at[1]),
                (
                    lambda h, m=m: near[m].at[0, pl.ds(2 * h, 2)],
                    lambda h, m=m: near[m].at[1, pl.ds(2 * h, 2)],
                ),
            )
        )
        rings[m].plain()
    spread_heads(q, qs, 1.0 / math.sqrt(HEAD_SIZE))
    spread_heads(grad, gs, 1.0)
    spread_heads(att, os, 1.0)
    first_key = REACH * TOK + iota((TOK, 1), 0) - pos[...]
    rows = (REACH + 1) * TOK
    grad_keys[...] = jnp.zeros((rows, 128), F32)
    grad_values[...] = jnp.zeros((rows, 128), F32)

    def one(head, carry):
        keys = seen[:, :, :128].reshape(rows, 128)
        values = seen[:, :, 128:].reshape(rows, 128)
        here = iota((TOK, 128), 1) == head
        log_total = jnp.sum(jnp.where(here, logs[...], 0.0), axis=1, keepdims=True)
        delta = jnp.sum(
            gs[head].astype(F32) * os[head].astype(F32), axis=1, keepdims=True
        )
        scores = jnp.where(seen_mask(first_key), dot_t(qs[head], keys), -jnp.inf)
        probability = jnp.exp(scores - log_total)
        grad_scores = (probability * (dot_t(gs[head], values) - delta)).astype(BF)
        grad_values[...] += t_dot(probability.astype(BF), gs[head])
        grad_keys[...] += t_dot(grad_scores, qs[head])
        grad_query = dot(grad_scores, keys) * (1.0 / math.sqrt(HEAD_SIZE))
        os[head] = turned(grad_query, turn[0], turn[1]).astype(BF)
        return carry

    lax.fori_loop(0, HEADS // 2, one, 0)
    for m in range(n):
        rings[m].forward()
    lax.fori_loop(HEADS // 2, HEADS, one, 0)
    parts[:, :, :128] = grad_keys[: REACH * TOK].astype(BF).reshape(REACH, TOK, 128)
    parts[:, :, 128:] = grad_values[: REACH * TOK].astype(BF).reshape(REACH, TOK, 128)
    copies = [
        cp.go(parts.at[REACH - o], got.at[o - 1], stretch_device(me - o))
        for o in range(REACH, 0, -1)
    ]
    join_heads(os, out)
    for m in range(n):
        rings[m].finish()
        sum_line(own[m], near[m], sums[m], PIECES[m][1], z if PIECES[m][1] else x)
    for copy in copies:
        copy.wait_recv()
    total_keys, total_values = grad_keys[REACH * TOK :], grad_values[REACH * TOK :]
    for o in range(REACH):
        total_keys = total_keys + got[o, :, :128].astype(F32)
        total_values = total_values + got[o, :, 128:].astype(F32)
    out[:, 896:1024] = turned(total_keys, turn[0], turn[1]).astype(BF)
    out[:, 1024:] = total_values.astype(BF)
    cp.finish()


def half_of(ref, way, p, h):
    some = pl.ds(2 * h, 2)
    return ref.at[p, some] if way else ref.at[some, p]


def add_half(ref, way, p, h, got):
    def one(j, carry):
        at = (p, 2 * h + j) if way else (2 * h + j, p)
        ref[at] = (ref[at].astype(F32) + got[j].astype(F32)).astype(BF)
        return carry

    lax.fori_loop(0, 2, one, 0)
    return half_of(ref, way, p, h)


def sum_line(own, near, out, way, p):
    def one(j, carry):
        at = (p, j) if way else (j, p)
        total = own[at].astype(F32) + near[0, j].astype(F32)
        out[j] = (total + near[1, j].astype(F32)).astype(BF)
        return carry

    lax.fori_loop(0, 4, one, 0)


def back(q, grad, att, logs, seen, pos, turn, arrays):
    n = len(PIECES)
    shapes = [s.shape[2:] for s in arrays]
    count = REACH + 6 * n
    rows = (REACH + 1) * TOK
    return pl.pallas_call(
        back_kernel,
        out_shape=[jax.ShapeDtypeStruct((TOK, 1152), BF)]
        + [jax.ShapeDtypeStruct((4,) + s, BF) for s in shapes],
        in_specs=[VMEM] * 7 + [ANY] * n,
        out_specs=[VMEM] * (n + 1),
        scratch_shapes=[pltpu.VMEM((4, 4) + s, BF) for s in shapes]
        + [pltpu.VMEM((2, 2) + s, BF) for s in shapes]
        + [pltpu.VMEM((2, 4) + s, BF) for s in shapes]
        + [pltpu.VMEM((HEADS, TOK, 128), BF)] * 3
        + [pltpu.VMEM((rows, 128), F32)] * 2
        + [pltpu.VMEM((REACH, TOK, 256), BF)] * 2
        + [
            pltpu.SemaphoreType.DMA((count,)),
            pltpu.SemaphoreType.DMA((count,)),
            pltpu.SemaphoreType.DMA((n,)),
        ],
        compiler_params=pltpu.CompilerParams(
            collective_id=2, has_side_effects=True, vmem_limit_bytes=58 * 1024 * 1024
        ),
        name="attention_backward",
    )(q, grad, att, logs, seen, pos, turn, *arrays)


def tokens_ring(cp, t, acc, far, near, c, ys):
    rows = halves(t.shape[1])

    def send(p, h):
        return t.at[p, rows[h]]

    def add(p, h, got):
        acc[h] = (t[p, rows[h]].astype(F32) + got[...].astype(F32)).astype(BF)
        return acc.at[h]

    return RingScatter(
        cp,
        send,
        add,
        c,
        *ys,
        (far.at[0], far.at[1]),
        (lambda h: near.at[0, rows[h]], lambda h: near.at[1, rows[h]]),
    )


def tokens_scratch(rows):
    half = (2, rows[0] // 2, rows[1])
    return [pltpu.VMEM(half, BF), pltpu.VMEM(half, BF), pltpu.VMEM((2,) + rows, BF)]


def tokens_sum_kernel(*refs):
    n = len(PIECES)

    def take(count):
        nonlocal refs
        head, refs = refs[:count], refs[count:]
        return head

    ins, (out, part_out), sums = take(7), take(2), take(n)
    loaded, full, got = take(7), take(3), take(n)
    part, acc, far, near, send, recv, load, store = refs
    t, hidden, cot, mid, gg, gu, wd = loaded
    z, x, k, c = place()
    ys = [device(z, x, k, plus(c, i)) for i in (1, 3)]
    sibling = device(z, x, 1 - k, c)
    loads = [pltpu.make_async_copy(ins[i], loaded[i], load.at[i]) for i in range(7)]
    for copy in loads:
        copy.start()
    greet(ys + [sibling])
    cp = Copies(send, recv)
    loads[0].wait()
    ring = tokens_ring(cp, t, acc, far, near, c, ys)
    ring.plain()
    firsts = {}

    def product(m, lhs, rhs):
        rows = lhs.shape[1] // 4
        shape = (4, 2) + full[m].shape[3:]

        def one(i, carry):
            columns = pl.ds(pl.multiple_of(i * rows, 128), rows)
            full[m][i] = t_dot(lhs[:, columns], rhs[...]).astype(BF).reshape(shape)
            return carry

        lax.fori_loop(0, 4, one, 0)
        for j in range(n):
            a, _, first, count, _ = PIECES[j]
            if a == m:
                src = full[m].at[:, :, 1 - k, :, pl.ds(first, count)]
                firsts[j] = cp.go(src, got[j], sibling)

    loads[1].wait()
    loads[2].wait()
    product(0, hidden, cot)
    ring.forward()
    loads[3].wait()
    loads[4].wait()
    product(1, mid, gg)
    loads[5].wait()
    product(2, mid, gu)
    ring.finish()
    out[...] = t[c].astype(F32) + near[0].astype(F32) + near[1].astype(F32)

    def down(i, carry):
        rows = pl.ds(pl.multiple_of(i * TOK, TOK), TOK)
        part[i] = dot(hidden[rows], wd[...]).astype(BF)
        return carry

    loads[6].wait()
    lax.fori_loop(0, 4, down, 0)
    stores = [pltpu.make_async_copy(part, part_out, store.at[n])]
    stores[0].start()
    for j in (0, 2, 1, 3):
        a, _, first, count, _ = PIECES[j]
        firsts[j].wait_recv()

        def add(i, carry, j=j, a=a, first=first, count=count):
            at = (i // 4, i % 4)
            mine = full[a][at + (k, slice(None), slice(first, first + count))]
            got[j][at] = (mine.astype(F32) + got[j][at].astype(F32)).astype(BF)
            return carry

        lax.fori_loop(0, 16, add, 0)
        copy = pltpu.make_async_copy(got[j], sums[j], store.at[j])
        copy.start()
        stores.append(copy)
    for copy in stores:
        copy.wait()
    cp.finish()


def tokens_sum(t, hidden, cot, mid, gg, gu, wd):
    rows = t.shape[1:]
    n = len(PIECES)
    shapes = [(p[4], p[3]) for p in PIECES]
    return pl.pallas_call(
        tokens_sum_kernel,
        out_shape=[jax.ShapeDtypeStruct(rows, F32), jax.ShapeDtypeStruct(t.shape, BF)]
        + [jax.ShapeDtypeStruct((4, 4) + s, BF) for s in shapes],
        in_specs=[HBM] * 7,
        out_specs=[VMEM] + [HBM] * (n + 1),
        scratch_shapes=[pltpu.VMEM(s.shape, BF) for s in (t, hidden, cot, mid, gg, gu, wd)]
        + [pltpu.VMEM((4, 4, 2) + s, BF) for s in FFN]
        + [pltpu.VMEM((4, 4) + s, BF) for s in shapes]
        + [pltpu.VMEM(t.shape, BF)]
        + tokens_scratch(rows)
        + [
            pltpu.SemaphoreType.DMA((6 + n,)),
            pltpu.SemaphoreType.DMA((6 + n,)),
            pltpu.SemaphoreType.DMA((7,)),
            pltpu.SemaphoreType.DMA((n + 1,)),
        ],
        compiler_params=pltpu.CompilerParams(
            collective_id=4, has_side_effects=True, vmem_limit_bytes=58 * 1024 * 1024
        ),
        name="scatter_tokens",
    )(t, hidden, cot, mid, gg, gu, wd)


def scatter_kernel(a, o, p0, p1, p2, p3, t, mid, *refs):
    n = len(PIECES)

    def take(count):
        nonlocal refs
        head, refs = refs[:count], refs[count:]
        return head

    (q_out, k_out, v_out, a_vec, o_out, o_vec, d_out), outs, (t_out,) = take(7), take(n - 1), take(1)
    own, got1, far2, near2, sum2 = (take(2) for _ in range(5))
    line = sum2 + take(n)
    far3, near3, fins, gots = take(2 + n), take(2 + n), take(2 + n), take(2)
    acc, far, near, send, recv, loc = refs
    ins = (a, o)
    ways = (0, 1) + tuple(p[1] for p in PIECES)
    z, x, k, c = place()
    zs = [device(plus(z, i), x, k, c) for i in (1, 3)]
    xs = [device(z, plus(x, i), k, c) for i in (1, 3)]
    ys = [device(z, x, k, plus(c, i)) for i in (1, 2, 3)]
    sibling = device(z, x, 1 - k, c)

    def spot(m, i):
        return plus(z if ways[m] else x, i)

    def piece(ref, m, p, *rest):
        return ref.at[(p, slice(None)) + rest] if ways[m] else ref.at[(slice(None), p) + rest]

    local = {}
    for i in (2, 1, 3, 0):
        for m in range(2):
            p = spot(m, i)
            copy = pltpu.make_async_copy(
                piece(ins[m], m, p, k), piece(own[m], m, p), loc.at[m * 4 + i]
            )
            copy.start()
            local[m, i] = copy
    loads = []
    for m, src in enumerate((p0, p1, p2, p3)):
        loads.append(pltpu.make_async_copy(src, line[2 + m], loc.at[8 + m]))
        loads[m].start()
    greet(zs + xs + ys + [sibling])
    cp = Copies(send, recv)
    first, second, third, closing = {}, [], {}, {}
    for i in (2, 1, 3, 0):
        for m in range(2):
            p = spot(m, i)
            first[m, i] = cp.go(piece(ins[m], m, p, 1 - k), piece(got1[m], m, p), sibling)

    def rows_of(some):
        return pl.ds(0, some.size)

    def start_third(m):
        ref, rows = line[m], halves(line[m].shape[1])

        def send(p, h):
            return ref.at[p, rows[h]]

        def add(p, h, got):
            ref[p, rows[h]] = (ref[p, rows[h]].astype(F32) + got[...].astype(F32)).astype(BF)
            return send(p, h)

        third[m] = RingScatter(
            cp,
            send,
            add,
            x if ways[m] else z,
            *(xs if ways[m] else zs),
            (far3[m].at[0, rows_of(rows[0])], far3[m].at[1, rows_of(rows[1])]),
            (lambda h: near3[m].at[0, rows[h]], lambda h: near3[m].at[1, rows[h]]),
        )
        third[m].plain()

    def close(m):
        third[m].finish()
        total = line[m][x if ways[m] else z].astype(F32)
        total = total + near3[m][0].astype(F32) + near3[m][1].astype(F32)
        if m == 2:
            d_out[...] = total[:UN]
            return
        fins[m][...] = total.reshape(fins[m].shape)
        for i in (1, 2, 3):
            target = gots[m].at[i - 1] if m < 2 else outs[m - 3].at[c]
            closing[m, i] = cp.go(fins[m].at[plus(c, i)], target, ys[i - 1])
        if m > 2:
            outs[m - 3][c] = fins[m][c]

    def join(m, i):
        p = spot(m, i)
        local[m, i].wait()
        first[m, i].wait_recv()

        def add(j, carry):
            at = (p, j) if ways[m] else (j, p)
            own[m][at] = (own[m][at].astype(F32) + got1[m][at].astype(F32)).astype(BF)
            return carry

        lax.fori_loop(0, 4, add, 0)

    for m in range(2):
        join(m, 2)
        second.append(
            RingScatter(
                cp,
                functools.partial(half_of, own[m], ways[m]),
                functools.partial(add_half, own[m], ways[m]),
                spot(m, 0),
                *(zs if ways[m] else xs),
                (far2[m].at[0], far2[m].at[1]),
                (
                    lambda h, m=m: near2[m].at[0, pl.ds(2 * h, 2)],
                    lambda h, m=m: near2[m].at[1, pl.ds(2 * h, 2)],
                ),
            )
        )
    for m in range(2):
        join(m, 1)
        join(m, 3)
        second[m].plain()
    for m in range(n):
        loads[m].wait()
        start_third(2 + m)
    tokens = tokens_ring(cp, t, acc, far, near, c, (ys[0], ys[2]))
    tokens.plain()
    for m in range(2):
        second[m].forward()
    for m in range(2):
        join(m, 0)
    for m in range(n):
        third[2 + m].forward()
    tokens.forward()
    for m in range(2):
        second[m].finish()
        sum_line(own[m], near2[m], line[m], ways[m], spot(m, 0))
        start_third(m)
    for m in range(n):
        close(2 + m)
    for m in range(2):
        third[m].forward()
    tokens.finish()
    total = t[c].astype(F32) + near[0].astype(F32) + near[1].astype(F32)
    t_out[...] = (mid[...] + total).astype(BF)
    for m in range(2):
        close(m)
    for copy in closing.values():
        copy.wait_recv()
    joined = []
    for m in range(2):
        total = fins[m][c]
        for i in range(3):
            total = total + gots[m][i]
        joined.append(total)
    q_out[...] = joined[0][:7, :896]
    k_out[...] = joined[0][:7, 896:1024]
    v_out[...] = joined[0][:7, 1024:]
    a_vec[...] = joined[0][7:]
    o_out[...] = joined[1][:7]
    o_vec[...] = joined[1][7:]
    cp.finish()


def scatter(a, o, sums, t, mid):
    n = len(PIECES)
    pair = [a.shape[3:], o.shape[3:]]
    shapes = pair + [s.shape[1:] for s in sums]
    quarter = [(s[0] // 4, s[1]) for s in shapes]
    outs = [(7, 896), (7, 128), (7, 128), (1, 1152), (7, D), (1, D), (UN, D)]
    outs += [(4,) + q for q in quarter[3:]]
    scratch = []
    for lead in ((4, 4), (4, 4), (2, 2), (2, 4)):
        scratch += [pltpu.VMEM(lead + s, BF) for s in pair]
    scratch += [pltpu.VMEM((4,) + s, BF) for s in shapes]
    scratch += [pltpu.VMEM((2, halves(s[0])[1].size, s[1]), BF) for s in shapes]
    scratch += [pltpu.VMEM((2,) + s, BF) for s in shapes]
    scratch += [pltpu.VMEM((4,) + q if m != 2 else (8, 128), F32) for m, q in enumerate(quarter)]
    scratch += [pltpu.VMEM((3,) + q, F32) for q in quarter[:2]]
    scratch += tokens_scratch(t.shape[1:])
    count = 2 * 19 + 6 * n + 3 * (n - 1) + 6
    scratch += [
        pltpu.SemaphoreType.DMA((count,)),
        pltpu.SemaphoreType.DMA((count,)),
        pltpu.SemaphoreType.DMA((8 + n,)),
    ]
    return pl.pallas_call(
        scatter_kernel,
        out_shape=[jax.ShapeDtypeStruct(s, F32) for s in outs]
        + [jax.ShapeDtypeStruct(t.shape[1:], BF)],
        in_specs=[ANY] * (2 + n) + [VMEM] * 2,
        out_specs=[VMEM] * (7 + n),
        scratch_shapes=scratch,
        compiler_params=pltpu.CompilerParams(
            collective_id=5, has_side_effects=True, vmem_limit_bytes=58 * 1024 * 1024
        ),
        name="scatter_grads",
    )(a, o, *sums, t, mid)


def norm_forward(values):
    factor = lax.rsqrt(jnp.mean(values * values, axis=-1, keepdims=True) + EPSILON)
    return (values * factor, factor)


def norm_backward(grad_out, normed, factor, gain):
    grad_normed = grad_out * gain
    inner = jnp.mean(grad_normed * normed, axis=-1, keepdims=True)
    return (factor * (grad_normed - normed * inner), jnp.sum(grad_out * normed, axis=0))


def dot(a, b):
    return jnp.dot(a, b, preferred_element_type=F32)


def dot_t(a, b):
    return lax.dot_general(a, b, (((1,), (1,)), ((), ())), preferred_element_type=F32)


def t_dot(a, b):
    return lax.dot_general(a, b, (((0,), (0,)), ((), ())), preferred_element_type=F32)


def choose(flags):
    return flags.astype(BF)


def local(
    block_input,
    positions,
    first_gain,
    query_weight,
    query_bias,
    key_weight,
    value_weight,
    value_bias,
    output_weight,
    second_gain,
    gate_weight,
    up_weight,
    down_weight,
    cotangent,
):
    f = lax.axis_index("fsdp")
    c = lax.axis_index("ctx")
    stretch = f * 4 + c

    i896 = jnp.arange(D)
    spread = choose((i896 + i896 // 7)[:, None] == jnp.arange(DP)[None, :])

    half = HEAD_SIZE // 2
    frequency = ROTARY_BASE ** (-(np.arange(half) * 2.0 / HEAD_SIZE))
    places = positions[:, None]
    (
        all_a,
        all_o,
        all_d,
        all_g,
        all_u,
        cot_all,
        mid_all,
        seen,
        query_rot,
        attended,
        logs,
        residual_mid,
        gains,
        turn,
    ) = forward(
        (
            query_weight,
            key_weight,
            value_weight,
            output_weight,
            down_weight,
            gate_weight,
            up_weight,
        ),
        jnp.concatenate([query_bias, value_bias, first_gain, second_gain])[None],
        cotangent,
        block_input,
        places,
        jnp.asarray(np.tile(frequency, 4)[None], F32),
    )
    gain_first, gain_second = gains[0], gains[1]
    all_a = all_a.reshape(DP, 1152)
    weight_output = all_o.reshape(DP, D)
    all_g = all_g.reshape(DP, UC)
    all_u = all_u.reshape(DP, UC)
    all_d = all_d.reshape(UC, D)
    cot_all = cot_all.reshape(4 * TOK, D)
    mid_all = mid_all.reshape(4 * TOK, D)
    pad_ones = (jnp.arange(DP) % 8 == 7).astype(F32)[None, :]
    residual_in = block_input.astype(F32)
    normed_one, scale_one = norm_forward(residual_in)
    normed_input = (normed_one * gain_first).astype(BF)
    input_pad = (dot(normed_input, spread) + pad_ones).astype(BF)
    attended_pad = dot(attended, spread).astype(BF)
    normed_two, scale_two = norm_forward(residual_mid)
    mid_pad = dot(mid_all, spread).astype(BF)
    gate_pre = dot(mid_pad, all_g)
    up_pre = dot(mid_pad, all_u)
    sigma = jax.nn.sigmoid(gate_pre)
    hidden = (gate_pre * sigma * up_pre).astype(BF)
    grad_hidden = dot_t(cot_all, all_d)
    grad_gate_pre = (grad_hidden * up_pre * sigma * (1.0 + gate_pre * (1.0 - sigma))).astype(BF)
    grad_up_pre = (grad_hidden * gate_pre * sigma).astype(BF)
    mid_part = (dot_t(grad_gate_pre, all_g) + dot_t(grad_up_pre, all_u)).astype(BF)
    mid_part = dot_t(mid_part, spread).astype(BF)
    grad_normed_mid, out_part, *sums = tokens_sum(
        mid_part.reshape(4, TOK, D), hidden, cot_all, mid_pad, grad_gate_pre, grad_up_pre, all_d
    )
    grad_norm_part, grad_gain_two = norm_backward(
        grad_normed_mid, normed_two, scale_two, gain_second
    )
    grad_mid = cotangent.astype(F32) + grad_norm_part

    grad_mid_low = grad_mid.astype(BF)
    grad_output_w = t_dot(attended_pad, grad_mid_low)
    grad_attended = dot_t(dot_t(grad_mid_low, weight_output).astype(BF), spread).astype(BF)
    lows, *sums = back(query_rot, grad_attended, attended, logs, seen, places, turn, sums)
    grad_qkv_w = t_dot(input_pad, lows)
    grad_normed_input = dot_t(dot_t(lows, all_a).astype(BF), spread)
    grad_in_part, grad_gain_one = norm_backward(
        grad_normed_input, normed_one, scale_one, gain_first
    )
    grad_input = (grad_mid + grad_in_part).astype(BF)

    group = jnp.arange(DP)[:, None] // 8
    gains = jnp.where(
        i896[None, :] // 7 == group, grad_gain_one[None, :], jnp.roll(grad_gain_two, 448)[None, :]
    )
    grad_output_w = jnp.where(jnp.arange(DP)[:, None] % 8 == 7, gains, grad_output_w)
    sum_q, sum_k, sum_v, vec_a, sum_o, vec_o, sum_d, sum_u0, sum_g, sum_u1, block_output = scatter(
        grad_qkv_w.astype(BF).reshape(4, 4, 2, 32, 1152),
        grad_output_w.astype(BF).reshape(4, 4, 2, 32, D),
        sums,
        out_part,
        residual_mid,
    )
    sum_u = jnp.concatenate([sum_u0, sum_u1], axis=2)

    def columns(parts):
        parts = parts[:, :7].reshape(4, 7, 32, UP)[..., :UN]
        return jnp.transpose(parts, (1, 2, 0, 3)).reshape(7, FF)

    at = 7 * stretch
    return (
        block_output,
        grad_input,
        lax.dynamic_slice(vec_o[0], (at,), (7,)),
        sum_q,
        lax.dynamic_slice(vec_a[0], (at,), (7,)),
        sum_k,
        sum_v,
        lax.dynamic_slice(vec_a[0], (1024 + stretch,), (1,)),
        sum_o,
        lax.dynamic_slice(vec_o[0], (lax.rem(at + 448, 896),), (7,)),
        columns(sum_g),
        columns(sum_u),
        sum_d,
    )


def solution(mesh):
    tokens = P(("fsdp", "ctx"), None)
    entries = P(("fsdp", "ctx"))
    rows = P("fsdp", None)
    vector = P("fsdp")
    in_specs = (
        tokens,
        entries,
        vector,
        rows,
        vector,
        rows,
        rows,
        vector,
        rows,
        vector,
        rows,
        rows,
        rows,
        tokens,
    )
    out_specs = (
        tokens,
        tokens,
        entries,
        tokens,
        entries,
        tokens,
        tokens,
        entries,
        tokens,
        entries,
        tokens,
        tokens,
        tokens,
    )
    return jax.shard_map(local, mesh=mesh, in_specs=in_specs, out_specs=out_specs, check_vma=False)
```

```python
import functools
import math

import jax
import jax.numpy as jnp
import numpy as np
from jax import lax
from jax.experimental import pallas as pl
from jax.experimental.pallas import tpu as pltpu
from jax.sharding import PartitionSpec as P

D = 896
HEADS = 14
KV_HEADS = 2
HEAD_SIZE = 64
FF = 4864
SEQ = 1024
TOK = 128
REACH = 8
DP = 1024
UN = 38
UP = 48
UC = 32 * UP
AW = 2048

EPSILON = 1e-06
ROTARY_BASE = 1000000.0
MESH = pl.DeviceIdType.MESH
BF = jnp.bfloat16
F32 = jnp.float32
ANY = pl.BlockSpec(memory_space=pl.ANY)
VMEM = pl.BlockSpec(memory_space=pltpu.VMEM)
HBM = pl.BlockSpec(memory_space=pltpu.HBM)
VMEM_FORWARD = 58 * 1024 * 1024


def place():
    f = lax.axis_index("fsdp")
    return f // 8, (f // 2) % 4, f % 2, lax.axis_index("ctx")


def plus(i, d):
    return lax.rem(i + d, 4)


def device(z, x, k, c):
    return ((z * 4 + x) * 2 + k, c)


def greet(targets):
    barrier = pltpu.get_barrier_semaphore()
    for t in targets:
        pl.semaphore_signal(barrier, inc=1, device_id=t, device_id_type=MESH)
    pl.semaphore_wait(barrier, len(targets))


class Copies:
    def __init__(self, send, recv):
        self.send, self.recv, self.count, self.all = send, recv, 0, []

    def go(self, src, dst, target):
        n = self.count
        self.count += 1
        copy = pltpu.make_async_remote_copy(
            src_ref=src,
            dst_ref=dst,
            send_sem=self.send.at[n],
            recv_sem=self.recv.at[n],
            device_id=target,
            device_id_type=MESH,
        )
        copy.start()
        self.all.append(copy)
        return copy

    def finish(self):
        for copy in self.all:
            copy.wait_send()


class RingGather:
    def __init__(self, cp, part, own, p, up, down):
        self.cp, self.part, self.p, self.up, self.down = cp, part, p, up, down
        self.up0 = cp.go(own(0), part(p, 0), up)
        self.down1 = cp.go(own(1), part(p, 1), down)
        self.up1 = cp.go(own(1), part(p, 1), up)
        self.down0 = cp.go(own(0), part(p, 0), down)

    def forward(self):
        self.up0.wait_recv()
        ref = self.part(plus(self.p, 3), 0)
        self.far0 = self.cp.go(ref, ref, self.up)
        self.down1.wait_recv()
        ref = self.part(plus(self.p, 1), 1)
        self.far1 = self.cp.go(ref, ref, self.down)

    def near(self):
        self.up1.wait_recv()
        self.down0.wait_recv()

    def far(self):
        self.far0.wait_recv()
        self.far1.wait_recv()


class RingScatter:
    def __init__(self, cp, send, add, p, up, down, far, near):
        self.cp, self.send, self.add, self.p, self.up, self.down = cp, send, add, p, up, down
        self.far, self.near = far, near
        self.far0 = cp.go(send(plus(p, 2), 0), far[0], up)
        self.far1 = cp.go(send(plus(p, 2), 1), far[1], down)

    def plain(self):
        self.up1 = self.cp.go(self.send(plus(self.p, 1), 1), self.near[0](1), self.up)
        self.down0 = self.cp.go(self.send(plus(self.p, 3), 0), self.near[1](0), self.down)

    def forward(self):
        self.far0.wait_recv()
        ref = self.add(plus(self.p, 1), 0, self.far[0])
        self.up0 = self.cp.go(ref, self.near[0](0), self.up)
        self.far1.wait_recv()
        ref = self.add(plus(self.p, 3), 1, self.far[1])
        self.down1 = self.cp.go(ref, self.near[1](1), self.down)

    def finish(self):
        for copy in (self.up1, self.down0, self.up0, self.down1):
            copy.wait_recv()


def halves(rows):
    first = rows // 2 // 16 * 16
    return (pl.ds(0, first), pl.ds(first, rows - first))


PIECES = ((0, 0, 0, D, UP), (2, 0, 0, 768, 32), (1, 1, 0, UC, 32), (2, 1, 768, 768, 32))
FFN = ((UP, D), (32, UC), (32, UC))


def start_line(cp, spot, refs, own):
    z, x, k, c, zs, xs = spot
    rings = []
    for n, way, first, count, rows in PIECES:
        cut, cols = halves(rows), pl.ds(first, count)

        def part(p, h, n=n, way=way, cut=cut, cols=cols):
            at = (z, p, k, cut[h], cols) if way else (p, x, k, cut[h], cols)
            return refs[n].at[at]

        def mine(h, n=n, cut=cut, cols=cols):
            return own[n].at[cut[h], cols]

        rings.append(RingGather(cp, part, mine, x if way else z, *(xs if way else zs)))
    return rings


def start_plane(cp, spot, refs):
    z, x, k, c, zs, xs = spot
    rings = []
    for n, way, first, count, rows in PIECES:
        cols = pl.ds(first, count)

        def part(p, h, n=n, way=way, cols=cols):
            some = pl.ds(2 * h, 2)
            at = (p, some, k, slice(None), cols) if way else (some, p, k, slice(None), cols)
            return refs[n].at[at]

        p = z if way else x
        rings.append(RingGather(cp, part, functools.partial(part, p), p, *(zs if way else xs)))
    return rings


def stretch_device(i):
    i = lax.rem(i + 128, 128)
    return (i // 4, lax.rem(i, 4))


def iota(shape, axis):
    return lax.broadcasted_iota(jnp.int32, shape, axis)


def head_move(head, scale):
    i, j = iota((128, 128), 0), iota((128, 128), 1)
    half, group = head % 2, head // (HEADS // KV_HEADS)
    hit = (i // 64 == half) & (j // 64 == group) & (i % 64 == j % 64)
    return (hit.astype(F32) * scale).astype(BF)


def spread_heads(src, out, scale):
    for pair in range(HEADS // 2):
        tile = src[:, pair * 128 : (pair + 1) * 128]
        for head in (2 * pair, 2 * pair + 1):
            out[head] = dot(tile, head_move(head, scale)).astype(BF)


def join_heads(src, out):
    for pair in range(HEADS // 2):
        total = 0.0
        for head in (2 * pair, 2 * pair + 1):
            total = total + dot_t(src[head], head_move(head, 1.0))
        out[:, pair * 128 : (pair + 1) * 128] = total.astype(BF)


def column(row):
    same = iota((TOK, TOK), 0) == iota((TOK, TOK), 1)
    return jnp.sum(jnp.where(same, row.astype(F32), 0.0), axis=1, keepdims=True).astype(jnp.int32)


def seen_mask(first_key):
    key = iota((TOK, (REACH + 1) * TOK), 1)
    query = REACH * TOK + iota((TOK, 1), 0)
    return (key >= first_key) & (key <= query)


def where(flags):
    return flags.astype(F32).astype(BF)


def spread_matrix():
    i, j = iota((D, DP), 0), iota((D, DP), 1)
    return where(i + i // 7 == j)


def rotary(pos, freq):
    angles = pos.astype(F32) * freq[...]
    sign = jnp.where(iota((TOK, 128), 1) % 64 < 32, 1.0, -1.0)
    return jnp.cos(angles), jnp.sin(angles) * sign


def turned(values, cosine, sine):
    low = iota(values.shape, 1) % 64 < 32
    other = jnp.where(low, pltpu.roll(values, 96, 1), pltpu.roll(values, 32, 1))
    return values * cosine + other * sine


def forward_kernel(q, kw, v, o, down, gate, up, qb, vb, g1, g2, t, block, pos, freq, *refs):
    a_out, o_out, do, go, uo, to, mo, seen, qo, att, logs, mid, gains, turn = refs[:14]
    wq, wk, wv, wo, wd, wg, wu, units, own_a, own_o, own_d, own_g, own_u = refs[14:27]
    spread, kv, low, qs, os, ao, oo, send, recv, load, loc = refs[27:]
    z, x, k, c = place()
    f = lax.axis_index("fsdp")
    me = f * 4 + c
    zs = [device(plus(z, i), x, k, c) for i in (1, 3)]
    xs = [device(z, plus(x, i), k, c) for i in (1, 3)]
    ys = [device(z, x, k, plus(c, i)) for i in (1, 3)]
    sibling = device(z, x, 1 - k, c)
    barrier = pltpu.get_barrier_semaphore()
    window = [stretch_device(me - o) for o in range(1, REACH + 1)]
    for device_id in zs + xs + ys + [sibling] + window:
        pl.semaphore_signal(barrier, inc=1, device_id=device_id, device_id_type=MESH)
    loads = [
        pltpu.make_async_copy(src, dst, load.at[i])
        for i, (src, dst) in enumerate(
            ((q, wq), (kw, wk), (v, wv), (o, wo), (gate, wg), (up, wu), (down, wd))
        )
    ]
    for copy in loads:
        copy.start()
    token_copy = pltpu.make_async_copy(t, to.at[c], loc.at[5])
    token_copy.start()

    i = iota((32, 28), 1)
    rows28 = where(i + i // 7 == iota((32, 28), 0))
    row = iota((32, 1), 0)
    i, j = iota((28, D), 0), iota((28, D), 1)
    entries = where(28 * f + i == j)
    extra = jnp.where(row == 7, dot(qb[...], entries), 0.0)
    i, j = iota((4, 128), 0), iota((4, 128), 1)
    extra_value = jnp.where(row == 7, dot(vb[...], where(4 * f + i == j)), 0.0)
    for copy in loads[:3]:
        copy.wait()
    own_a[:, :896] = (dot(rows28, wq[...]) + extra).astype(BF)
    own_a[:, 896:1024] = dot(rows28, wk[...]).astype(BF)
    own_a[:, 1024:] = (dot(rows28, wv[...]) + extra_value).astype(BF)
    one, two = dot(g1[...], entries), dot(g2[...], entries)
    loads[3].wait()
    own_o[...] = (
        dot(rows28, wo[...]) + jnp.where(row == 7, one, 0.0) + jnp.where(row == 15, two, 0.0)
    ).astype(BF)

    pl.semaphore_wait(barrier, 7 + REACH)
    cp = Copies(send, recv)
    ways = (0, 1)
    own, outs = (own_a, own_o), (ao, oo)
    local = []

    def keep(src, out):
        copy = pltpu.make_async_copy(src, out.at[z, x, k], loc.at[len(local)])
        copy.start()
        local.append(copy)

    first, second, third = [], [], []
    cut = halves(32)
    for m in range(2):

        def part(p, h, m=m):
            return outs[m].at[z, p, k, cut[h]] if ways[m] else outs[m].at[p, x, k, cut[h]]

        def mine(h, m=m):
            return own[m].at[cut[h]]

        first.append(RingGather(cp, part, mine, x if ways[m] else z, *(xs if ways[m] else zs)))
        keep(own[m], outs[m])
    rows = halves(TOK)
    tokens = RingGather(cp, lambda p, h: to.at[p, rows[h]], lambda h: t.at[rows[h]], c, *ys)

    loads[6].wait()
    i, j = iota((UP, 152), 0), iota((UP, 152), 1)
    own_d[...] = dot(where(jnp.where(i < UN, i + UN * c, -1) == j), wd[...]).astype(BF)
    j = iota((1, 16 * UP), 1)
    wanted = jnp.where(j % UP < UN, (j // UP) * 152 + j % UP, -1000) + UN * c
    for m in range(2):
        first[m].forward()
    for r in range(19):
        units[r * 128 : (r + 1) * 128] = where(iota((128, 16 * UP), 0) + r * 128 == wanted)
    for m in range(2):
        first[m].near()
        first[m].far()
        local[m].wait()

        def part(p, h, m=m):
            some = pl.ds(2 * h, 2)
            return outs[m].at[p, some, k] if ways[m] else outs[m].at[some, p, k]

        p = z if ways[m] else x
        second.append(
            RingGather(cp, part, functools.partial(part, p), p, *(zs if ways[m] else xs))
        )

    def pass_on(m, i):
        p = plus(z if ways[m] else x, i)
        ref = outs[m].at[p, :, k] if ways[m] else outs[m].at[:, p, k]
        third.append(cp.go(ref, ref, sibling))

    for m in range(2):
        pass_on(m, 0)
    for copy, src, out in ((loads[4], wg, own_g), (loads[5], wu, own_u)):
        copy.wait()
        wide = dot(rows28, src[...]).astype(BF)
        for h in range(2):
            some = dot(wide[:, h * 2432 : (h + 1) * 2432], units[...])
            out[:, h * 768 : (h + 1) * 768] = some.astype(BF)
    for m in range(2):
        second[m].forward()
    spot = (z, x, k, c, zs, xs)
    line = start_line(cp, spot, (do, go, uo), (own_d, own_g, own_u))
    for src, out in ((own_d, do), (own_g, go), (own_u, uo)):
        keep(src, out)
    tokens.forward()
    spread[...] = spread_matrix()
    spots = column(pos[...])
    cosine, sine = rotary(spots, freq)
    turn[0] = cosine
    turn[1] = sine
    for m in range(2):
        second[m].near()
        pass_on(m, 1)
        pass_on(m, 3)
    for ring in line:
        ring.forward()
    for m in range(2):
        second[m].far()
        pass_on(m, 2)
    for copy in local[2:]:
        copy.wait()
    for copy in third:
        copy.wait_recv()
    stores = [
        pltpu.make_async_copy(ao, a_out, loc.at[6]),
        pltpu.make_async_copy(oo, o_out, loc.at[7]),
    ]
    for copy in stores:
        copy.start()
    for ring in line:
        ring.near()
        ring.far()
    plane = start_plane(cp, spot, (do, go, uo))

    i, j = iota((8, DP), 0), iota((8, DP), 1)
    both = dot(where(j % 32 == 7 + 8 * i), oo[...].reshape(DP, D))
    gains[...] = both
    residual = block[...].astype(F32)
    factor = lax.rsqrt(jnp.mean(residual * residual, axis=-1, keepdims=True) + EPSILON)
    normed = (residual * factor * both[0:1]).astype(BF)
    pad = jnp.where(iota((TOK, DP), 1) % 8 == 7, 1.0, dot(normed, spread[...])).astype(BF)
    qkv = dot(pad, ao[...].reshape(DP, 1152))
    kv[:, :128] = turned(qkv[:, 896:1024], cosine, -sine).astype(BF)
    kv[:, 128:] = qkv[:, 1024:].astype(BF)
    copies = [
        cp.go(kv, seen.at[REACH - o], stretch_device(me + o)) for o in range(REACH, 0, -1)
    ]
    seen[REACH] = kv[...]
    for pair in range(HEADS // 2):
        some = slice(pair * 128, (pair + 1) * 128)
        qo[:, some] = turned(qkv[:, some], cosine, -sine).astype(BF)
    spread_heads(qo, qs, 1.0 / math.sqrt(HEAD_SIZE))
    logs[...] = jnp.zeros(logs.shape, F32)
    first_key = REACH * TOK + iota((TOK, 1), 0) - spots
    for copy in copies:
        copy.wait_recv()
    for ring in plane:
        ring.forward()

    def one_head(head, carry):
        keys = seen[:, :, :128].reshape((REACH + 1) * TOK, 128)
        values = seen[:, :, 128:].reshape((REACH + 1) * TOK, 128)
        scores = jnp.where(seen_mask(first_key), dot_t(qs[head], keys), -jnp.inf)
        top = jnp.max(scores, axis=1, keepdims=True)
        weights = jnp.exp(scores - top)
        total = jnp.sum(weights, axis=1, keepdims=True)
        os[head] = dot((weights * (1.0 / total)).astype(BF), values).astype(BF)
        logs[...] += jnp.where(iota((TOK, 128), 1) == head, top + jnp.log(total), 0.0)
        return carry

    lax.fori_loop(0, HEADS, one_head, 0)
    join_heads(os, att)
    att_pad = dot(att[...], spread[...]).astype(BF)
    middle = residual + dot(att_pad, oo[...].reshape(DP, D))
    mid[...] = middle
    factor = lax.rsqrt(jnp.mean(middle * middle, axis=-1, keepdims=True) + EPSILON)
    low[...] = (middle * factor * both[1:2]).astype(BF)
    mid_ring = RingGather(cp, lambda p, h: mo.at[p, rows[h]], lambda h: low.at[rows[h]], c, *ys)
    stores.append(pltpu.make_async_copy(low, mo.at[c], loc.at[8]))
    stores[2].start()
    for ring in plane:
        ring.near()
        ring.far()
    last = [cp.go(ref.at[:, :, k], ref.at[:, :, k], sibling) for ref in (go, uo, do)]
    tokens.near()
    tokens.far()
    token_copy.wait()
    mid_ring.forward()
    mid_ring.near()
    mid_ring.far()
    for copy in last:
        copy.wait_recv()
    for copy in stores:
        copy.wait()
    cp.finish()


def forward(weights, vectors, t, block, pos, freq):
    def out(rows, columns):
        return jax.ShapeDtypeStruct((4, 4, 2, rows, columns), BF)

    packed = ((32, 1152), (32, D)) + FFN
    count = 16 * 2 + 6 + 12 * len(PIECES) + REACH + 3 + 6
    group = jax.ShapeDtypeStruct((4,) + t.shape, BF)
    rows = jax.ShapeDtypeStruct((TOK, D), BF)
    return pl.pallas_call(
        forward_kernel,
        out_shape=[out(*p) for p in packed]
        + [
            group,
            group,
            jax.ShapeDtypeStruct((REACH + 1, TOK, 256), BF),
            rows,
            rows,
            jax.ShapeDtypeStruct((TOK, 128), F32),
            jax.ShapeDtypeStruct((TOK, D), F32),
            jax.ShapeDtypeStruct((8, D), F32),
            jax.ShapeDtypeStruct((2, TOK, 128), F32),
        ],
        in_specs=[HBM] * 7 + [VMEM] * 4 + [HBM] + [VMEM] * 3,
        out_specs=[HBM] * 7 + [VMEM] * 7,
        scratch_shapes=[pltpu.VMEM(w.shape, BF) for w in weights]
        + [pltpu.VMEM((2432, 16 * UP), BF)]
        + [pltpu.VMEM(p, BF) for p in packed]
        + [
            pltpu.VMEM((D, DP), BF),
            pltpu.VMEM((TOK, 256), BF),
            pltpu.VMEM((TOK, D), BF),
            pltpu.VMEM((HEADS, TOK, 128), BF),
            pltpu.VMEM((HEADS, TOK, 128), BF),
            pltpu.VMEM((4, 4, 2) + packed[0], BF),
            pltpu.VMEM((4, 4, 2) + packed[1], BF),
            pltpu.SemaphoreType.DMA((count,)),
            pltpu.SemaphoreType.DMA((count,)),
            pltpu.SemaphoreType.DMA((7,)),
            pltpu.SemaphoreType.DMA((9,)),
        ],
        compiler_params=pltpu.CompilerParams(
            collective_id=0, has_side_effects=True, vmem_limit_bytes=VMEM_FORWARD
        ),
        name="forward",
    )(*weights, *vectors, t, block, pos, freq)


def back_kernel(q, grad, att, logs, seen, pos, turn, *refs):
    n = len(PIECES)

    def take(count):
        nonlocal refs
        head, refs = refs[:count], refs[count:]
        return head

    ins, (out,), sums = take(n), take(1), take(n)
    own, far, near = take(n), take(n), take(n)
    qs, gs, os, grad_keys, grad_values, parts, got, send, recv, loc = refs
    me = lax.axis_index("fsdp") * 4 + lax.axis_index("ctx")
    z, x, k, c = place()
    zs = [device(plus(z, i), x, k, c) for i in (1, 3)]
    xs = [device(z, plus(x, i), k, c) for i in (1, 3)]
    loads = []
    for m in range(n):
        loads.append(pltpu.make_async_copy(ins[m], own[m], loc.at[m]))
        loads[m].start()
    greet([stretch_device(me + o) for o in range(1, REACH + 1)] + zs + xs)
    cp = Copies(send, recv)
    rings = []
    for m in range(n):
        way = PIECES[m][1]
        loads[m].wait()
        rings.append(
            RingScatter(
                cp,
                functools.partial(half_of, own[m], way),
                functools.partial(add_half, own[m], way),
                z if way else x,
                *(zs if way else xs),
                (far[m].at[0], far[m].at[1]),
                (
                    lambda h, m=m: near[m].at[0, pl.ds(2 * h, 2)],
                    lambda h, m=m: near[m].at[1, pl.ds(2 * h, 2)],
                ),
            )
        )
        rings[m].plain()
    spread_heads(q, qs, 1.0 / math.sqrt(HEAD_SIZE))
    spread_heads(grad, gs, 1.0)
    spread_heads(att, os, 1.0)
    first_key = REACH * TOK + iota((TOK, 1), 0) - column(pos[...])
    rows = (REACH + 1) * TOK
    grad_keys[...] = jnp.zeros((rows, 128), F32)
    grad_values[...] = jnp.zeros((rows, 128), F32)

    def one(head, carry):
        keys = seen[:, :, :128].reshape(rows, 128)
        values = seen[:, :, 128:].reshape(rows, 128)
        here = iota((TOK, 128), 1) == head
        log_total = jnp.sum(jnp.where(here, logs[...], 0.0), axis=1, keepdims=True)
        delta = jnp.sum(
            gs[head].astype(F32) * os[head].astype(F32), axis=1, keepdims=True
        )
        scores = jnp.where(seen_mask(first_key), dot_t(qs[head], keys), -jnp.inf)
        probability = jnp.exp(scores - log_total)
        grad_scores = (probability * (dot_t(gs[head], values) - delta)).astype(BF)
        grad_values[...] += t_dot(probability.astype(BF), gs[head])
        grad_keys[...] += t_dot(grad_scores, qs[head])
        grad_query = dot(grad_scores, keys) * (1.0 / math.sqrt(HEAD_SIZE))
        os[head] = turned(grad_query, turn[0], turn[1]).astype(BF)
        return carry

    lax.fori_loop(0, HEADS // 2, one, 0)
    for m in range(n):
        rings[m].forward()
    lax.fori_loop(HEADS // 2, HEADS, one, 0)
    parts[:, :, :128] = grad_keys[: REACH * TOK].astype(BF).reshape(REACH, TOK, 128)
    parts[:, :, 128:] = grad_values[: REACH * TOK].astype(BF).reshape(REACH, TOK, 128)
    copies = [
        cp.go(parts.at[REACH - o], got.at[o - 1], stretch_device(me - o))
        for o in range(REACH, 0, -1)
    ]
    join_heads(os, out)
    for m in range(n):
        rings[m].finish()
        sum_line(own[m], near[m], sums[m], PIECES[m][1], z if PIECES[m][1] else x)
    for copy in copies:
        copy.wait_recv()
    total_keys, total_values = grad_keys[REACH * TOK :], grad_values[REACH * TOK :]
    for o in range(REACH):
        total_keys = total_keys + got[o, :, :128].astype(F32)
        total_values = total_values + got[o, :, 128:].astype(F32)
    out[:, 896:1024] = turned(total_keys, turn[0], turn[1]).astype(BF)
    out[:, 1024:] = total_values.astype(BF)
    cp.finish()


def half_of(ref, way, p, h):
    some = pl.ds(2 * h, 2)
    return ref.at[p, some] if way else ref.at[some, p]


def add_half(ref, way, p, h, got):
    def one(j, carry):
        at = (p, 2 * h + j) if way else (2 * h + j, p)
        ref[at] = (ref[at].astype(F32) + got[j].astype(F32)).astype(BF)
        return carry

    lax.fori_loop(0, 2, one, 0)
    return half_of(ref, way, p, h)


def sum_line(own, near, out, way, p):
    def one(j, carry):
        at = (p, j) if way else (j, p)
        total = own[at].astype(F32) + near[0, j].astype(F32)
        out[j] = (total + near[1, j].astype(F32)).astype(BF)
        return carry

    lax.fori_loop(0, 4, one, 0)


def back(q, grad, att, logs, seen, pos, turn, arrays):
    n = len(PIECES)
    shapes = [s.shape[2:] for s in arrays]
    count = REACH + 6 * n
    rows = (REACH + 1) * TOK
    return pl.pallas_call(
        back_kernel,
        out_shape=[jax.ShapeDtypeStruct((TOK, 1152), BF)]
        + [jax.ShapeDtypeStruct((4,) + s, BF) for s in shapes],
        in_specs=[VMEM] * 7 + [ANY] * n,
        out_specs=[VMEM] * (n + 1),
        scratch_shapes=[pltpu.VMEM((4, 4) + s, BF) for s in shapes]
        + [pltpu.VMEM((2, 2) + s, BF) for s in shapes]
        + [pltpu.VMEM((2, 4) + s, BF) for s in shapes]
        + [pltpu.VMEM((HEADS, TOK, 128), BF)] * 3
        + [pltpu.VMEM((rows, 128), F32)] * 2
        + [pltpu.VMEM((REACH, TOK, 256), BF)] * 2
        + [
            pltpu.SemaphoreType.DMA((count,)),
            pltpu.SemaphoreType.DMA((count,)),
            pltpu.SemaphoreType.DMA((n,)),
        ],
        compiler_params=pltpu.CompilerParams(
            collective_id=2, has_side_effects=True, vmem_limit_bytes=58 * 1024 * 1024
        ),
        name="attention_backward",
    )(q, grad, att, logs, seen, pos, turn, *arrays)


def tokens_ring(cp, t, acc, far, near, c, ys):
    rows = halves(t.shape[1])

    def send(p, h):
        return t.at[p, rows[h]]

    def add(p, h, got):
        acc[h] = (t[p, rows[h]].astype(F32) + got[...].astype(F32)).astype(BF)
        return acc.at[h]

    return RingScatter(
        cp,
        send,
        add,
        c,
        *ys,
        (far.at[0], far.at[1]),
        (lambda h: near.at[0, rows[h]], lambda h: near.at[1, rows[h]]),
    )


def tokens_scratch(rows):
    half = (2, rows[0] // 2, rows[1])
    return [pltpu.VMEM(half, BF), pltpu.VMEM(half, BF), pltpu.VMEM((2,) + rows, BF)]


def tokens_sum_kernel(*refs):
    n = len(PIECES)

    def take(count):
        nonlocal refs
        head, refs = refs[:count], refs[count:]
        return head

    ins, (out, part_out), sums = take(7), take(2), take(n)
    loaded, full, got = take(7), take(3), take(n)
    part, acc, far, near, send, recv, load, store = refs
    t, hidden, cot, mid, gg, gu, wd = loaded
    z, x, k, c = place()
    ys = [device(z, x, k, plus(c, i)) for i in (1, 3)]
    sibling = device(z, x, 1 - k, c)
    loads = [pltpu.make_async_copy(ins[i], loaded[i], load.at[i]) for i in range(7)]
    for copy in loads:
        copy.start()
    greet(ys + [sibling])
    cp = Copies(send, recv)
    loads[0].wait()
    ring = tokens_ring(cp, t, acc, far, near, c, ys)
    ring.plain()
    firsts = {}

    def product(m, lhs, rhs):
        rows = lhs.shape[1] // 4
        shape = (4, 2) + full[m].shape[3:]

        def one(i, carry):
            columns = pl.ds(pl.multiple_of(i * rows, 128), rows)
            full[m][i] = t_dot(lhs[:, columns], rhs[...]).astype(BF).reshape(shape)
            return carry

        lax.fori_loop(0, 4, one, 0)
        for j in range(n):
            a, _, first, count, _ = PIECES[j]
            if a == m:
                src = full[m].at[:, :, 1 - k, :, pl.ds(first, count)]
                firsts[j] = cp.go(src, got[j], sibling)

    loads[1].wait()
    loads[2].wait()
    product(0, hidden, cot)
    ring.forward()
    loads[3].wait()
    loads[4].wait()
    product(1, mid, gg)
    loads[5].wait()
    product(2, mid, gu)
    ring.finish()
    out[...] = t[c].astype(F32) + near[0].astype(F32) + near[1].astype(F32)

    def down(i, carry):
        rows = pl.ds(pl.multiple_of(i * TOK, TOK), TOK)
        part[i] = dot(hidden[rows], wd[...]).astype(BF)
        return carry

    loads[6].wait()
    lax.fori_loop(0, 4, down, 0)
    stores = [pltpu.make_async_copy(part, part_out, store.at[n])]
    stores[0].start()
    for j in (0, 2, 1, 3):
        a, _, first, count, _ = PIECES[j]
        firsts[j].wait_recv()

        def add(i, carry, j=j, a=a, first=first, count=count):
            at = (i // 4, i % 4)
            mine = full[a][at + (k, slice(None), slice(first, first + count))]
            got[j][at] = (mine.astype(F32) + got[j][at].astype(F32)).astype(BF)
            return carry

        lax.fori_loop(0, 16, add, 0)
        copy = pltpu.make_async_copy(got[j], sums[j], store.at[j])
        copy.start()
        stores.append(copy)
    for copy in stores:
        copy.wait()
    cp.finish()


def tokens_sum(t, hidden, cot, mid, gg, gu, wd):
    rows = t.shape[1:]
    n = len(PIECES)
    shapes = [(p[4], p[3]) for p in PIECES]
    return pl.pallas_call(
        tokens_sum_kernel,
        out_shape=[jax.ShapeDtypeStruct(rows, F32), jax.ShapeDtypeStruct(t.shape, BF)]
        + [jax.ShapeDtypeStruct((4, 4) + s, BF) for s in shapes],
        in_specs=[HBM] * 7,
        out_specs=[VMEM] + [HBM] * (n + 1),
        scratch_shapes=[pltpu.VMEM(s.shape, BF) for s in (t, hidden, cot, mid, gg, gu, wd)]
        + [pltpu.VMEM((4, 4, 2) + s, BF) for s in FFN]
        + [pltpu.VMEM((4, 4) + s, BF) for s in shapes]
        + [pltpu.VMEM(t.shape, BF)]
        + tokens_scratch(rows)
        + [
            pltpu.SemaphoreType.DMA((6 + n,)),
            pltpu.SemaphoreType.DMA((6 + n,)),
            pltpu.SemaphoreType.DMA((7,)),
            pltpu.SemaphoreType.DMA((n + 1,)),
        ],
        compiler_params=pltpu.CompilerParams(
            collective_id=4, has_side_effects=True, vmem_limit_bytes=58 * 1024 * 1024
        ),
        name="scatter_tokens",
    )(t, hidden, cot, mid, gg, gu, wd)


def scatter_kernel(a, o, p0, p1, p2, p3, t, mid, *refs):
    n = len(PIECES)

    def take(count):
        nonlocal refs
        head, refs = refs[:count], refs[count:]
        return head

    (q_out, k_out, v_out, a_vec, o_out, o_vec, d_out), (wide, t_out) = take(7), take(2)
    own, got1, far2, near2, sum2 = (take(2) for _ in range(5))
    line = sum2 + take(n)
    far3, near3, fins, gots = take(2 + n), take(2 + n), take(2 + n), take(2)
    acc, far, near, send, recv, loc = refs
    ins = (a, o)
    ways = (0, 1) + tuple(p[1] for p in PIECES)
    z, x, k, c = place()
    zs = [device(plus(z, i), x, k, c) for i in (1, 3)]
    xs = [device(z, plus(x, i), k, c) for i in (1, 3)]
    ys = [device(z, x, k, plus(c, i)) for i in (1, 2, 3)]
    sibling = device(z, x, 1 - k, c)

    def spot(m, i):
        return plus(z if ways[m] else x, i)

    def piece(ref, m, p, *rest):
        return ref.at[(p, slice(None)) + rest] if ways[m] else ref.at[(slice(None), p) + rest]

    local = {}
    for i in (2, 1, 3, 0):
        for m in range(2):
            p = spot(m, i)
            copy = pltpu.make_async_copy(
                piece(ins[m], m, p, k), piece(own[m], m, p), loc.at[m * 4 + i]
            )
            copy.start()
            local[m, i] = copy
    loads = []
    for m, src in enumerate((p0, p1, p2, p3)):
        loads.append(pltpu.make_async_copy(src, line[2 + m], loc.at[8 + m]))
        loads[m].start()
    greet(zs + xs + ys + [sibling])
    cp = Copies(send, recv)
    first, second, third, closing = {}, [], {}, {}
    for i in (2, 1, 3, 0):
        for m in range(2):
            p = spot(m, i)
            first[m, i] = cp.go(piece(ins[m], m, p, 1 - k), piece(got1[m], m, p), sibling)

    def rows_of(some):
        return pl.ds(0, some.size)

    def start_third(m):
        ref, rows = line[m], halves(line[m].shape[1])

        def send(p, h):
            return ref.at[p, rows[h]]

        def add(p, h, got):
            ref[p, rows[h]] = (ref[p, rows[h]].astype(F32) + got[...].astype(F32)).astype(BF)
            return send(p, h)

        third[m] = RingScatter(
            cp,
            send,
            add,
            x if ways[m] else z,
            *(xs if ways[m] else zs),
            (far3[m].at[0, rows_of(rows[0])], far3[m].at[1, rows_of(rows[1])]),
            (lambda h: near3[m].at[0, rows[h]], lambda h: near3[m].at[1, rows[h]]),
        )
        third[m].plain()

    def columns(m):
        array, _, first, count, _ = PIECES[m - 2]
        return pl.ds((array - 1) * UC + first, count)

    def close(m):
        third[m].finish()
        total = line[m][x if ways[m] else z].astype(F32)
        total = total + near3[m][0].astype(F32) + near3[m][1].astype(F32)
        if m == 2:
            d_out[...] = total[:UN]
            return
        fins[m][...] = total.reshape(fins[m].shape)
        for i in (1, 2, 3):
            target = gots[m].at[i - 1] if m < 2 else wide.at[c, :, columns(m)]
            closing[m, i] = cp.go(fins[m].at[plus(c, i)], target, ys[i - 1])
        if m > 2:
            wide[c, :, columns(m)] = fins[m][c]

    def join(m, i):
        p = spot(m, i)
        local[m, i].wait()
        first[m, i].wait_recv()

        def add(j, carry):
            at = (p, j) if ways[m] else (j, p)
            own[m][at] = (own[m][at].astype(F32) + got1[m][at].astype(F32)).astype(BF)
            return carry

        lax.fori_loop(0, 4, add, 0)

    for m in range(2):
        join(m, 2)
        second.append(
            RingScatter(
                cp,
                functools.partial(half_of, own[m], ways[m]),
                functools.partial(add_half, own[m], ways[m]),
                spot(m, 0),
                *(zs if ways[m] else xs),
                (far2[m].at[0], far2[m].at[1]),
                (
                    lambda h, m=m: near2[m].at[0, pl.ds(2 * h, 2)],
                    lambda h, m=m: near2[m].at[1, pl.ds(2 * h, 2)],
                ),
            )
        )
    for m in range(2):
        join(m, 1)
        join(m, 3)
        second[m].plain()
    for m in range(n):
        loads[m].wait()
        start_third(2 + m)
    tokens = tokens_ring(cp, t, acc, far, near, c, (ys[0], ys[2]))
    tokens.plain()
    for m in range(2):
        second[m].forward()
    for m in range(2):
        join(m, 0)
    for m in range(n):
        third[2 + m].forward()
    tokens.forward()
    for m in range(2):
        second[m].finish()
        sum_line(own[m], near2[m], line[m], ways[m], spot(m, 0))
        start_third(m)
    for m in range(n):
        close(2 + m)
    for m in range(2):
        third[m].forward()
    tokens.finish()
    total = t[c].astype(F32) + near[0].astype(F32) + near[1].astype(F32)
    t_out[...] = (mid[...] + total).astype(BF)
    for m in range(2):
        close(m)
    for copy in closing.values():
        copy.wait_recv()
    joined = []
    for m in range(2):
        total = fins[m][c]
        for i in range(3):
            total = total + gots[m][i]
        joined.append(total)
    q_out[...] = joined[0][:7, :896]
    k_out[...] = joined[0][:7, 896:1024]
    v_out[...] = joined[0][:7, 1024:]
    a_vec[...] = joined[0][7:]
    o_out[...] = joined[1][:7]
    o_vec[...] = joined[1][7:]
    cp.finish()


def scatter(a, o, sums, t, mid):
    n = len(PIECES)
    pair = [a.shape[3:], o.shape[3:]]
    shapes = pair + [s.shape[1:] for s in sums]
    quarter = [(s[0] // 4, s[1]) for s in shapes]
    outs = [(7, 896), (7, 128), (7, 128), (1, 1152), (7, D), (1, D), (UN, D)]
    outs += [(4, 8, 2 * UC)]
    scratch = []
    for lead in ((4, 4), (4, 4), (2, 2), (2, 4)):
        scratch += [pltpu.VMEM(lead + s, BF) for s in pair]
    scratch += [pltpu.VMEM((4,) + s, BF) for s in shapes]
    scratch += [pltpu.VMEM((2, halves(s[0])[1].size, s[1]), BF) for s in shapes]
    scratch += [pltpu.VMEM((2,) + s, BF) for s in shapes]
    scratch += [pltpu.VMEM((4,) + q if m != 2 else (8, 128), F32) for m, q in enumerate(quarter)]
    scratch += [pltpu.VMEM((3,) + q, F32) for q in quarter[:2]]
    scratch += tokens_scratch(t.shape[1:])
    count = 2 * 19 + 6 * n + 3 * (n - 1) + 6
    scratch += [
        pltpu.SemaphoreType.DMA((count,)),
        pltpu.SemaphoreType.DMA((count,)),
        pltpu.SemaphoreType.DMA((8 + n,)),
    ]
    return pl.pallas_call(
        scatter_kernel,
        out_shape=[jax.ShapeDtypeStruct(s, F32) for s in outs]
        + [jax.ShapeDtypeStruct(t.shape[1:], BF)],
        in_specs=[ANY] * (2 + n) + [VMEM] * 2,
        out_specs=[VMEM] * 9,
        scratch_shapes=scratch,
        compiler_params=pltpu.CompilerParams(
            collective_id=5, has_side_effects=True, vmem_limit_bytes=58 * 1024 * 1024
        ),
        name="scatter_grads",
    )(a, o, *sums, t, mid)


def norm_forward(values):
    factor = lax.rsqrt(jnp.mean(values * values, axis=-1, keepdims=True) + EPSILON)
    return (values * factor, factor)


def norm_backward(grad_out, normed, factor, gain):
    grad_normed = grad_out * gain
    inner = jnp.mean(grad_normed * normed, axis=-1, keepdims=True)
    return (factor * (grad_normed - normed * inner), jnp.sum(grad_out * normed, axis=0))


def dot(a, b):
    return jnp.dot(a, b, preferred_element_type=F32)


def dot_t(a, b):
    return lax.dot_general(a, b, (((1,), (1,)), ((), ())), preferred_element_type=F32)


def t_dot(a, b):
    return lax.dot_general(a, b, (((0,), (0,)), ((), ())), preferred_element_type=F32)


def choose(flags):
    return flags.astype(BF)


def local(
    block_input,
    positions,
    first_gain,
    query_weight,
    query_bias,
    key_weight,
    value_weight,
    value_bias,
    output_weight,
    second_gain,
    gate_weight,
    up_weight,
    down_weight,
    cotangent,
):
    f = lax.axis_index("fsdp")
    c = lax.axis_index("ctx")
    stretch = f * 4 + c

    i896 = jnp.arange(D)
    spread = choose((i896 + i896 // 7)[:, None] == jnp.arange(DP)[None, :])

    half = HEAD_SIZE // 2
    frequency = ROTARY_BASE ** (-(np.arange(half) * 2.0 / HEAD_SIZE))
    places = positions[None]
    (
        all_a,
        all_o,
        all_d,
        all_g,
        all_u,
        cot_all,
        mid_all,
        seen,
        query_rot,
        attended,
        logs,
        residual_mid,
        gains,
        turn,
    ) = forward(
        (
            query_weight,
            key_weight,
            value_weight,
            output_weight,
            down_weight,
            gate_weight,
            up_weight,
        ),
        (query_bias[None], value_bias[None], first_gain[None], second_gain[None]),
        cotangent,
        block_input,
        places,
        jnp.asarray(np.tile(frequency, 4)[None], F32),
    )
    gain_first, gain_second = gains[0], gains[1]
    all_a = all_a.reshape(DP, 1152)
    weight_output = all_o.reshape(DP, D)
    all_g = all_g.reshape(DP, UC)
    all_u = all_u.reshape(DP, UC)
    all_d = all_d.reshape(UC, D)
    cot_all = cot_all.reshape(4 * TOK, D)
    mid_all = mid_all.reshape(4 * TOK, D)
    pad_ones = (jnp.arange(DP) % 8 == 7).astype(F32)[None, :]
    residual_in = block_input.astype(F32)
    normed_one, scale_one = norm_forward(residual_in)
    normed_input = (normed_one * gain_first).astype(BF)
    input_pad = (dot(normed_input, spread) + pad_ones).astype(BF)
    attended_pad = dot(attended, spread).astype(BF)
    normed_two, scale_two = norm_forward(residual_mid)
    mid_pad = dot(mid_all, spread).astype(BF)
    gate_pre = dot(mid_pad, all_g)
    up_pre = dot(mid_pad, all_u)
    sigma = jax.nn.sigmoid(gate_pre)
    hidden = (gate_pre * sigma * up_pre).astype(BF)
    grad_hidden = dot_t(cot_all, all_d)
    grad_gate_pre = (grad_hidden * up_pre * sigma * (1.0 + gate_pre * (1.0 - sigma))).astype(BF)
    grad_up_pre = (grad_hidden * gate_pre * sigma).astype(BF)
    mid_part = (dot_t(grad_gate_pre, all_g) + dot_t(grad_up_pre, all_u)).astype(BF)
    mid_part = dot_t(mid_part, spread).astype(BF)
    grad_normed_mid, out_part, *sums = tokens_sum(
        mid_part.reshape(4, TOK, D), hidden, cot_all, mid_pad, grad_gate_pre, grad_up_pre, all_d
    )
    grad_norm_part, grad_gain_two = norm_backward(
        grad_normed_mid, normed_two, scale_two, gain_second
    )
    grad_mid = cotangent.astype(F32) + grad_norm_part

    grad_mid_low = grad_mid.astype(BF)
    grad_output_w = t_dot(attended_pad, grad_mid_low)
    grad_attended = dot_t(dot_t(grad_mid_low, weight_output).astype(BF), spread).astype(BF)
    lows, *sums = back(query_rot, grad_attended, attended, logs, seen, places, turn, sums)
    grad_qkv_w = t_dot(input_pad, lows)
    grad_normed_input = dot_t(dot_t(lows, all_a).astype(BF), spread)
    grad_in_part, grad_gain_one = norm_backward(
        grad_normed_input, normed_one, scale_one, gain_first
    )
    grad_input = (grad_mid + grad_in_part).astype(BF)

    group = jnp.arange(DP)[:, None] // 8
    gains = jnp.where(
        i896[None, :] // 7 == group, grad_gain_one[None, :], jnp.roll(grad_gain_two, 448)[None, :]
    )
    grad_output_w = jnp.where(jnp.arange(DP)[:, None] % 8 == 7, gains, grad_output_w)
    sum_q, sum_k, sum_v, vec_a, sum_o, vec_o, sum_d, wide, block_output = scatter(
        grad_qkv_w.astype(BF).reshape(4, 4, 2, 32, 1152),
        grad_output_w.astype(BF).reshape(4, 4, 2, 32, D),
        sums,
        out_part,
        residual_mid,
    )
    wide = wide[:, :7].reshape(4, 7, 64, UP)[..., :UN]
    wide = jnp.transpose(wide, (1, 2, 0, 3)).reshape(7, 2 * FF)
    at = 7 * stretch
    return (
        block_output,
        grad_input,
        lax.dynamic_slice(vec_o[0], (at,), (7,)),
        sum_q,
        lax.dynamic_slice(vec_a[0], (at,), (7,)),
        sum_k,
        sum_v,
        lax.dynamic_slice(vec_a[0], (1024 + stretch,), (1,)),
        sum_o,
        lax.dynamic_slice(vec_o[0], (lax.rem(at + 448, 896),), (7,)),
        wide[:, :FF],
        wide[:, FF:],
        sum_d,
    )


def solution(mesh):
    tokens = P(("fsdp", "ctx"), None)
    entries = P(("fsdp", "ctx"))
    rows = P("fsdp", None)
    vector = P("fsdp")
    in_specs = (
        tokens,
        entries,
        vector,
        rows,
        vector,
        rows,
        rows,
        vector,
        rows,
        vector,
        rows,
        rows,
        rows,
        tokens,
    )
    out_specs = (
        tokens,
        tokens,
        entries,
        tokens,
        entries,
        tokens,
        tokens,
        entries,
        tokens,
        entries,
        tokens,
        tokens,
        tokens,
    )
    return jax.shard_map(local, mesh=mesh, in_specs=in_specs, out_specs=out_specs, check_vma=False)
```
